32 devices in a mesh: dp: 16 (over z, y, x), head: 2 (over core).
Axes of the slice: x: 2, y: 2, z: 4, core: 2. Of those that a mesh axis runs over, the one named last changes fastest.
Arguments:
- master: float32 [2, 5412864], P('head', 'dp'), as said below
- first_moment: float32 [2, 5412864], P('head', 'dp'), as said below
- second_moment: float32 [2, 5412864], P('head', 'dp'), as said below
- token_ids: int32 [32, 512], P('dp'), may hold values from 0 to 30521
- token_types: int32 [32, 512], P('dp'), may hold values from 0 to 1
- counts: int32 [32, 8], P('dp'), may hold values from 1 to 256, 512 in all within a row
- mask_pos: int32 [32, 40], P('dp'), may hold values from 0 to 255
- teacher_states: bfloat16 [32, 512, 768], P('dp'), may hold values from -6 to 6
- teacher_qk: bfloat16 [768, 2, 768], P(None, None, 'head'), may hold values from -0.21875 to 0.21875
- mentor_logits: bfloat16 [32, 40, 30522], P('dp', None, 'head'), may hold values from -16 to 16
Outputs:
- loss_sum: float32 [], replicated
- grad_norm: float32 [], replicated
- new_master: float32 [2, 5412864], P('head', 'dp')
- new_first: float32 [2, 5412864], P('head', 'dp')
- new_second: float32 [2, 5412864], P('head', 'dp')
- new_weights: bfloat16 [2, 5412864], P('head', 'dp')
The draws below stay inside these ranges and needn't reach their ends.
Inputs may be any that keep to these rules, and one draw needn't show every extreme that they name: `counts`: the last entry of a row is its padding; the others count its sentences' tokens; a row's entries sum to 512. `mask_pos`: masked positions lie before a row's padding and may repeat. `master`: entries from 5412864 on are zero. `first_moment`: entries from 5412864 on are zero. `second_moment`: every entry is positive.
All inputs are finite; a program needn't handle non-finite values.
Results may differ from the reference program's by a relative error of at most 0.0035.
The reference program's roundings to bfloat16 on the way (of `weights`) count: a program that leaves them out, or rounds other values in their place, can miss the bound.
Values may be sent and summed in bfloat16 or wider, within the bound.
No kernel may reach another device: no remote copies, remote signals or barrier semaphores. Data moves between devices by JAX's collectives and lax.ppermute only.
A program may use at most 256 MiB of HBM per device.

```python
import math
import jax
import jax.numpy as jnp
import numpy as np
from jax import lax

D = 312
HEADS = 12
HD = 26
FF = 1200
VOCAB = 30522
TD = 768
THEADS = 12
THD = 64
LAYERS = 1
LEN = 512
SENTS = 8
MOST = 256
MASKS = 40
STEP = 10
HSPLIT = 2
DH = 156
FH = 600
VH = 15261
SROWS = 522
PH = 5412864
VSTART = 5410704
FLAT = 5412864
ROWS = 32


CLIP_NORM = 1.0


def layout(rise):
    column = jnp.arange(FLAT, dtype=jnp.int32)[None, :]
    row_index = jnp.arange(HSPLIT, dtype=jnp.int32)[:, None]
    edge_table = VH * D
    edge_in = edge_table + LAYERS * 3 * D * DH
    edge_out = edge_in + LAYERS * DH * D
    edge_up = edge_out + LAYERS * D * FH
    edge_down = edge_up + LAYERS * FH * D
    edge_shared = edge_down + SROWS * DH
    vocab_row = (row_index * VH + column // D).astype(jnp.float32)
    spread = jnp.where(column < edge_table, (1.0 + rise * vocab_row / VOCAB) / math.sqrt(D), 0.0)
    spread = jnp.where((column >= edge_table) & (column < edge_in), 1.0 / math.sqrt(D), spread)
    spread = jnp.where((column >= edge_in) & (column < edge_out), 4.0 / math.sqrt(D), spread)
    spread = jnp.where((column >= edge_out) & (column < edge_up), 1.0 / math.sqrt(D), spread)
    spread = jnp.where((column >= edge_up) & (column < edge_down), 1.0 / math.sqrt(FF), spread)
    in_shared = (column >= edge_down) & (column < edge_shared)
    shared_row = (column - edge_down) // DH
    layer_row = (shared_row - LEN - 4) % 6
    gain_like = in_shared & ((shared_row == LEN + 2) | (shared_row >= LEN + 4) & ((layer_row == 0) | (layer_row == 2)))
    spread = jnp.where(in_shared, 0.1, spread)
    spread = jnp.where((column >= edge_shared) & (column < PH), 0.1, spread)
    return (spread, gain_like, column < PH, column >= VSTART)


def grad_scale(vector):
    base = CLIP_NORM / math.sqrt(HSPLIT * PH)
    return jnp.where(vector, 5.0 * base, base)


def draw_master(key, part):
    key = jax.random.fold_in(key, 11)
    spread, gain_like, live, vector = layout(2.0)
    noise = jax.random.normal(key, (HSPLIT, FLAT), jnp.float32)
    return jnp.where(live, spread * noise + jnp.where(gain_like, 1.0, 0.0), 0.0)


def draw_first_moment(key, part):
    key = jax.random.fold_in(key, 12)
    spread, gain_like, live, vector = layout(2.0)
    noise = jax.random.normal(key, (HSPLIT, FLAT), jnp.float32)
    return jnp.where(live, noise * grad_scale(vector) * (0.1 / 0.9), 0.0)


def draw_second_moment(key, part):
    key = jax.random.fold_in(key, 13)
    spread, gain_like, live, vector = layout(2.0)
    factor = jnp.exp(jax.random.uniform(key, (HSPLIT, FLAT), jnp.float32, math.log(0.5), math.log(2.0)))
    magnitude = grad_scale(vector)
    return factor * 2.0 * (0.001 / 0.999) * magnitude * magnitude


def set_ends(values, own_key, low, high):
    shape = values.shape
    index_at = [jax.random.randint(jax.random.fold_in(own_key, axis), (), 0, shape[axis]) for axis in range(len(shape))]
    values = values.at[tuple(index_at)].set(low)
    longest = shape.index(max(shape))
    index_at[longest] = (index_at[longest] + 1) % shape[longest]
    return values.at[tuple(index_at)].set(high)


def steps_of(rng, shape, cuts, smallest, high):
    def one(position, shards_of):
        heights = jax.random.uniform(jax.random.fold_in(jax.random.fold_in(rng, 6), position), (shards_of,), jnp.float32, smallest / len(cuts), high / len(cuts))
        return jnp.repeat(jnp.exp(heights), shape[position] // shards_of).reshape((-1,) + (1,) * (len(shape) - position - 1))

    level = one(*cuts[0])
    for cut in cuts[1:]:
        level = level * one(*cut)
    return level


def cumulative_ranks(amount, skew):
    loads = [(1 << 20) // math.isqrt(standing ** skew) + 1 for standing in range(1, amount + 1)]
    scale = 1 + sum(loads) // (1 << 30)
    return np.cumsum(np.array([max(1, weight // scale) for weight in loads]))


def ranked(key, dims, number_of, lean):
    grid = cumulative_ranks(number_of, lean)
    pick = jax.random.randint(jax.random.fold_in(key, 1), dims, 0, int(grid[number_of - 1]))
    standing = jnp.searchsorted(jnp.asarray(grid, jnp.int32), pick, side="right")
    return jax.random.permutation(jax.random.fold_in(key, 2), number_of)[standing].astype(jnp.int32)


def profile(amount, total, bound, slope):
    portions = [(1 << 20) // math.isqrt(grade ** slope) + 1 for grade in range(2, amount + 1)]
    surplus, given = total - bound - (amount - 1), [1] * (amount - 1)
    while surplus > 0:
        candidates = [i for i in range(amount - 1) if given[i] < bound]
        mass, remaining = sum([portions[i] for i in candidates]), surplus
        for i in candidates:
            more = min(bound - given[i], max(1, remaining * portions[i] // mass), surplus)
            given[i] = given[i] + more
            surplus = surplus - more
    return np.array([bound] + given)


def uneven_parts(stream_key, count, total, reach, slope):
    if count == 2:
        one = jax.random.randint(stream_key, (), max(1, total - reach), min(reach, total - 1) + 1)
        return jnp.stack([one, total - one])
    sizes = jnp.asarray(profile(count, total, reach, slope), jnp.int32)
    couples = (count - 1) // 2
    giver, receiver = sizes[1:1 + 2 * couples:2], sizes[2:2 + 2 * couples:2]
    room = jnp.minimum(giver - 1, reach - receiver)
    moved = jax.random.randint(jax.random.fold_in(stream_key, 1), (couples,), 0, 1 << 20) % (room + 1)
    sizes = sizes.at[1:1 + 2 * couples:2].set(giver - moved).at[2:2 + 2 * couples:2].set(receiver + moved)
    return sizes[jax.random.permutation(jax.random.fold_in(stream_key, 2), count)]


def scatter_about(stream_key, dims, width, limit, split=(), held_as=jnp.bfloat16):
    entries = jax.random.normal(stream_key, dims, jnp.float32) * width
    if len(split) > 0:
        entries = steps_of(stream_key, dims, split, -0.22, 0.18) * entries
    return jnp.clip(entries, min=-limit, max=limit).astype(held_as)


def setup_inputs(seed: int = 0) -> dict:
    key_of = jax.random.split(jax.random.key(seed), 11)
    return {
        "master": draw_master(jax.random.fold_in(key_of[10], 71), 0),
        "first_moment": draw_first_moment(jax.random.fold_in(key_of[10], 71), 0),
        "second_moment": draw_second_moment(jax.random.fold_in(key_of[10], 71), 0),
        "token_ids": set_ends(ranked(key_of[3], (ROWS, LEN), VOCAB, 2), jax.random.fold_in(key_of[3], 3), 0, VOCAB - 1).astype(jnp.int32),
        "token_types": set_ends(jax.random.randint(key_of[4], (ROWS, LEN), 0, 2), jax.random.fold_in(key_of[4], 1), 0, 1).astype(jnp.int32),
        "counts": jax.vmap(lambda own: uneven_parts(own, SENTS, LEN, MOST, 2))(jax.random.split(key_of[5], ROWS)).reshape((ROWS, SENTS)).astype(jnp.int32),
        "mask_pos": set_ends(jax.random.randint(key_of[6], (ROWS, MASKS), 0, LEN - MOST), jax.random.fold_in(key_of[6], 1), 0, (LEN - MOST) - 1).astype(jnp.int32),
        "teacher_states": scatter_about(key_of[7], (ROWS, LEN, TD), 1.0, 6.0, ((0, 16),)),
        "teacher_qk": scatter_about(key_of[8], (TD, 2, TD), TD ** -0.5, 0.21875, ((2, 2),)),
        "mentor_logits": scatter_about(key_of[9], (ROWS, MASKS, VOCAB), 3.0, 16.0, ((0, 16), (2, 2))),
    }


ATT_WEIGHT = 1.0
SOFTEN_FACTOR = 2.0
CLIP_NORM = 1.0
BETA_ONE = 0.9
BETA_TWO = 0.999
RATE_MATRIX = 0.06
RATE_VECTOR = 0.6
WEIGHT_DECAY = 0.01
ADAM_EPS = 1e-08
NORM_EPS = 1e-12
MASKED = -1000000000.0
PRECISE_MATMUL = lax.Precision.HIGHEST

@jax.custom_vjp
def low(v):
    return lax.optimization_barrier(v.astype(jnp.bfloat16)).astype(jnp.float32)

@jax.custom_vjp
def low_back(v):
    return v

def low_keep(v):
    return (low(v), None)

def low_pass(kept, grad):
    return (grad,)

def back_keep(v):
    return (v, None)

def back_low(kept, grad):
    return (low(grad),)
low.defvjp(low_keep, low_pass)
low_back.defvjp(back_keep, back_low)

def round_both(value):
    return low(low_back(value))

def matmul_high(left, right):
    return jnp.matmul(left, right, precision=PRECISE_MATMUL)
JOIN_AXES = (0, 3, 1, 2, 1, 1, 2, 1)

def piece_shapes():
    return [(VH, D), (LAYERS, 3, D, DH), (LAYERS, DH, D), (LAYERS, D, FH), (LAYERS, FH, D), (SROWS, DH), (LAYERS, 2, DH), (LAYERS, FH)]

def unpack(flat_weights):
    result = []
    offset = 0
    for piece_shape, join_axis in zip(piece_shapes(), JOIN_AXES):
        length = math.prod(piece_shape)
        pieces = [flat_weights[head_index, offset:offset + length].reshape(piece_shape) for head_index in range(HSPLIT)]
        result.append(jnp.concatenate(pieces, axis=join_axis))
        offset += length
    return tuple(result)

def structure(counts):
    sentence_ends = jnp.cumsum(counts, axis=-1)
    positions = jnp.arange(LEN, dtype=jnp.int32)
    passed = (positions[None, :, None] >= sentence_ends[:, None, :]).astype(jnp.int32)
    sentence = lax.optimization_barrier(jnp.sum(passed, axis=-1))
    within = positions[None, :] - lax.optimization_barrier(jnp.sum(passed * counts[:, None, :], axis=-1))
    return (sentence, within)

def layer_norm(value, gain_row, bias_row):
    centred = value - lax.optimization_barrier(jnp.mean(value, axis=-1, keepdims=True))
    variance = lax.optimization_barrier(jnp.mean(centred * centred, axis=-1, keepdims=True))
    return centred * lax.rsqrt(variance + NORM_EPS) * gain_row + bias_row

def softmax_masked(scores, allowed):
    return jax.nn.softmax(jnp.where(allowed, scores, MASKED), axis=-1)

def block_loss(weights, teacher_weight, token_ids, token_types, counts, mask_pos, teacher_in, mentor_logits):
    word_embedding_matrix, attn_in, attn_out, ffn_in, ffn_out, shared, qv_bias, up_bias = weights
    batch_rows = token_ids.shape[0]
    sentence, within = structure(counts)
    allowed = (sentence[:, :, None] == sentence[:, None, :])[:, None]
    valid_rows = (sentence < SENTS - 1).astype(jnp.float32)[:, None, :, None]
    teacher_proj = low(jnp.einsum('bld,dce->blce', teacher_in.astype(jnp.float32), teacher_weight, precision=PRECISE_MATMUL))
    teacher_q = teacher_proj[:, :, 0].reshape(batch_rows, LEN, THEADS, THD)
    teacher_k = teacher_proj[:, :, 1].reshape(batch_rows, LEN, THEADS, THD)
    teacher_prob = softmax_masked(jnp.einsum('bqhe,bkhe->bhqk', teacher_q, teacher_k, precision=PRECISE_MATMUL) * THD ** (-0.5), allowed)
    hidden_state = low_back(word_embedding_matrix[token_ids]) + shared[within] + shared[LEN + token_types]
    hidden_state = layer_norm(hidden_state, shared[LEN + 2], shared[LEN + 3])
    map_loss = jnp.zeros((), jnp.float32)
    for layer_index in range(LAYERS):
        row_base = LEN + 4 + 6 * layer_index
        gathered = low(hidden_state)
        queries = round_both(matmul_high(gathered, attn_in[layer_index, 0]) + qv_bias[layer_index, 0])
        key_heads = round_both(matmul_high(gathered, attn_in[layer_index, 1]))
        values = round_both(matmul_high(gathered, attn_in[layer_index, 2]) + qv_bias[layer_index, 1])
        queries = queries.reshape(batch_rows, LEN, HEADS, HD)
        key_heads = key_heads.reshape(batch_rows, LEN, HEADS, HD)
        values = values.reshape(batch_rows, LEN, HEADS, HD)
        scores = low_back(jnp.einsum('bqhe,bkhe->bhqk', queries, key_heads, precision=PRECISE_MATMUL) * HD ** (-0.5))
        attn_prob = softmax_masked(scores, allowed)
        mismatch = attn_prob - teacher_prob
        map_loss = map_loss + ATT_WEIGHT * jnp.sum(mismatch * mismatch * valid_rows)
        mixed_heads = jnp.einsum('bhqk,bkhe->bqhe', low(attn_prob), values, precision=PRECISE_MATMUL)
        mixed_heads = round_both(mixed_heads.reshape(batch_rows, LEN, D))
        branch = low_back(matmul_high(mixed_heads, attn_out[layer_index]))
        hidden_state = layer_norm(hidden_state + branch + shared[row_base + 4], shared[row_base], shared[row_base + 1])
        pre_act = low_back(matmul_high(low(hidden_state), ffn_in[layer_index]) + up_bias[layer_index])
        branch = low_back(matmul_high(low(jax.nn.gelu(pre_act, approximate=False)), ffn_out[layer_index]))
        hidden_state = layer_norm(hidden_state + branch + shared[row_base + 5], shared[row_base + 2], shared[row_base + 3])
    picked_logit = low(jnp.take_along_axis(hidden_state, mask_pos[:, :, None], axis=1))
    pupil_logits = low_back(jnp.einsum('lop,zp->loz', picked_logit, word_embedding_matrix, precision=PRECISE_MATMUL)) / SOFTEN_FACTOR
    teacher_softened_probs = jax.nn.softmax(mentor_logits.astype(jnp.float32) / SOFTEN_FACTOR, axis=-1)
    entropy = -jnp.sum(teacher_softened_probs * jax.nn.log_softmax(pupil_logits, axis=-1))
    return map_loss + entropy

def reference(master, first_moment, second_moment, token_ids, token_types, counts, mask_pos, teacher_states, teacher_qk, mentor_logits):
    teacher_weight = teacher_qk.astype(jnp.float32)
    block_count = token_ids.shape[0] // 8
    blocks_in = (token_ids.reshape(block_count, 8, LEN), token_types.reshape(block_count, 8, LEN), counts.reshape(block_count, 8, SENTS), mask_pos.reshape(block_count, 8, MASKS), teacher_states.reshape(block_count, 8, LEN, TD), mentor_logits.reshape(block_count, 8, MASKS, VOCAB))
    checked = jax.checkpoint(block_loss)

    def total_loss(flat_weights):
        weights = unpack(low(flat_weights))

        def scan_step(running, block):
            return (running + checked(weights, teacher_weight, *block), None)
        return lax.scan(scan_step, jnp.zeros((), jnp.float32), blocks_in)[0]
    loss_sum, backward = jax.vjp(total_loss, master)
    gradient = backward(jnp.ones((), jnp.float32))[0]
    grad_norm = jnp.sqrt(jnp.sum(gradient * gradient))
    clipped = gradient * (CLIP_NORM / jnp.maximum(grad_norm, CLIP_NORM))
    flat_index = jnp.arange(FLAT, dtype=jnp.int32)[None, :]
    matrix_part = flat_index < VSTART
    step_rate = jnp.where(matrix_part, RATE_MATRIX, RATE_VECTOR)
    decay_rate = jnp.where(matrix_part, WEIGHT_DECAY, 0.0)
    new_first = BETA_ONE * first_moment + (1.0 - BETA_ONE) * clipped
    new_second = BETA_TWO * second_moment + (1.0 - BETA_TWO) * clipped * clipped
    adam_step = new_first / (1.0 - BETA_ONE ** STEP) / (jnp.sqrt(new_second / (1.0 - BETA_TWO ** STEP)) + ADAM_EPS)
    new_master = master - step_rate * (adam_step + decay_rate * master)
    return (loss_sum, grad_norm, new_master, new_first, new_second, new_master.astype(jnp.bfloat16))
```

```python
import functools

import jax
import jax.numpy as jnp
from jax import lax
from jax.experimental import pallas as pl
from jax.experimental.pallas import tpu as pltpu
from jax.sharding import PartitionSpec as P

D = 312
HEADS = 12
HD = 26
HP = 32
FF = 1200
VOCAB = 30522
THD = 64
LEN = 512
STEP = 10
SROWS = 522

ATT_WEIGHT = 1.0
SOFTEN_FACTOR = 2.0
CLIP_NORM = 1.0
BETA_ONE = 0.9
BETA_TWO = 0.999
RATE_MATRIX = 0.06
RATE_VECTOR = 0.6
WEIGHT_DECAY = 0.01
ADAM_EPS = 1e-08
NORM_EPS = 1e-12
MASKED = -1000000000.0

F32 = jnp.float32
BF16 = jnp.bfloat16
LANES = 128
BOTH = ("dp", "head")
VMEM_BYTES = 56 * 1024 * 1024


def ceil_to(value, unit):
    return -(-value // unit) * unit


def call(kernel, out_shape, *args, scratch=(), smem=0):
    in_specs = [
        pl.BlockSpec(memory_space=pltpu.SMEM if index < smem else pltpu.VMEM)
        for index in range(len(args))
    ]
    out_specs = jax.tree.map(lambda _: pl.BlockSpec(memory_space=pltpu.VMEM), out_shape)
    return pl.pallas_call(
        kernel,
        out_shape=out_shape,
        in_specs=in_specs,
        out_specs=out_specs,
        scratch_shapes=list(scratch),
        compiler_params=pltpu.CompilerParams(vmem_limit_bytes=VMEM_BYTES),
    )(*args)


class Plan:
    def __init__(self, n, m, share):
        self.n, self.m, self.share = n, m, share
        self.rows_share = share // LANES
        self.vocab = VOCAB // m
        self.width = D // m
        self.units = FF // m
        self.first = [min(-(-d * share // D), self.vocab) for d in range(n + 1)]
        widest = -(-share // D)
        self.rows = ceil_to(widest + 3, 16)
        table = self.vocab * D
        self.table = table
        self.tail_row = table // LANES
        self.tail_off = table % LANES
        self.tail_rows = n * self.rows_share - self.tail_row
        self.tail_pad = ceil_to(self.tail_rows + 40, 16)
        w, u = self.width, self.units
        self.pieces = []
        base = self.tail_off
        for rows, wide in ((3 * D, w), (w, D), (D, u), (u, D), (SROWS, w), (m, w), (1, u)):
            self.pieces.append((base, wide, rows))
            base += rows * wide
        self.special = n == 16 and self.tail_row // self.rows_share == n - 2
        if self.special:
            self.low_rows = (n - 1) * self.rows_share - self.tail_row
            self.slice_rows = ceil_to(-(-self.rows_share // 8), 16)


def period(width):
    step = 16
    while step * width % LANES:
        step *= 2
    return step, step * width // LANES


def rows_at(start, count, stride):
    return pl.ds(start, count) if count == 1 else pl.ds(start, count, stride=stride)


def spread_rows(src, dst, base, width, rows):
    step, lane_rows = period(width)
    tiles = -(-width // LANES)
    for phase in range(min(step, rows)):
        count = len(range(phase, rows, step))
        line, off = divmod(base + phase * width, LANES)
        loaded = [
            src[rows_at(line + j, count, lane_rows), :] for j in range(tiles + (1 if off else 0))
        ]
        lane = lax.broadcasted_iota(jnp.int32, (count, LANES), 1)
        for tile in range(tiles):
            value = loaded[tile]
            if off:
                value = jnp.where(
                    lane < LANES - off,
                    pltpu.roll(value, LANES - off, 1),
                    pltpu.roll(loaded[tile + 1], LANES - off, 1),
                )
            dst[tile, rows_at(phase, count, step), :] = value


def pack_rows(src, dst, base, width, rows):
    step, lane_rows = period(width)
    tiles = -(-width // LANES)
    for phase in range(min(step, rows)):
        count = len(range(phase, rows, step))
        line, off = divmod(base + phase * width, LANES)
        loaded = [
            src[tile, rows_at(phase, count, step), :] for tile in range(tiles)
        ]
        lane = lax.broadcasted_iota(jnp.int32, (count, LANES), 1)
        rolled = [pltpu.roll(value, off, 1) if off else value for value in loaded]
        for j in range(-(-(off + width) // LANES)):
            value = jnp.zeros((count, LANES), F32)
            if j < tiles:
                value = jnp.where(lane >= off, rolled[j], value)
            if off and j > 0:
                value = jnp.where(lane < off, rolled[j - 1], value)
            at = rows_at(line + j, count, lane_rows)
            dst[at, :] = dst[at, :] + value


def column_tiles(width):
    return [(t, t * LANES, min(LANES, width - t * LANES)) for t in range(-(-width // LANES))]


def shift_lines(source, count, start, max_line):
    low, high = start // LANES, lax.rem(start, LANES)
    first = source[0:count, :]
    second = source[1 : count + 1, :]
    for line in range(1, max_line + 1):
        first = jnp.where(low == line, source[line : count + line, :], first)
        second = jnp.where(low == line, source[line + 1 : count + line + 1, :], second)
    lane = lax.broadcasted_iota(jnp.int32, (count, LANES), 1)
    back = lax.rem(LANES - high, LANES)
    return jnp.where(lane < LANES - high, pltpu.roll(first, back, 1), pltpu.roll(second, back, 1))


def table_rows_kernel(plan, place, chunk, after, out, joined, shifted, rows):
    share = plan.rows_share
    lines = joined.shape[0]
    joined[share & -8 :, :] = jnp.zeros((lines - (share & -8), LANES), F32)
    joined[0:share, :] = chunk[...]
    joined[share : share + 8, :] = after[...]
    shifted[...] = jnp.zeros_like(shifted)
    shifted[0 : share + 1, :] = shift_lines(joined, share + 1, place[0], 2)
    spread_rows(shifted, rows, 0, D, plan.rows)
    row = lax.broadcasted_iota(jnp.int32, (plan.rows, LANES), 0)
    for tile, left, wide in column_tiles(D):
        value = jnp.where(row < place[1], rows[tile], 0.0).astype(BF16)
        out[:, left : left + wide] = value[:, 0:wide]


def table_rows(plan, place, chunk, after):
    lines = ceil_to(max(plan.rows_share + 16, plan.rows // 16 * 39 + 2), 8)
    return call(
        functools.partial(table_rows_kernel, plan),
        jax.ShapeDtypeStruct((plan.rows, D), BF16),
        place,
        chunk,
        after,
        scratch=[
            pltpu.VMEM((lines, LANES), F32),
            pltpu.VMEM((lines, LANES), F32),
            pltpu.VMEM((3, plan.rows, LANES), F32),
        ],
        smem=1,
    )


def table_pack_kernel(plan, place, grads, before, out, rows, lines):
    rows[...] = jnp.zeros_like(rows)
    for tile, left, wide in column_tiles(D):
        rows[tile, 16 : 16 + plan.rows, 0:wide] = grads[:, left : left + wide]
        rows[tile, 15:16, 0:wide] = before[0:1, left : left + wide]
    lines[...] = jnp.zeros_like(lines)
    pack_rows(rows, lines, 0, D, plan.rows + 16)
    count = plan.rows_share
    start = 39 * LANES - place[0]
    low, high = start // LANES - 36, lax.rem(start, LANES)
    first = lines[36 : 36 + count, :]
    second = lines[37 : 37 + count, :]
    for line in range(1, 4):
        first = jnp.where(low == line, lines[36 + line : 36 + line + count, :], first)
        second = jnp.where(low == line, lines[37 + line : 37 + line + count, :], second)
    lane = lax.broadcasted_iota(jnp.int32, (count, LANES), 1)
    back = lax.rem(LANES - high, LANES)
    out[...] = jnp.where(
        lane < LANES - high, pltpu.roll(first, back, 1), pltpu.roll(second, back, 1)
    )


def table_pack(plan, place, grads, before):
    lines = ceil_to(max(plan.rows_share + 48, (plan.rows // 16 + 1) * 39 + 2), 8)
    return call(
        functools.partial(table_pack_kernel, plan),
        jax.ShapeDtypeStruct((plan.rows_share, LANES), F32),
        place,
        grads,
        before,
        scratch=[
            pltpu.VMEM((3, plan.rows + 16, LANES), F32),
            pltpu.VMEM((lines, LANES), F32),
        ],
        smem=1,
    )


def unpack_kernel(plan, tail, *refs):
    outs, (lines, wide) = refs[:-2], refs[-2:]
    lines[...] = tail[0].astype(F32)
    for out, (base, width, rows) in zip(outs, plan.pieces):
        spread_rows(lines, wide, base, width, rows)
        for tile, left, part in column_tiles(width):
            out[0, :, left : left + part] = wide[tile, 0:rows, 0:part].astype(BF16)


def unpack_tail(plan, tail):
    m = tail.shape[0]
    shapes = [jax.ShapeDtypeStruct((m, rows, width), BF16) for _, width, rows in plan.pieces]
    tallest = max(rows for _, _, rows in plan.pieces)
    widest = max(-(-width // LANES) for _, width, _ in plan.pieces)
    return pl.pallas_call(
        functools.partial(unpack_kernel, plan),
        out_shape=shapes,
        grid=(m,),
        in_specs=[pl.BlockSpec((1,) + tail.shape[1:], lambda i: (i, 0, 0))],
        out_specs=[pl.BlockSpec((1,) + s.shape[1:], lambda i: (i, 0, 0)) for s in shapes],
        scratch_shapes=[
            pltpu.VMEM(tail.shape[1:], F32),
            pltpu.VMEM((widest, tallest, LANES), F32),
        ],
        compiler_params=pltpu.CompilerParams(vmem_limit_bytes=VMEM_BYTES),
    )(tail)


def pack_kernel(plan, *refs):
    ins, out, (wide, lines) = refs[:-3], refs[-3], refs[-2:]
    lines[...] = jnp.zeros_like(lines)
    for source, (base, width, rows) in zip(ins, plan.pieces):
        for tile, left, part in column_tiles(width):
            if part < LANES:
                wide[tile, 0:rows, :] = jnp.zeros((rows, LANES), F32)
            wide[tile, 0:rows, 0:part] = source[0, :, left : left + part]
        pack_rows(wide, lines, base, width, rows)
    out[0] = lines[...]


def pack_tail(plan, pieces):
    m = pieces[0].shape[0]
    tallest = max(rows for _, _, rows in plan.pieces)
    widest = max(-(-width // LANES) for _, width, _ in plan.pieces)
    return pl.pallas_call(
        functools.partial(pack_kernel, plan),
        out_shape=jax.ShapeDtypeStruct((m, plan.tail_pad, LANES), F32),
        grid=(m,),
        in_specs=[pl.BlockSpec((1,) + p.shape[1:], lambda i: (i, 0, 0)) for p in pieces],
        out_specs=pl.BlockSpec((1, plan.tail_pad, LANES), lambda i: (i, 0, 0)),
        scratch_shapes=[
            pltpu.VMEM((widest, tallest, LANES), F32),
            pltpu.VMEM((plan.tail_pad, LANES), F32),
        ],
        compiler_params=pltpu.CompilerParams(vmem_limit_bytes=VMEM_BYTES),
    )(*pieces)


def swap(value, axis, bit, size):
    return lax.ppermute(value, axis, [(i, i ^ bit) for i in range(size)])


def gather_to_all(value, plan):
    return lax.all_to_all(
        jnp.broadcast_to(value[None], (plan.n,) + value.shape), "dp", 0, 0, tiled=False
    )


def join_heads(value, head, m):
    if m != 2:
        return lax.all_gather(value, "head", axis=0, tiled=False)
    other = swap(value, "head", 1, m)
    mine_first = head == 0
    return jnp.stack([jnp.where(mine_first, value, other), jnp.where(mine_first, other, value)])


def total_all(value, plan):
    if plan.n & (plan.n - 1) or plan.m & (plan.m - 1):
        return lax.psum(value, BOTH)
    bit = 1
    while bit < plan.m:
        value = value + swap(value, "head", bit, plan.m)
        bit *= 2
    bit = 1
    while bit < plan.n:
        value = value + swap(value, "dp", bit, plan.n)
        bit *= 2
    return value


def gather_tail(plan, chunk):
    n, share = plan.n, plan.rows_share
    if not plan.special:
        whole = lax.all_gather(chunk, "dp", axis=0, tiled=True)
        tail = whole[plan.tail_row :]
        return jnp.pad(tail, ((0, plan.tail_pad - plan.tail_rows), (0, 0)))
    d = lax.axis_index("dp")
    low, size = plan.low_rows, plan.slice_rows
    padded = jnp.pad(chunk, ((0, 8 * size - share), (0, 0)))
    from_low = jnp.pad(chunk[share - low :], ((0, 8 * size - low), (0, 0)))
    own = jnp.where(d == n - 2, from_low, padded)
    mine = own[7 * size :]
    for k in range(7):
        part = lax.ppermute(
            own[k * size : (k + 1) * size], "dp", [(n - 2, 2 * k), (n - 1, 2 * k + 1)]
        )
        mine = jnp.where(d // 2 == k, part, mine)
    slices = gather_to_all(mine, plan)
    low_part = slices[0::2].reshape(8 * size, LANES)[:low]
    high_part = slices[1::2].reshape(8 * size, LANES)[:share]
    return jnp.pad(
        jnp.concatenate([low_part, high_part]), ((0, plan.tail_pad - plan.tail_rows), (0, 0))
    )


def reduce_tail(plan, tail):
    n, share = plan.n, plan.rows_share
    d = lax.axis_index("dp")
    if not plan.special:
        total = lax.psum(tail, "dp")
        front = jnp.zeros((share, LANES), F32)
        start = jnp.clip(d * share - plan.tail_row + share, 0, plan.tail_pad)
        return lax.dynamic_slice_in_dim(
            jnp.concatenate([front, total[: plan.tail_rows], front]), start, share
        )
    low, size = plan.low_rows, plan.slice_rows
    low_part = jnp.pad(tail[:low], ((0, 8 * size - low), (0, 0))).reshape(8, size, LANES)
    high_part = jnp.pad(tail[low : low + share], ((0, 8 * size - share), (0, 0)))
    both = jnp.stack([low_part, high_part.reshape(8, size, LANES)], axis=1)
    parts = lax.all_to_all(
        both.reshape(n, size, LANES).astype(BF16), "dp", 0, 0, tiled=False
    )
    mine = jnp.sum(parts.astype(F32), axis=0)
    whole = []
    for k in range(7):
        whole.append(lax.ppermute(mine, "dp", [(2 * k, n - 2), (2 * k + 1, n - 1)]))
    whole = jnp.concatenate(whole + [mine])
    for_low = jnp.pad(whole[:low], ((share - low, 0), (0, 0)))
    return jnp.where(d == n - 2, for_low, jnp.where(d == n - 1, whole[:share], 0.0))


def attention_kernel(proj, teacher, sent_col, sent_row, weight, plain, grad_q, grad_k, loss):
    @pl.when(pl.program_id(0) == 0)
    def _():
        loss[...] = jnp.zeros_like(loss)

    allowed = sent_col[...] == sent_row[...]

    def probs(queries, key_heads, scale):
        scores = lax.dot_general(
            queries, key_heads, (((0,), (0,)), ((), ())), preferred_element_type=F32
        )
        scores = jnp.where(allowed, scores * scale, MASKED)
        exponent = jnp.exp(scores - jnp.max(scores, axis=-1, keepdims=True))
        return exponent * (1.0 / jnp.sum(exponent, axis=-1, keepdims=True))

    teacher_prob = probs(teacher[0, 0], teacher[1, 0], THD ** (-0.5))
    queries, key_heads = proj[0, 0], proj[1, 0]
    prob = probs(queries, key_heads, HD ** (-0.5))
    gap = (prob - teacher_prob) * weight[...]
    loss[...] += jnp.sum(gap * gap, axis=0, keepdims=True) * ATT_WEIGHT
    pulled = prob * gap
    inner = jnp.sum(pulled, axis=-1, keepdims=True)
    grad_scores = (
        (pulled - prob * inner) * (plain[...] * (2.0 * ATT_WEIGHT))
    ).astype(BF16)
    grad_q[0] = lax.dot_general(
        key_heads, grad_scores, (((1,), (1,)), ((), ())), preferred_element_type=F32
    )
    grad_k[0] = lax.dot_general(
        queries, grad_scores, (((1,), (0,)), ((), ())), preferred_element_type=F32
    )


def map_attention(proj, teacher, sent_col, sent_row, weight, plain):
    whole = lambda i: (0, 0)
    return pl.pallas_call(
        attention_kernel,
        out_shape=[
            jax.ShapeDtypeStruct((HEADS, HP, LEN), F32),
            jax.ShapeDtypeStruct((HEADS, HP, LEN), F32),
            jax.ShapeDtypeStruct((1, LEN), F32),
        ],
        grid=(HEADS,),
        in_specs=[
            pl.BlockSpec((3, 1, HP, LEN), lambda i: (0, i, 0, 0)),
            pl.BlockSpec((2, 1, THD, LEN), lambda i: (0, i, 0, 0)),
            pl.BlockSpec((LEN, 1), whole),
            pl.BlockSpec((1, LEN), whole),
            pl.BlockSpec((LEN, 1), whole),
            pl.BlockSpec((LEN, 1), whole),
        ],
        out_specs=[
            pl.BlockSpec((1, HP, LEN), lambda i: (i, 0, 0)),
            pl.BlockSpec((1, HP, LEN), lambda i: (i, 0, 0)),
            pl.BlockSpec((1, LEN), whole),
        ],
        compiler_params=pltpu.CompilerParams(vmem_limit_bytes=VMEM_BYTES),
    )(proj, teacher, sent_col, sent_row, weight, plain)


def dot(spec, left, right, **options):
    return jnp.einsum(spec, left, right, preferred_element_type=F32, **options)


def one_hot(index, size):
    return (index[:, None] == jnp.arange(size, dtype=jnp.int32)[None, :]).astype(BF16)


def exact_dot(left, right, spec):
    high = right.astype(BF16)
    rest = right - high.astype(F32)
    middle = rest.astype(BF16)
    low = (rest - middle.astype(F32)).astype(BF16)
    return dot(spec, left, high) + dot(spec, left, middle) + dot(spec, left, low)


def norm_forward(value, gain_row, bias_row):
    centred = value - jnp.mean(value, axis=-1, keepdims=True)
    inverse = lax.rsqrt(jnp.mean(centred * centred, axis=-1, keepdims=True) + NORM_EPS)
    normed = centred * inverse
    return (normed * gain_row + bias_row, (normed, inverse))


def norm_backward(gradient, saved, gain_row):
    normed, inverse = saved
    scaled = gradient * gain_row
    inner_part = (
        scaled
        - jnp.mean(scaled, -1, keepdims=True)
        - normed * jnp.mean(scaled * normed, -1, keepdims=True)
    )
    return (inner_part * inverse, jnp.sum(gradient * normed, 0), jnp.sum(gradient, 0))


def masked_softmax(scores, allowed):
    scores = jnp.where(allowed, scores, MASKED)
    exponent = jnp.exp(scores - jnp.max(scores, axis=-1, keepdims=True))
    return exponent / jnp.sum(exponent, axis=-1, keepdims=True)


def local(
    master,
    first_moment,
    second_moment,
    token_ids,
    token_types,
    counts,
    mask_pos,
    teacher_states,
    teacher_qk,
    mentor_logits,
):
    n, m = lax.axis_size("dp"), lax.axis_size("head")
    d, h = lax.axis_index("dp"), lax.axis_index("head")
    share_len = master.shape[1]
    assert share_len % LANES == 0 and token_ids.shape[0] == m
    plan = Plan(n, m, share_len)
    share = plan.rows_share
    devices = n * m
    slots = max(8, 1024 // devices)
    masks = mask_pos.shape[1]
    picks = devices * masks

    own_row = lambda value: lax.dynamic_index_in_dim(value, h, 0, keepdims=False)
    ids, types, sizes, pos = (own_row(v) for v in (token_ids, token_types, counts, mask_pos))

    vocab_head = ids // plan.vocab
    vocab_row = ids - vocab_head * plan.vocab
    owner = (vocab_row * D) // share_len * m + vocab_head
    order = jnp.arange(LEN, dtype=jnp.int32)
    same = ids[:, None] == ids[None, :]
    leader = jnp.min(jnp.where(same, order[None, :], LEN), axis=1)
    leads = leader == order
    rank = jnp.sum(
        (owner[:, None] == owner[None, :]) & leads[None, :] & (order[None, :] < leader[:, None]),
        axis=1,
        dtype=jnp.int32,
    )
    rounds_here = jnp.max(rank) // slots + 1

    def token_slots(turn):
        place = rank - turn * slots
        return jnp.where((place >= 0) & (place < slots), owner * slots + place, -1)

    def ask(turn, extra):
        slot = token_slots(turn)
        hit = jnp.arange(devices * slots, dtype=jnp.int32)[:, None] == slot[None, :]
        wanted = jnp.max(jnp.where(hit, vocab_row[None, :], -1), axis=1).reshape(devices, slots)
        sent = jnp.concatenate(
            [wanted, jnp.broadcast_to(extra, (devices, 1)).astype(jnp.int32)], axis=1
        )
        sent = jnp.pad(sent, ((0, 0), (0, ceil_to(slots + 1, LANES) - slots - 1)))
        got = lax.all_to_all(sent, BOTH, 0, 0, tiled=True)
        asked = got[:, :slots].reshape(-1)
        return asked, got[:, slots]

    first_row = jnp.minimum((d * share_len + D - 1) // D, plan.vocab)
    row_count = jnp.minimum(((d + 1) * share_len + D - 1) // D, plan.vocab) - first_row

    chunk = master.reshape(share, LANES)
    after = lax.ppermute(chunk[:8], "dp", [(i + 1, i) for i in range(n - 1)])
    place = jnp.stack([first_row * D - d * share_len, row_count]).astype(jnp.int32)
    place = jnp.where(row_count > 0, place, 0)
    words_own = table_rows(plan, place, chunk, after)

    def fetch(turn, asked):
        rows = dot(
            "sv,vd->sd", one_hot(jnp.where(asked >= 0, asked - first_row, -1), plan.rows), words_own
        ).astype(BF16)
        back = lax.all_to_all(
            rows.reshape(devices, slots, D), BOTH, 0, 0, tiled=True
        ).reshape(-1, D)
        return dot("ts,sd->td", one_hot(token_slots(turn), devices * slots), back)

    asked_first, needs = ask(0, rounds_here)
    rounds = jnp.max(needs)
    words = fetch(0, asked_first)
    words = lax.while_loop(
        lambda state: state[0] < rounds,
        lambda state: (
            state[0] + 1,
            state[1] + fetch(state[0], ask(state[0], rounds_here)[0]),
        ),
        (jnp.int32(1), words),
    )[1]

    tail_own = gather_tail(plan, chunk.astype(BF16))
    tail = join_heads(tail_own, h, m)
    attn_in, attn_out, ffn_in, ffn_out, shared_half, qv_bias, up_bias = unpack_tail(plan, tail)
    shared = jnp.concatenate([shared_half[i] for i in range(m)], axis=1).astype(F32)
    per_head = plan.width // HD
    spread = (
        (jnp.arange(plan.width) // HD * HP + jnp.arange(plan.width) % HD)[:, None]
        == jnp.arange(per_head * HP)[None, :]
    ).astype(BF16)
    attn_in = attn_in.reshape(m, 3, D, plan.width)
    wide_in = dot("hcde,ef->hcdf", attn_in, spread).astype(BF16)
    wide_out = dot("ef,hed->hfd", spread, attn_out).astype(BF16).reshape(m * per_head * HP, D)
    wide_bias = dot("hce,ef->chf", qv_bias, spread).reshape(2, 1, m * per_head * HP)
    qkv_bias = jnp.concatenate(
        [wide_bias[0], jnp.zeros_like(wide_bias[0]), wide_bias[1]]
    ).reshape(3, m, per_head * HP)

    mentor = mentor_logits.reshape(m * masks, plan.vocab)
    halved = mentor.astype(F32) / SOFTEN_FACTOR
    mentor_top = jnp.max(halved, axis=-1)
    mentor_sum = jnp.sum(jnp.exp(halved - mentor_top[:, None]), axis=-1)
    pairs = join_heads(jnp.stack([mentor_top, mentor_sum]), h, m)
    top = jnp.max(pairs[:, 0], axis=0)
    log_total = top + jnp.log(jnp.sum(pairs[:, 1] * jnp.exp(pairs[:, 0] - top), axis=0))
    part_a = log_total.astype(BF16)
    part_b = (log_total - part_a.astype(F32)).astype(BF16)
    part_c = (log_total - part_a.astype(F32) - part_b.astype(F32)).astype(BF16)
    blocks = []
    room = plan.rows - 3
    for owner_index in range(n):
        low = plan.first[owner_index]
        high = min(low + room, plan.vocab)
        blocks.append(jnp.pad(mentor[:, low:high], ((0, 0), (0, room - (high - low)))))
    blocks = jnp.stack(blocks)
    stats = jnp.stack([part_a, part_b, part_c], axis=-1)
    blocks = jnp.concatenate(
        [blocks, jnp.broadcast_to(stats[None], (n,) + stats.shape)], axis=-1
    )
    mentor_here = lax.all_to_all(blocks, "dp", 0, 0, tiled=False).reshape(picks, plan.rows)

    teacher_weight = join_heads(teacher_qk, h, m)
    states = own_row(teacher_states)
    teacher_proj = dot("hdce,ld->chel", teacher_weight, states).astype(BF16)
    teacher_proj = teacher_proj.reshape(2, HEADS, THD, LEN)

    ends = jnp.cumsum(sizes)
    passed = (order[:, None] >= ends[None, :]).astype(jnp.int32)
    sentence = jnp.sum(passed, axis=-1)
    within = order - jnp.sum(passed * sizes[None, :], axis=-1)
    valid = (sentence < sizes.shape[0] - 1).astype(F32)

    position_hot = one_hot(within, LEN)
    positions = dot("lp,pd->ld", position_hot, shared[:LEN].astype(BF16))
    type_row = jnp.where(types[:, None] == 0, shared[LEN], shared[LEN + 1])
    state_zero, saved_zero = norm_forward(
        words + positions + type_row, shared[LEN + 2], shared[LEN + 3]
    )
    gathered = state_zero.astype(BF16)
    shared_rows = shared[LEN + 4 :]
    proj = dot("hcdf,ld->chfl", wide_in, gathered) + qkv_bias[..., None]
    proj = proj.astype(BF16).reshape(3, HEADS, HP, LEN)

    pick_hot = one_hot(pos, LEN)
    picked_any = jnp.sum(pick_hot.astype(F32), axis=0) > 0
    plain = jnp.where(picked_any, 0.0, 1.0)
    grad_q, grad_k, map_rows = map_attention(
        proj,
        teacher_proj,
        sentence[:, None],
        sentence[None, :],
        valid[:, None],
        plain[:, None],
    )

    pick_sentence = jnp.sum(jnp.where(pos[:, None] == order[None, :], sentence[None, :], 0), 1)
    pick_allowed = (pick_sentence[:, None] == sentence[None, :])[None]
    pick_valid = (pick_sentence < sizes.shape[0] - 1).astype(F32)[None, :, None]
    queries, key_heads, values = proj[0], proj[1], proj[2]
    pick_q = dot("hel,pl->hpe", queries, pick_hot).astype(BF16)
    prob = masked_softmax(dot("hpe,hel->hpl", pick_q, key_heads) * HD ** (-0.5), pick_allowed)
    pick_tq = dot("hel,pl->hpe", teacher_proj[0], pick_hot).astype(BF16)
    pick_teacher = masked_softmax(
        dot("hpe,hel->hpl", pick_tq, teacher_proj[1]) * THD ** (-0.5), pick_allowed
    )
    prob_low = prob.astype(BF16)
    mixed = dot("hpl,hel->phe", prob_low, values).astype(BF16).reshape(masks, HEADS * HP)
    state_pick = exact_dot(pick_hot, state_zero, "pl,ld->pd")
    state_one, saved_one = norm_forward(
        state_pick + dot("pf,fd->pd", mixed, wide_out) + shared_rows[4],
        shared_rows[0],
        shared_rows[1],
    )
    state_one_low = state_one.astype(BF16)
    pre_act = dot("pd,hdu->hpu", state_one_low, ffn_in) + up_bias.astype(F32)
    hidden_act = jax.nn.gelu(pre_act, approximate=False).astype(BF16)
    state_two, saved_two = norm_forward(
        state_one + dot("hpu,hud->pd", hidden_act, ffn_out) + shared_rows[5],
        shared_rows[2],
        shared_rows[3],
    )

    chosen = join_heads(gather_to_all(state_two.astype(BF16), plan), h, m)
    chosen = jnp.swapaxes(chosen, 0, 1).reshape(picks, D)
    column_ok = jnp.arange(plan.rows, dtype=jnp.int32)[None, :] < row_count
    logits = dot("md,vd->mv", chosen, words_own) / SOFTEN_FACTOR
    logits = jnp.where(column_ok, logits, -1e30)
    local_top = jnp.max(logits, axis=-1)
    local_sum = jnp.sum(
        jnp.where(column_ok, jnp.exp(logits - local_top[:, None]), 0.0), axis=-1
    )
    pairs = join_heads(jnp.stack([local_top, local_sum]), h, m)
    top = jnp.max(pairs[:, 0], axis=0)
    total = jnp.sum(pairs[:, 1] * jnp.exp(pairs[:, 0] - top), axis=0)
    pairs = gather_to_all(jnp.stack([top, total]), plan)
    top = jnp.max(pairs[:, 0], axis=0)
    student_total = top + jnp.log(jnp.sum(pairs[:, 1] * jnp.exp(pairs[:, 0] - top), axis=0))
    mentor_f32 = mentor_here.astype(F32)
    mentor_total = mentor_f32[:, room] + mentor_f32[:, room + 1] + mentor_f32[:, room + 2]
    target = jnp.where(
        column_ok, jnp.exp(mentor_f32 / SOFTEN_FACTOR - mentor_total[:, None]), 0.0
    )
    student = jnp.where(column_ok, jnp.exp(logits - student_total[:, None]), 0.0)
    grad_logits = ((student - target) / SOFTEN_FACTOR).astype(BF16)
    cross = jnp.sum(jnp.where(column_ok, target * logits, 0.0))
    own_totals = lax.dynamic_slice_in_dim(student_total, (d * m + h) * masks, masks)
    loss_local = jnp.sum(map_rows) + jnp.sum(own_totals) - cross

    grad_chosen = dot("mv,vd->md", grad_logits, words_own).reshape(n, m, masks, D)
    if m == 2:
        mine = lax.dynamic_index_in_dim(grad_chosen, h, 1, keepdims=False)
        other = lax.dynamic_index_in_dim(grad_chosen, 1 - h, 1, keepdims=False)
        mine = mine + swap(other.astype(BF16), "head", 1, 2).astype(F32)
    else:
        mine = lax.psum_scatter(grad_chosen, "head", scatter_dimension=1, tiled=False)
    grad_pick = jnp.sum(
        lax.all_to_all(mine.astype(BF16), "dp", 0, 0, tiled=False).astype(F32), axis=0
    )

    repeats = pos[:, None] == pos[None, :]
    mask_order = jnp.arange(masks, dtype=jnp.int32)
    leads_pick = jnp.min(jnp.where(repeats, mask_order[None, :], masks), axis=1) == mask_order
    grad_pick = jnp.where(
        leads_pick[:, None], exact_dot(repeats.astype(BF16), grad_pick, "pq,qd->pd"), 0.0
    )
    grad_res, gain_two, bias_two = norm_backward(grad_pick, saved_two, shared_rows[2])
    grad_branch = grad_res.astype(BF16)
    grad_ffn_out = dot("hpu,pd->hud", hidden_act, grad_branch)
    grad_hidden = dot("pd,hud->hpu", grad_branch, ffn_out)
    _, gelu_pull = jax.vjp(lambda value: jax.nn.gelu(value, approximate=False), pre_act)
    grad_pre = gelu_pull(grad_hidden)[0].astype(BF16)
    grad_ffn_in = dot("pd,hpu->hdu", state_one_low, grad_pre)
    grad_up_bias = jnp.sum(grad_pre.astype(F32), 1, keepdims=True)
    grad_one = grad_res + dot("hpu,hdu->pd", grad_pre, ffn_in)
    grad_mid, gain_one, bias_one = norm_backward(grad_one, saved_one, shared_rows[0])
    grad_attended = grad_mid.astype(BF16)
    grad_attn_out = dot("pf,pd->fd", mixed, grad_attended).reshape(m, per_head * HP, D)
    grad_mixed = dot("pd,fd->pf", grad_attended, wide_out).astype(BF16)
    grad_mixed = grad_mixed.reshape(masks, HEADS, HP)
    grad_values = dot("hpl,phe->hel", prob_low, grad_mixed)
    grad_prob = dot("phe,hel->hpl", grad_mixed, values)
    grad_prob = grad_prob + 2.0 * ATT_WEIGHT * (prob - pick_teacher) * pick_valid
    grad_scores = prob * (grad_prob - jnp.sum(prob * grad_prob, -1, keepdims=True))
    grad_scores = jnp.where(leads_pick[None, :, None], grad_scores, 0.0).astype(BF16)
    pick_grad_q = dot("hpl,hel->hpe", grad_scores, key_heads) * HD ** (-0.5)
    grad_k = (grad_k + dot("hpl,hpe->hel", grad_scores, pick_q)) * HD ** (-0.5)
    grad_q = grad_q * HD ** (-0.5) + dot("hpe,pl->hel", pick_grad_q.astype(BF16), pick_hot)
    grad_proj = jnp.stack([grad_q, grad_k, grad_values]).astype(BF16)
    grad_proj = grad_proj.reshape(3, m, per_head * HP, LEN)
    narrow = dot("ef,chfl->chel", spread, grad_proj).astype(BF16)
    grad_attn_in = dot("ld,chel->hcde", gathered, narrow).reshape(m, 3 * D, plan.width)
    bias_sums = jnp.sum(narrow.astype(F32), axis=-1)
    grad_qv = jnp.stack([bias_sums[0], bias_sums[2]], axis=1)
    grad_in = dot("chfl,hcdf->ld", grad_proj, wide_in) + exact_dot(
        pick_hot, grad_mid, "pl,pd->ld"
    )
    grad_embed, gain_embed, bias_embed = norm_backward(grad_in, saved_zero, shared[LEN + 2])

    grad_positions = exact_dot(position_hot, grad_embed, "lp,ld->pd")
    type_one = jnp.sum(jnp.where(types[:, None] == 1, grad_embed, 0.0), axis=0)
    type_zero = jnp.sum(jnp.where(types[:, None] == 0, grad_embed, 0.0), axis=0)
    vectors = jnp.stack(
        [
            type_zero,
            type_one,
            gain_embed,
            bias_embed,
            gain_one,
            bias_one,
            gain_two,
            bias_two,
            jnp.sum(grad_mid, 0),
            jnp.sum(grad_res, 0),
        ]
    )
    grad_shared = jnp.concatenate([grad_positions, vectors]).reshape(SROWS, m, plan.width)
    grad_attn_out = exact_dot(spread, grad_attn_out, "ef,hfd->hed")

    word_grads = grad_embed.astype(BF16)

    def deliver(turn, asked):
        slot_grads = dot("ts,td->sd", one_hot(token_slots(turn), devices * slots), word_grads)
        got = lax.all_to_all(
            slot_grads.astype(BF16).reshape(devices, slots, D), BOTH, 0, 0, tiled=True
        ).reshape(-1, D)
        hot = one_hot(jnp.where(asked >= 0, asked - first_row, -1), plan.rows)
        return dot("sv,sd->vd", hot, got)

    grad_table = dot("mv,md->vd", grad_logits, chosen) + deliver(0, asked_first)
    grad_table = lax.while_loop(
        lambda state: state[0] < rounds,
        lambda state: (
            state[0] + 1,
            state[1] + deliver(state[0], ask(state[0], rounds_here)[0]),
        ),
        (jnp.int32(1), grad_table),
    )[1]
    last_row = lax.dynamic_slice_in_dim(grad_table, jnp.maximum(row_count - 1, 0), 1)
    before = lax.ppermute(
        jnp.broadcast_to(last_row, (8, D)), "dp", [(i, i + 1) for i in range(n - 1)]
    )
    gradient = table_pack(plan, place, grad_table, before)
    line = d * share + jnp.arange(share, dtype=jnp.int32)[:, None]
    flat_index = line * LANES + jnp.arange(LANES, dtype=jnp.int32)[None, :]
    gradient = jnp.where(flat_index < plan.table, gradient, 0.0)

    tail_grads = pack_tail(
        plan,
        [
            grad_attn_in,
            grad_attn_out,
            grad_ffn_in,
            grad_ffn_out,
            jnp.swapaxes(grad_shared, 0, 1),
            grad_qv,
            grad_up_bias,
        ],
    )
    if m == 2:
        other = lax.dynamic_index_in_dim(tail_grads, 1 - h, 0, keepdims=False)
        tail_grad = own_row(tail_grads) + swap(other, "head", 1, 2)
    else:
        tail_grad = lax.psum_scatter(tail_grads, "head", scatter_dimension=0, tiled=False)
    gradient = gradient + reduce_tail(plan, tail_grad)

    numbers = jnp.stack([jnp.sum(gradient * gradient), loss_local])
    numbers = total_all(jnp.zeros((8, LANES), F32).at[0, :2].set(numbers), plan)
    square_sum, loss_sum = numbers[0, 0], numbers[0, 1]
    grad_norm = jnp.sqrt(square_sum)
    clipped = gradient * (CLIP_NORM / jnp.maximum(grad_norm, CLIP_NORM))
    vector_start = plan.table + plan.width * D * 4 + 2 * D * plan.units + (LEN + 2) * plan.width
    matrix_part = flat_index < vector_start
    step_rate = jnp.where(matrix_part, RATE_MATRIX, RATE_VECTOR)
    decay_rate = jnp.where(matrix_part, WEIGHT_DECAY, 0.0)
    first_moment = first_moment.reshape(share, LANES)
    second_moment = second_moment.reshape(share, LANES)
    new_first = BETA_ONE * first_moment + (1.0 - BETA_ONE) * clipped
    new_second = BETA_TWO * second_moment + (1.0 - BETA_TWO) * clipped * clipped
    adam_step = (
        new_first
        / (1.0 - BETA_ONE**STEP)
        / (jnp.sqrt(new_second / (1.0 - BETA_TWO**STEP)) + ADAM_EPS)
    )
    new_master = chunk - step_rate * (adam_step + decay_rate * chunk)
    flat = lambda value: value.reshape(1, share_len)
    return (
        loss_sum,
        grad_norm,
        flat(new_master),
        flat(new_first),
        flat(new_second),
        flat(new_master.astype(BF16)),
    )


def solution(mesh):
    return jax.shard_map(
        local,
        mesh=mesh,
        in_specs=(
            P("head", "dp"),
            P("head", "dp"),
            P("head", "dp"),
            P("dp", None),
            P("dp", None),
            P("dp", None),
            P("dp", None),
            P("dp", None, None),
            P(None, None, "head"),
            P("dp", None, "head"),
        ),
        out_specs=(P(), P(), P("head", "dp"), P("head", "dp"), P("head", "dp"), P("head", "dp")),
        check_vma=False,
    )
```

```python
import functools

import jax
import jax.numpy as jnp
from jax import lax
from jax.experimental import pallas as pl
from jax.experimental.pallas import tpu as pltpu
from jax.sharding import PartitionSpec as P

D = 312
HEADS = 12
HD = 26
HP = 32
FF = 1200
VOCAB = 30522
THD = 64
LEN = 512
STEP = 10
SROWS = 522

ATT_WEIGHT = 1.0
SOFTEN_FACTOR = 2.0
CLIP_NORM = 1.0
BETA_ONE = 0.9
BETA_TWO = 0.999
RATE_MATRIX = 0.06
RATE_VECTOR = 0.6
WEIGHT_DECAY = 0.01
ADAM_EPS = 1e-08
NORM_EPS = 1e-12
MASKED = -1000000000.0

F32 = jnp.float32
BF16 = jnp.bfloat16
LANES = 128
BOTH = ("dp", "head")
VMEM_BYTES = 56 * 1024 * 1024


def ceil_to(value, unit):
    return -(-value // unit) * unit


def call(kernel, out_shape, *args, scratch=(), smem=0, hbm=(), hbm_out=()):
    space = lambda index: pltpu.SMEM if index < smem else pl.ANY if index in hbm else pltpu.VMEM
    in_specs = [pl.BlockSpec(memory_space=space(index)) for index in range(len(args))]
    outs = out_shape if isinstance(out_shape, list) else [out_shape]
    out_specs = [
        pl.BlockSpec(memory_space=pl.ANY if index in hbm_out else pltpu.VMEM)
        for index in range(len(outs))
    ]
    out_specs = out_specs if isinstance(out_shape, list) else out_specs[0]
    return pl.pallas_call(
        kernel,
        out_shape=out_shape,
        in_specs=in_specs,
        out_specs=out_specs,
        scratch_shapes=list(scratch),
        compiler_params=pltpu.CompilerParams(vmem_limit_bytes=VMEM_BYTES),
    )(*args)


class Plan:
    def __init__(self, n, m, share):
        self.n, self.m, self.share = n, m, share
        self.rows_share = share // LANES
        self.vocab = VOCAB // m
        self.width = D // m
        self.units = FF // m
        self.first = [min(-(-d * share // D), self.vocab) for d in range(n + 1)]
        widest = -(-share // D)
        self.rows = ceil_to(widest + 3, 16)
        table = self.vocab * D
        self.table = table
        self.tail_row = table // LANES
        self.tail_off = table % LANES
        self.tail_rows = n * self.rows_share - self.tail_row
        self.tail_pad = ceil_to(self.tail_rows + 40, 16)
        w, u = self.width, self.units
        self.pieces = []
        base = self.tail_off
        for rows, wide in ((3 * D, w), (w, D), (D, u), (u, D), (SROWS, w), (2, w), (1, u)):
            self.pieces.append((base, wide, rows))
            base += rows * wide
        self.special = n == 16 and self.tail_row // self.rows_share == n - 2
        if self.special:
            self.low_rows = (n - 1) * self.rows_share - self.tail_row
            self.slice_rows = ceil_to(-(-self.rows_share // 8), 16)
            self.half_rows = 4 * self.slice_rows


def period(width):
    step = 16
    while step * width % LANES:
        step *= 2
    return step, step * width // LANES


def rows_at(start, count, stride):
    return pl.ds(start, count) if count == 1 else pl.ds(start, count, stride=stride)


def spread_rows(src, dst, base, width, rows):
    step, lane_rows = period(width)
    tiles = -(-width // LANES)
    for phase in range(min(step, rows)):
        count = len(range(phase, rows, step))
        line, off = divmod(base + phase * width, LANES)
        loaded = [
            src[rows_at(line + j, count, lane_rows), :] for j in range(tiles + (1 if off else 0))
        ]
        lane = lax.broadcasted_iota(jnp.int32, (count, LANES), 1)
        for tile in range(tiles):
            value = loaded[tile]
            if off:
                value = jnp.where(
                    lane < LANES - off,
                    pltpu.roll(value, LANES - off, 1),
                    pltpu.roll(loaded[tile + 1], LANES - off, 1),
                )
            dst[tile, rows_at(phase, count, step), :] = value


def pack_rows(src, dst, base, width, rows):
    step, lane_rows = period(width)
    tiles = -(-width // LANES)
    for phase in range(min(step, rows)):
        count = len(range(phase, rows, step))
        line, off = divmod(base + phase * width, LANES)
        loaded = [
            src[tile, rows_at(phase, count, step), :] for tile in range(tiles)
        ]
        lane = lax.broadcasted_iota(jnp.int32, (count, LANES), 1)
        rolled = [pltpu.roll(value, off, 1) if off else value for value in loaded]
        for j in range(-(-(off + width) // LANES)):
            value = jnp.zeros((count, LANES), F32)
            if j < tiles:
                value = jnp.where(lane >= off, rolled[j], value)
            if off and j > 0:
                value = jnp.where(lane < off, rolled[j - 1], value)
            at = rows_at(line + j, count, lane_rows)
            dst[at, :] = dst[at, :] + value


def column_tiles(width):
    return [(t, t * LANES, min(LANES, width - t * LANES)) for t in range(-(-width // LANES))]


def shift_lines(source, count, start, max_line):
    low, high = start // LANES, lax.rem(start, LANES)
    first = source[0:count, :]
    second = source[1 : count + 1, :]
    for line in range(1, max_line + 1):
        first = jnp.where(low == line, source[line : count + line, :], first)
        second = jnp.where(low == line, source[line + 1 : count + line + 1, :], second)
    lane = lax.broadcasted_iota(jnp.int32, (count, LANES), 1)
    back = lax.rem(LANES - high, LANES)
    return jnp.where(lane < LANES - high, pltpu.roll(first, back, 1), pltpu.roll(second, back, 1))


def bring(source, target, sem):
    copy = pltpu.make_async_copy(source, target, sem)
    copy.start()
    copy.wait()


def share_rows_kernel(plan, place, chunk, out, lines, sem):
    share, low = plan.rows_share, plan.low_rows
    lines[share & -8 :, :] = jnp.zeros((lines.shape[0] - (share & -8), LANES), F32)
    bring(chunk.at[:, 0, :], lines.at[0:share], sem)
    count = out.shape[0]
    begins_late = place[2] == plan.n - 2
    first = share - low
    out[...] = jnp.where(
        begins_late, lines[first : first + count, :], lines[0:count, :]
    ).astype(BF16)


def share_rows(plan, place, chunk):
    count = 8 * plan.slice_rows
    return call(
        functools.partial(share_rows_kernel, plan),
        jax.ShapeDtypeStruct((count, LANES), BF16),
        place,
        chunk,
        scratch=[
            pltpu.VMEM((ceil_to(count + plan.rows_share - plan.low_rows, 8), LANES), F32),
            pltpu.SemaphoreType.DMA,
        ],
        smem=1,
        hbm=(1,),
    )


def table_rows_kernel(plan, place, chunk, after, out, joined, shifted, rows, sem):
    share = plan.rows_share
    lines = joined.shape[0]
    joined[share & -8 :, :] = jnp.zeros((lines - (share & -8), LANES), F32)
    bring(chunk.at[:, 0, :], joined.at[0:share], sem)
    joined[share : share + 8, :] = after[...]
    shifted[...] = jnp.zeros_like(shifted)
    shifted[0 : share + 2, :] = shift_lines(joined, share + 2, place[0], 2)
    spread_rows(shifted, rows, 0, D, plan.rows)
    row = lax.broadcasted_iota(jnp.int32, (plan.rows, LANES), 0)
    for tile, left, wide in column_tiles(D):
        value = jnp.where(row < place[1], rows[tile], 0.0).astype(BF16)
        out[:, left : left + wide] = value[:, 0:wide]


def table_rows(plan, place, chunk, after):
    lines = ceil_to(max(plan.rows_share + 16, plan.rows // 16 * 39 + 2), 8)
    return call(
        functools.partial(table_rows_kernel, plan),
        jax.ShapeDtypeStruct((plan.rows, D), BF16),
        place,
        chunk,
        after,
        scratch=[
            pltpu.VMEM((lines, LANES), F32),
            pltpu.VMEM((lines, LANES), F32),
            pltpu.VMEM((3, plan.rows, LANES), F32),
            pltpu.SemaphoreType.DMA,
        ],
        smem=1,
        hbm=(1,),
    )


def table_pack_kernel(plan, place, grads, before, out, rows, lines):
    rows[...] = jnp.zeros_like(rows)
    for tile, left, wide in column_tiles(D):
        rows[tile, 16 : 16 + plan.rows, 0:wide] = grads[:, left : left + wide]
        rows[tile, 15:16, 0:wide] = before[0:1, left : left + wide]
    lines[...] = jnp.zeros_like(lines)
    pack_rows(rows, lines, 0, D, plan.rows + 16)
    count = plan.rows_share
    start = 39 * LANES - place[0]
    low, high = start // LANES - 36, lax.rem(start, LANES)
    first = lines[36 : 36 + count, :]
    second = lines[37 : 37 + count, :]
    for line in range(1, 4):
        first = jnp.where(low == line, lines[36 + line : 36 + line + count, :], first)
        second = jnp.where(low == line, lines[37 + line : 37 + line + count, :], second)
    lane = lax.broadcasted_iota(jnp.int32, (count, LANES), 1)
    back = lax.rem(LANES - high, LANES)
    value = jnp.where(
        lane < LANES - high, pltpu.roll(first, back, 1), pltpu.roll(second, back, 1)
    )
    line = lax.broadcasted_iota(jnp.int32, (count, LANES), 0)
    index = (line + place[2] * count) * LANES + lane
    out[...] = jnp.where(index < plan.table, value, 0.0)


def merge_kernel(plan, place, loss, table, *refs):
    extra, (out, numbers, whole, sem) = refs[:-4], refs[-4:]
    share = plan.rows_share
    whole[...] = table[...]
    if plan.special:
        d, low = place[2], plan.low_rows
        for owner, first, count in ((plan.n - 2, share - low, low), (plan.n - 1, 0, share)):

            @pl.when(d == owner)
            def _(first=first, count=count):
                whole[first : first + count, :] = (
                    whole[first : first + count, :] + extra[0][0:count, :]
                )
    else:
        whole[...] = whole[...] + extra[0][...]
    copy = pltpu.make_async_copy(whole, out.at[:, 0, :], sem)
    copy.start()
    value = whole[...]
    squares = jnp.sum(jnp.sum(value * value, axis=0, keepdims=True), axis=1, keepdims=True)
    line = lax.broadcasted_iota(jnp.int32, (8, LANES), 0)
    numbers[...] = jnp.where(
        line == 0, jnp.broadcast_to(squares, (8, LANES)), jnp.where(line == 1, loss[0], 0.0)
    )
    copy.wait()


def merge(plan, place, loss, table, extra):
    return call(
        functools.partial(merge_kernel, plan),
        [
            jax.ShapeDtypeStruct((plan.rows_share, 1, LANES), F32),
            jax.ShapeDtypeStruct((8, LANES), F32),
        ],
        place,
        loss,
        table,
        extra,
        scratch=[pltpu.VMEM((plan.rows_share, LANES), F32), pltpu.SemaphoreType.DMA],
        smem=2,
        hbm_out=(0,),
    )


def adam_kernel(plan, edge, place, scale, master, gradient, first, second, *outs):
    new_master, new_first, new_second, new_weights = outs
    clipped = gradient[...] * scale[0]
    moment = BETA_ONE * first[...] + (1.0 - BETA_ONE) * clipped
    spread = BETA_TWO * second[...] + (1.0 - BETA_TWO) * clipped * clipped
    step = (
        moment
        / (1.0 - BETA_ONE**STEP)
        / (jnp.sqrt(spread / (1.0 - BETA_TWO**STEP)) + ADAM_EPS)
    )
    index = lax.broadcasted_iota(jnp.int32, step.shape, 1) + place[2] * plan.share
    matrix_part = index < edge
    rate = jnp.where(matrix_part, RATE_MATRIX, RATE_VECTOR)
    decay = jnp.where(matrix_part, WEIGHT_DECAY, 0.0)
    value = master[...] - rate * (step + decay * master[...])
    new_master[...] = value
    new_first[...] = moment
    new_second[...] = spread
    new_weights[...] = value.astype(BF16)


def mentor_kernel(plan, room, cuts, mentor, *outs):
    m, masks, vocab = mentor.shape
    for owner in range(plan.n):
        low = plan.first[owner]
        high = min(low + room, vocab)
        if high <= low:
            for out in outs:
                out[owner] = jnp.zeros(out.shape[1:], BF16)
            continue
        left = low // LANES * LANES
        right = min(ceil_to(high, LANES), vocab)
        for part in range(m):
            value = mentor[part, :, left:right].astype(F32)
            value = jnp.pad(value, ((0, 0), (0, ceil_to(high, LANES) + LANES - right)))
            if low > left:
                value = pltpu.roll(value, value.shape[1] - (low - left), 1)
            if high - low < room:
                value = jnp.pad(value[:, : high - low], ((0, 0), (0, room - (high - low))))
            value = value[:, 0:room].astype(BF16)
            for out, start in zip(outs, cuts):
                first = max(start, part * masks)
                last = min(start + out.shape[1], (part + 1) * masks)
                if first < last:
                    out[owner, first - start : last - start, :] = value[
                        first - part * masks : last - part * masks, :
                    ]


def table_pack(plan, place, grads, before):
    lines = ceil_to(max(plan.rows_share + 48, (plan.rows // 16 + 1) * 39 + 2), 8)
    return call(
        functools.partial(table_pack_kernel, plan),
        jax.ShapeDtypeStruct((plan.rows_share, LANES), F32),
        place,
        grads,
        before,
        scratch=[
            pltpu.VMEM((3, plan.rows + 16, LANES), F32),
            pltpu.VMEM((lines, LANES), F32),
        ],
        smem=1,
    )


def unpack_kernel(plan, place, *refs):
    count = 4 if plan.special else 1
    own, other, refs = refs[:count], refs[count : 2 * count], refs[2 * count :]
    outs, (lines, wide) = refs[:-2], refs[-2:]
    share = plan.rows_share

    def load(tails):
        if not plan.special:
            lines[...] = tails[0][...].astype(F32)
            return
        half = plan.half_rows
        for quarter in range(4):
            y, x = divmod(quarter, 2)
            first = y * half
            end = min(first + half, share if x else plan.low_rows)
            at = first + (plan.low_rows if x else 0)
            for k in range(4):

                @pl.when(lax.rem(place[2], 4) == quarter ^ k)
                def _(k=k, at=at, length=end - first):
                    lines[at : at + length, :] = tails[k][...].astype(F32)[0:length]

    mine = place[3] == pl.program_id(0)
    pl.when(mine)(lambda: load(own))
    pl.when(jnp.logical_not(mine))(lambda: load(other))
    for out, (base, width, rows) in zip(outs, plan.pieces):
        spread_rows(lines, wide, base, width, rows)
        for tile, left, part in column_tiles(width):
            if len(out.shape) == 4:
                for kind in range(3):
                    value = wide[tile, kind * D : (kind + 1) * D, 0:part]
                    out[0, kind, :, left : left + part] = value.astype(BF16)
            else:
                out[0, :, left : left + part] = wide[tile, 0:rows, 0:part].astype(BF16)


def leading_block(value):
    rest = value.shape[1:]
    return pl.BlockSpec((1,) + rest, lambda i, *_: (i,) + (0,) * len(rest))


def unpack_tail(plan, place, own, other):
    m = plan.m
    shapes = [jax.ShapeDtypeStruct((m, rows, width), BF16) for _, width, rows in plan.pieces]
    shapes[0] = jax.ShapeDtypeStruct((m, 3, D, plan.width), BF16)
    tallest = max(rows for _, _, rows in plan.pieces)
    widest = max(-(-width // LANES) for _, width, _ in plan.pieces)
    return pl.pallas_call(
        functools.partial(unpack_kernel, plan),
        out_shape=shapes,
        grid=(m,),
        in_specs=[pl.BlockSpec(memory_space=pltpu.SMEM)]
        + [pl.BlockSpec(memory_space=pltpu.VMEM)] * (len(own) + len(other)),
        out_specs=[leading_block(shape) for shape in shapes],
        scratch_shapes=[
            pltpu.VMEM((plan.tail_pad, LANES), F32),
            pltpu.VMEM((widest, tallest, LANES), F32),
        ],
        compiler_params=pltpu.CompilerParams(vmem_limit_bytes=VMEM_BYTES),
    )(place, *own, *other)


def pack_kernel(plan, part_index, *refs):
    ins, out, (wide, lines) = refs[:-3], refs[-3], refs[-2:]
    lines[...] = jnp.zeros_like(lines)
    for source, (base, width, rows) in zip(ins, plan.pieces):
        for tile, left, part in column_tiles(width):
            if part < LANES:
                wide[tile, 0:rows, :] = jnp.zeros((rows, LANES), F32)
            if len(source.shape) == 4:
                for kind in range(3):
                    wide[tile, kind * D : (kind + 1) * D, 0:part] = source[
                        0, kind, :, left : left + part
                    ]
            else:
                wide[tile, 0:rows, 0:part] = source[0, :, left : left + part]
        pack_rows(wide, lines, base, width, rows)
    out[...] = lines[...]


def pack_tail(plan, part, pieces):
    tallest = max(rows for _, _, rows in plan.pieces)
    widest = max(-(-width // LANES) for _, width, _ in plan.pieces)

    def chosen_block(value):
        rest = value.shape[1:]
        return pl.BlockSpec((1,) + rest, lambda i, part: (part[0],) + (0,) * len(rest))

    return pl.pallas_call(
        functools.partial(pack_kernel, plan),
        out_shape=jax.ShapeDtypeStruct((plan.tail_pad, LANES), F32),
        grid_spec=pltpu.PrefetchScalarGridSpec(
            num_scalar_prefetch=1,
            grid=(1,),
            in_specs=[chosen_block(piece) for piece in pieces],
            out_specs=pl.BlockSpec((plan.tail_pad, LANES), lambda i, part: (0, 0)),
            scratch_shapes=[
                pltpu.VMEM((widest, tallest, LANES), F32),
                pltpu.VMEM((plan.tail_pad, LANES), F32),
            ],
        ),
        compiler_params=pltpu.CompilerParams(vmem_limit_bytes=VMEM_BYTES),
    )(part.reshape(1).astype(jnp.int32), *pieces)


def fold_kernel(plan, own, other, out):
    size, low, share = plan.slice_rows, plan.low_rows, plan.rows_share
    for index in range(8):
        for side, base, end in ((0, 0, low), (1, low, low + share)):
            first = base + index * size
            count = min(size, end - first)
            value = own[first : first + count, :] + other[first : first + count, :]
            value = jnp.pad(value, ((0, size - count), (0, 0)))
            out[2 * index + side] = value.astype(BF16)


def add_rows_kernel(over, index, rows, total, out):
    size = rows.shape[0] if over == NN else out.shape[0]
    out[...] = total[...] + mm(hot_rows(index[...], size), rows[...], over)


def add_rows(over, index, rows, total):
    return call(
        functools.partial(add_rows_kernel, over),
        jax.ShapeDtypeStruct(total.shape, F32),
        index[:, None],
        rows,
        total,
    )


def rows_grad_kernel(place, grads, chosen, asked, got, out):
    rows = out.shape[0]
    hot = hot_rows(asked[...], rows)
    out[...] = mm(grads[...], chosen[:, 0:D], TN) + mm(hot, got[...], TN)


def swap(value, axis, bit, size):
    return lax.ppermute(value, axis, [(i, i ^ bit) for i in range(size)])


def gather_to_all(value, plan):
    return lax.all_to_all(
        jnp.broadcast_to(value[None], (plan.n,) + value.shape), "dp", 0, 0, tiled=False
    )


def join_heads(value, head, m):
    if m != 2:
        return lax.all_gather(value, "head", axis=0, tiled=False)
    other = swap(value, "head", 1, m)
    mine_first = head == 0
    return jnp.stack([jnp.where(mine_first, value, other), jnp.where(mine_first, other, value)])


def total_all(value, plan):
    if plan.m == 2:
        value = value + swap(value, "head", 1, 2)
    else:
        value = lax.psum(value, "head")
    return jnp.sum(gather_to_all(value, plan), axis=0)


def tail_to_plane(plan, own):
    half = plan.half_rows
    d = lax.axis_index("dp")
    part = lax.ppermute(own[:half], "dp", [(14, 12), (15, 13)])
    return jnp.where(d >= 14, own[half:], part)


def tail_along_z(part, step):
    pairs = [[(12, 4)], [(12, 8), (4, 0)]][step]
    got = lax.ppermute(part, "dp", [(a + p, b + p) for a, b in pairs for p in range(4)])
    z = lax.axis_index("dp") // 4
    return jnp.where(z == 1 if step == 0 else (z == 0) | (z == 2), got, part)


def tail_in_plane(part, n):
    return [part] + [swap(part, "dp", k, n) for k in (1, 2, 3)]


def merge_stats(value, plan):
    steps = [("head", 1 << bit, plan.m) for bit in range(plan.m.bit_length() - 1)]
    steps += [("dp", 1 << bit, plan.n) for bit in range(plan.n.bit_length() - 1)]
    for axis, bit, size in steps:
        other = swap(value, axis, bit, size)
        top = jnp.maximum(value[:1], other[:1])
        total = value[1:] * jnp.exp(value[:1] - top) + other[1:] * jnp.exp(other[:1] - top)
        value = jnp.concatenate([top, total])
    return value


def gather_tail(plan, value):
    whole = lax.all_gather(value, "dp", axis=0, tiled=True)
    return jnp.pad(whole[plan.tail_row :], ((0, plan.tail_pad - plan.tail_rows), (0, 0)))


def reduce_tail(plan, own, other):
    n, share = plan.n, plan.rows_share
    d = lax.axis_index("dp")
    if not plan.special:
        total = lax.psum(own + other, "dp")
        front = jnp.zeros((share, LANES), F32)
        start = jnp.clip(d * share - plan.tail_row + share, 0, plan.tail_pad)
        return lax.dynamic_slice_in_dim(
            jnp.concatenate([front, total[: plan.tail_rows], front]), start, share
        )
    slices = call(
        functools.partial(fold_kernel, plan),
        jax.ShapeDtypeStruct((n, plan.slice_rows, LANES), BF16),
        own,
        other,
    )
    parts = lax.all_to_all(slices, "dp", 0, 0, tiled=False)
    mine = jnp.sum(parts.astype(F32), axis=0)
    whole = []
    for k in range(7):
        whole.append(lax.ppermute(mine, "dp", [(2 * k, n - 2), (2 * k + 1, n - 1)]))
    return jnp.concatenate(whole + [mine])


def attention_kernel(proj, teacher, columns, sent_row, grad_q, grad_k, loss):
    @pl.when(pl.program_id(0) == 0)
    def _():
        loss[...] = jnp.zeros_like(loss)

    allowed = columns[:, 2:3] == sent_row[...]
    weight = columns[:, 3:4].astype(F32)
    plain = columns[:, 4:5].astype(F32)

    def probs(queries, key_heads, scale):
        scores = lax.dot_general(
            queries, key_heads, (((0,), (0,)), ((), ())), preferred_element_type=F32
        )
        scores = jnp.where(allowed, scores * scale, MASKED)
        exponent = jnp.exp(scores - jnp.max(scores, axis=-1, keepdims=True))
        return exponent * (1.0 / jnp.sum(exponent, axis=-1, keepdims=True))

    teacher_prob = probs(teacher[0, 0], teacher[1, 0], THD ** (-0.5))
    queries, key_heads = proj[0, 0], proj[1, 0]
    prob = probs(queries, key_heads, HD ** (-0.5))
    gap = (prob - teacher_prob) * weight
    loss[...] += jnp.sum(gap * gap, axis=0, keepdims=True) * ATT_WEIGHT
    pulled = prob * gap
    inner = jnp.sum(pulled, axis=-1, keepdims=True)
    grad_scores = (
        (pulled - prob * inner) * (plain * (2.0 * ATT_WEIGHT))
    ).astype(BF16)
    grad_q[0] = lax.dot_general(
        key_heads, grad_scores, (((1,), (1,)), ((), ())), preferred_element_type=F32
    )
    grad_k[0] = lax.dot_general(
        queries, grad_scores, (((1,), (0,)), ((), ())), preferred_element_type=F32
    )


def map_attention(first, heads, proj, teacher, columns, sent_row):
    whole = lambda i: (0, 0)
    return pl.pallas_call(
        attention_kernel,
        out_shape=[
            jax.ShapeDtypeStruct((heads, HP, LEN), F32),
            jax.ShapeDtypeStruct((heads, HP, LEN), F32),
            jax.ShapeDtypeStruct((1, LEN), F32),
        ],
        grid=(heads,),
        in_specs=[
            pl.BlockSpec((3, 1, HP, LEN), lambda i: (0, first + i, 0, 0)),
            pl.BlockSpec((2, 1, THD, LEN), lambda i: (0, first + i, 0, 0)),
            pl.BlockSpec(columns.shape, whole),
            pl.BlockSpec((1, LEN), whole),
        ],
        out_specs=[
            pl.BlockSpec((1, HP, LEN), lambda i: (i, 0, 0)),
            pl.BlockSpec((1, HP, LEN), lambda i: (i, 0, 0)),
            pl.BlockSpec((1, LEN), whole),
        ],
        compiler_params=pltpu.CompilerParams(vmem_limit_bytes=VMEM_BYTES),
    )(proj, teacher, columns, sent_row)


def mm(left, right, over):
    return lax.dot_general(left, right, (over, ((), ())), preferred_element_type=F32)


NN, NT, TN = ((1,), (0,)), ((1,), (1,)), ((0,), (0,))


def exact(hot, value, over, parts=3):
    total = None
    for _ in range(parts):
        piece = value.astype(BF16)
        value = value - piece.astype(F32)
        term = mm(hot, piece, over)
        total = term if total is None else total + term
    return total


def head_spread(width, per_head):
    row = lax.broadcasted_iota(jnp.int32, (width, per_head * HP), 0)
    column = lax.broadcasted_iota(jnp.int32, (width, per_head * HP), 1)
    for head in range(1, per_head):
        column = column - jnp.where(row >= head * HD, HP - HD, 0)
    return jnp.where(row == column, 1.0, 0.0).astype(BF16)


def hot_rows(index, size):
    column = lax.broadcasted_iota(jnp.int32, (index.shape[0], size), 1)
    return jnp.where(index == column, 1.0, 0.0).astype(BF16)


def softmax_rows(scores, allowed):
    scores = jnp.where(allowed, scores, MASKED)
    exponent = jnp.exp(scores - jnp.max(scores, axis=-1, keepdims=True))
    return exponent * (1.0 / jnp.sum(exponent, axis=-1, keepdims=True))


def norm_pull(gradient, normed, inverse, gain_row):
    scaled = gradient * gain_row
    inner_part = (
        scaled
        - jnp.mean(scaled, -1, keepdims=True)
        - normed * jnp.mean(scaled * normed, -1, keepdims=True)
    )
    return (
        inner_part * inverse,
        jnp.sum(gradient * normed, 0, keepdims=True),
        jnp.sum(gradient, 0, keepdims=True),
    )


ROOT_HALF = 0.5**0.5
BELL = (2.0 * 3.141592653589793) ** -0.5


def forward_kernel(
    back,
    more_words,
    columns,
    pick_columns,
    sent_row,
    log_parts,
    attn_in,
    attn_out,
    ffn_in,
    ffn_out,
    shared_half,
    qv_bias,
    up_bias,
    chosen,
    normed_zero,
    inverse_zero,
    proj,
    prob,
    mixed,
    normed_one,
    inverse_one,
    state_low,
    pre_act,
    hidden_act,
    normed_two,
    inverse_two,
    shared,
):
    m, _, _, width = attn_in.shape
    per_head = width // HD
    for part in range(m):
        shared[:, part * width : (part + 1) * width] = shared_half[part].astype(F32)
    position_hot = hot_rows(columns[:, 0:1], LEN)
    state = mm(hot_rows(columns[:, 5:6], back.shape[0]), back[...], NN) + more_words[...]
    state = state + mm(position_hot, shared[0:LEN, :].astype(BF16), NN)
    state = state + jnp.where(columns[:, 1:2] == 0, shared[LEN : LEN + 1, :], shared[LEN + 1 : LEN + 2, :])
    state, (normed, inverse) = norm_forward(
        state, shared[LEN + 2 : LEN + 3, :], shared[LEN + 3 : LEN + 4, :]
    )
    normed_zero[...] = normed
    inverse_zero[...] = inverse
    gathered = state.astype(BF16)
    base = LEN + 4
    row = lambda index: shared[base + index : base + index + 1, :]

    spread = head_spread(width, per_head)
    for part in range(m):
        for kind in range(3):
            wide = mm(attn_in[part, kind], spread, NN).astype(BF16)
            value = mm(wide, gathered, ((0,), (1,)))
            if kind != 1:
                bias_row = qv_bias[part, kind // 2 : kind // 2 + 1, :]
                bias = mm(spread, jnp.broadcast_to(bias_row, (8, width)), ((0,), (1,)))
                value = value + bias[:, 0:1]
            value = value.astype(BF16).reshape(per_head, HP, LEN)
            proj[kind, part * per_head : (part + 1) * per_head] = value

    pick_hot = hot_rows(pick_columns[:, 0:1], LEN)
    allowed = pick_columns[:, 1:2] == sent_row[...]
    masks = pick_columns.shape[0]
    branch = jnp.zeros((masks, D), F32)
    for part in range(m):
        wide_out = mm(spread, attn_out[part], TN).astype(BF16)
        for index in range(per_head):
            head = part * per_head + index
            query = mm(pick_hot, proj[0, head], NT).astype(BF16)
            value = softmax_rows(mm(query, proj[1, head], NN) * HD ** (-0.5), allowed)
            prob[head] = value
            mix = mm(value.astype(BF16), proj[2, head], NT).astype(BF16)
            mixed[part, :, index * HP : (index + 1) * HP] = mix
            branch = branch + mm(mix, wide_out[index * HP : (index + 1) * HP, :], NN)
    state_one, (normed, inverse) = norm_forward(
        exact(pick_hot, state, NN) + branch + row(4), row(0), row(1)
    )
    normed_one[...] = normed
    inverse_one[...] = inverse
    low = state_one.astype(BF16)
    state_low[...] = low
    branch = jnp.zeros((masks, D), F32)
    for part in range(m):
        pre = mm(low, ffn_in[part], NN) + up_bias[part].astype(F32)
        pre_act[part] = pre
        act = (0.5 * pre * (1.0 + lax.erf(pre * ROOT_HALF))).astype(BF16)
        hidden_act[part] = act
        branch = branch + mm(act, ffn_out[part], NN)
    state_two, (normed, inverse) = norm_forward(state_one + branch + row(5), row(2), row(3))
    normed_two[...] = normed
    inverse_two[...] = inverse
    chosen[...] = jnp.zeros_like(chosen)
    chosen[:, 0:D] = state_two.astype(BF16)
    chosen[:, D : D + 3] = log_parts[...]


def backward_kernel(
    last_sentence,
    grad_pick,
    columns,
    pick_columns,
    pos_row,
    sent_row,
    attn_in,
    attn_out,
    ffn_in,
    ffn_out,
    shared_half,
    normed_zero,
    inverse_zero,
    proj,
    prob,
    mixed,
    normed_one,
    inverse_one,
    state_low,
    pre_act,
    hidden_act,
    normed_two,
    inverse_two,
    teacher,
    map_q_low,
    map_k_low,
    map_q_high,
    map_k_high,
    grad_attn_in,
    grad_attn_out,
    grad_ffn_in,
    grad_ffn_out,
    grad_shared,
    grad_qv,
    grad_up,
    word_grads,
    slot_grads,
    shared,
    grad_proj,
    wide_out,
):
    m, _, _, width = attn_in.shape
    per_head = width // HD
    pos = pick_columns[:, 0:1]
    pick_sentence = pick_columns[:, 1:2]
    masks = pos.shape[0]
    for part in range(m):
        shared[:, part * width : (part + 1) * width] = shared_half[part, LEN:, :].astype(F32)
    row = lambda index: shared[index : index + 1, :]
    spread = head_spread(width, per_head)
    score_scale = HD ** (-0.5)

    repeats = pos == pos_row[...]
    order = lax.broadcasted_iota(jnp.int32, (masks, masks), 1)
    lead = jnp.min(jnp.where(repeats, order, masks).astype(F32), axis=1, keepdims=True)
    leads = lead == lax.broadcasted_iota(jnp.int32, (masks, 1), 0).astype(F32)
    gradient = exact(jnp.where(repeats, 1.0, 0.0).astype(BF16), grad_pick[...], NN)
    gradient = jnp.where(leads, gradient, 0.0)

    grad_res, gain_two, bias_two = norm_pull(
        gradient, normed_two[...], inverse_two[...], row(6)
    )
    grad_branch = grad_res.astype(BF16)
    grad_one = grad_res
    for part in range(m):
        pre = pre_act[part]
        grad_hidden = mm(grad_branch, ffn_out[part], NT)
        slope = 0.5 * (1.0 + lax.erf(pre * ROOT_HALF)) + pre * jnp.exp(-0.5 * pre * pre) * BELL
        grad_pre = (grad_hidden * slope).astype(BF16)
        grad_ffn_out[part] = mm(hidden_act[part], grad_branch, TN)
        grad_ffn_in[part] = mm(state_low[...], grad_pre, TN)
        grad_up[part] = jnp.sum(grad_pre.astype(F32), 0, keepdims=True)
        grad_one = grad_one + mm(grad_pre, ffn_in[part], NT)
    grad_mid, gain_one, bias_one = norm_pull(grad_one, normed_one[...], inverse_one[...], row(4))
    grad_attended = grad_mid.astype(BF16)

    pick_hot = hot_rows(pos, LEN)
    allowed = pick_sentence == sent_row[...]
    weight = jnp.where(pick_sentence < last_sentence[0], 2.0 * ATT_WEIGHT, 0.0)
    for part in range(m):
        narrow = mm(mixed[part], spread, NT).astype(BF16)
        grad_attn_out[part] = mm(narrow, grad_attended, TN)
        wide_out[part] = mm(spread, attn_out[part], TN).astype(BF16)
        for index in range(per_head):
            head = part * per_head + index
            at = slice(head * HP, (head + 1) * HP)
            map_q, map_k = (map_q_low, map_k_low) if head < HEADS // 2 else (map_q_high, map_k_high)
            grad_mixed = mm(
                grad_attended, wide_out[part, index * HP : (index + 1) * HP, :], NT
            ).astype(BF16)
            value = prob[head]
            teacher_query = mm(pick_hot, teacher[0, head], NT).astype(BF16)
            teacher_prob = softmax_rows(
                mm(teacher_query, teacher[1, head], NN) * THD ** (-0.5), allowed
            )
            grad_prob = mm(grad_mixed, proj[2, head], NN) + (value - teacher_prob) * weight
            grad_proj[2, at, :] = mm(grad_mixed, value.astype(BF16), TN).astype(BF16)
            grad_scores = value * (
                grad_prob - jnp.sum(value * grad_prob, axis=-1, keepdims=True)
            )
            grad_scores = jnp.where(leads, grad_scores, 0.0).astype(BF16)
            grad_query = (mm(grad_scores, proj[1, head], NT) * score_scale).astype(BF16)
            grad_proj[0, at, :] = (
                map_q[head % (HEADS // 2)] * score_scale + mm(grad_query, pick_hot, TN)
            ).astype(BF16)
            query = mm(pick_hot, proj[0, head], NT).astype(BF16)
            grad_proj[1, at, :] = (
                (map_k[head % (HEADS // 2)] + mm(query, grad_scores, TN)) * score_scale
            ).astype(BF16)

    normed = normed_zero[...]
    gathered = (normed * row(2) + row(3)).astype(BF16)
    grad_in = exact(pick_hot, grad_mid, TN)
    ones = jnp.ones((8, LEN), BF16)
    for part in range(m):
        for kind in range(3):
            first = part * per_head * HP
            narrow = mm(spread, grad_proj[kind, first : first + per_head * HP, :], NN).astype(BF16)
            grad_attn_in[part, kind] = mm(gathered, narrow, ((0,), (1,)))
            grad_in = grad_in + mm(narrow, attn_in[part, kind], ((0,), (1,)))
            if kind != 1:
                sums = mm(ones, narrow, NT)
                grad_qv[part, kind // 2 : kind // 2 + 1, :] = sums[0:1, :]
    grad_embed, gain_zero, bias_zero = norm_pull(grad_in, normed, inverse_zero[...], row(2))
    low = grad_embed.astype(BF16)
    word_grads[...] = low
    slot_grads[...] = mm(hot_rows(columns[:, 5:6], slot_grads.shape[0]), low, TN).astype(BF16)
    positions = exact(hot_rows(columns[:, 0:1], LEN), grad_embed, TN, 2)
    ones_type = columns[:, 1:2] == 1
    rows = [
        jnp.sum(jnp.where(ones_type, 0.0, grad_embed), axis=0, keepdims=True),
        jnp.sum(jnp.where(ones_type, grad_embed, 0.0), axis=0, keepdims=True),
        gain_zero,
        bias_zero,
        gain_one,
        bias_one,
        gain_two,
        bias_two,
        jnp.sum(grad_mid, axis=0, keepdims=True),
        jnp.sum(grad_res, axis=0, keepdims=True),
    ]
    for part in range(m):
        at = slice(part * width, (part + 1) * width)
        grad_shared[part, 0:LEN, :] = positions[:, at]
        for index, value in enumerate(rows):
            grad_shared[part, LEN + index : LEN + index + 1, :] = value[:, at]


def logits_kernel(block, places, chosen, words, out):
    logits = mm(chosen[:, 0:D], words[...], NT) * (1.0 / SOFTEN_FACTOR)
    column = lax.broadcasted_iota(jnp.int32, logits.shape, 1)
    own = column < places[1]
    logits = jnp.where(own, logits, -1e30)
    top = jnp.max(logits, axis=-1, keepdims=True)
    total = jnp.sum(jnp.where(own, jnp.exp(logits - top), 0.0), axis=-1, keepdims=True)
    lane = lax.broadcasted_iota(jnp.int32, (block, LANES), 1)
    both = jnp.where(lane == 0, top, jnp.where(lane == 1, total, 0.0))
    out[...] = jnp.transpose(both)[0:8, :]


def logits_stats(plan, place, chosen, words):
    picks = chosen.shape[0]
    block = 256
    return pl.pallas_call(
        functools.partial(logits_kernel, block),
        out_shape=jax.ShapeDtypeStruct((8, picks), F32),
        grid=(picks // block,),
        in_specs=[
            pl.BlockSpec(memory_space=pltpu.SMEM),
            pl.BlockSpec((block, chosen.shape[1]), lambda i: (i, 0)),
            pl.BlockSpec(words.shape, lambda i: (0, 0)),
        ],
        out_specs=pl.BlockSpec((8, block), lambda i: (0, i)),
        compiler_params=pltpu.CompilerParams(vmem_limit_bytes=VMEM_BYTES),
    )(place, chosen, words)


def grad_logits_kernel(block, places, chosen, words, mentor, stats, grads, pulled, losses):
    step = pl.program_id(0)
    log_total = stats[0:1, :] + jnp.log(stats[1:2, :])
    column_total = jnp.transpose(jnp.broadcast_to(log_total, (LANES, block)))[:, 0:1]
    logits = mm(chosen[:, 0:D], words[...], NT) * (1.0 / SOFTEN_FACTOR)
    column = lax.broadcasted_iota(jnp.int32, logits.shape, 1)
    own = column < places[1]
    parts = chosen[:, D : D + 3].astype(F32)
    mentor_total = jnp.sum(parts, axis=-1, keepdims=True)
    target = jnp.exp(mentor[...].astype(F32) * (1.0 / SOFTEN_FACTOR) - mentor_total)
    target = jnp.where(own, target, 0.0)
    student = jnp.where(own, jnp.exp(jnp.where(own, logits, -1e30) - column_total), 0.0)
    value = ((student - target) * (1.0 / SOFTEN_FACTOR)).astype(BF16)
    grads[...] = value
    pulled[...] = mm(value, words[...], NN)

    @pl.when(step == 0)
    def _():
        losses[...] = jnp.zeros_like(losses)

    cross = jnp.sum(jnp.sum(target * logits, axis=0, keepdims=True), axis=1, keepdims=True)
    own_share = jnp.sum(log_total, axis=1, keepdims=True)
    row = lax.broadcasted_iota(jnp.int32, (8, LANES), 0)
    losses[...] += jnp.where(row == 0, cross, jnp.where(row == 1, own_share, 0.0))


def grad_logits_call(plan, place, chosen, words, mentor, stats):
    picks = chosen.shape[0]
    block = 256
    rows = words.shape[0]
    return pl.pallas_call(
        functools.partial(grad_logits_kernel, block),
        out_shape=[
            jax.ShapeDtypeStruct((picks, rows), BF16),
            jax.ShapeDtypeStruct((picks, D), F32),
            jax.ShapeDtypeStruct((8, LANES), F32),
        ],
        grid=(picks // block,),
        in_specs=[
            pl.BlockSpec(memory_space=pltpu.SMEM),
            pl.BlockSpec((block, chosen.shape[1]), lambda i: (i, 0)),
            pl.BlockSpec(words.shape, lambda i: (0, 0)),
            pl.BlockSpec((block, rows), lambda i: (i, 0)),
            pl.BlockSpec((2, block), lambda i: (0, i)),
        ],
        out_specs=[
            pl.BlockSpec((block, rows), lambda i: (i, 0)),
            pl.BlockSpec((block, D), lambda i: (i, 0)),
            pl.BlockSpec((8, LANES), lambda i: (0, 0)),
        ],
        compiler_params=pltpu.CompilerParams(vmem_limit_bytes=VMEM_BYTES),
    )(place, chosen, words, mentor, stats)


def dot(spec, left, right, **options):
    return jnp.einsum(spec, left, right, preferred_element_type=F32, **options)


def one_hot(index, size):
    return (index[:, None] == jnp.arange(size, dtype=jnp.int32)[None, :]).astype(BF16)


def norm_forward(value, gain_row, bias_row):
    centred = value - jnp.mean(value, axis=-1, keepdims=True)
    inverse = lax.rsqrt(jnp.mean(centred * centred, axis=-1, keepdims=True) + NORM_EPS)
    normed = centred * inverse
    return (normed * gain_row + bias_row, (normed, inverse))


def local(
    master,
    first_moment,
    second_moment,
    token_ids,
    token_types,
    counts,
    mask_pos,
    teacher_states,
    teacher_qk,
    mentor_logits,
):
    n, m = lax.axis_size("dp"), lax.axis_size("head")
    d, h = lax.axis_index("dp"), lax.axis_index("head")
    share_len = master.shape[1]
    assert share_len % LANES == 0 and token_ids.shape[0] == m
    plan = Plan(n, m, share_len)
    share = plan.rows_share
    devices = n * m
    slots = max(8, 1024 // devices)
    masks = mask_pos.shape[1]
    picks = devices * masks

    own_row = lambda value: lax.dynamic_index_in_dim(value, h, 0, keepdims=False)
    ids, types, sizes, pos = (own_row(v) for v in (token_ids, token_types, counts, mask_pos))

    vocab_head = ids // plan.vocab
    vocab_row = ids - vocab_head * plan.vocab
    owner = (vocab_row * D) // share_len * m + vocab_head
    order = jnp.arange(LEN, dtype=jnp.int32)
    same = ids[:, None] == ids[None, :]
    leader = jnp.min(jnp.where(same, order[None, :], LEN), axis=1)
    leads = leader == order
    rank = jnp.sum(
        (owner[:, None] == owner[None, :]) & leads[None, :] & (order[None, :] < leader[:, None]),
        axis=1,
        dtype=jnp.int32,
    )
    rounds_here = jnp.max(rank) // slots + 1

    def token_slots(turn):
        place = rank - turn * slots
        return jnp.where((place >= 0) & (place < slots), owner * slots + place, -1)

    def slots_sent(turn, extra):
        slot = token_slots(turn)
        hit = jnp.arange(devices * slots, dtype=jnp.int32)[:, None] == slot[None, :]
        wanted = jnp.max(jnp.where(hit, vocab_row[None, :], -1), axis=1).reshape(devices, slots)
        sent = jnp.concatenate(
            [wanted, jnp.broadcast_to(extra, (devices, 1)).astype(jnp.int32)], axis=1
        )
        return jnp.pad(sent, ((0, 0), (0, ceil_to(slots + 1, LANES) - slots - 1)))

    def ask(sent):
        got = lax.all_to_all(sent, BOTH, 0, 0, tiled=True)
        asked = got[:, :slots].reshape(-1)
        return asked, got[:, slots]

    first_row = jnp.minimum((d * share_len + D - 1) // D, plan.vocab)
    row_count = jnp.minimum(((d + 1) * share_len + D - 1) // D, plan.vocab) - first_row

    chunk = master.reshape(share, 1, LANES)
    after = lax.ppermute(
        master[0, : 8 * LANES].reshape(8, LANES), "dp", [(i + 1, i) for i in range(n - 1)]
    )
    shift = jnp.where(row_count > 0, first_row * D - d * share_len, 0)
    place = jnp.stack([shift, row_count, d, h]).astype(jnp.int32)
    if plan.special:
        tail_part = share_rows(plan, place, chunk)
    else:
        tail_part = chunk.reshape(share, LANES).astype(BF16)

    room = plan.rows
    cuts = (0, 32)
    counts_of = [b - a for a, b in zip(cuts, cuts[1:] + (m * masks,))]
    blocks = call(
        functools.partial(mentor_kernel, plan, room, cuts),
        [jax.ShapeDtypeStruct((n, count, room), BF16) for count in counts_of],
        mentor_logits,
    )
    send_mentor = lambda block: lax.all_to_all(block, "dp", 0, 0, tiled=False)
    sent_first, tail_part = lax.optimization_barrier((slots_sent(0, rounds_here), tail_part))
    words_own = table_rows(plan, place, chunk, after)

    own_index = lambda asked: jnp.where(asked >= 0, asked - first_row, -1)

    def fetch(turn, asked):
        rows = dot(
            "sv,vd->sd", one_hot(own_index(asked), plan.rows), words_own
        ).astype(BF16)
        return lax.all_to_all(
            rows.reshape(devices, slots, D), BOTH, 0, 0, tiled=True
        ).reshape(-1, D)

    asked_first, needs = ask(sent_first)
    if plan.special:
        tail_part = tail_along_z(tail_to_plane(plan, tail_part), 0)
        asked_first, tail_part = lax.optimization_barrier((asked_first, tail_part))
    rounds = jnp.max(needs)
    back = fetch(0, asked_first)
    more_words = lax.while_loop(
        lambda state: state[0] < rounds,
        lambda state: (
            state[0] + 1,
            add_rows(
                NN,
                token_slots(state[0]),
                fetch(state[0], ask(slots_sent(state[0], rounds_here))[0]),
                state[1],
            ),
        ),
        (jnp.int32(1), jnp.zeros((LEN, D), F32)),
    )[1]
    if plan.special:
        tail_own = tail_in_plane(tail_along_z(tail_part, 1), n)
    else:
        tail_own = [gather_tail(plan, tail_part)]

    mentor = mentor_logits.reshape(m * masks, plan.vocab)
    halved = mentor.astype(F32) / SOFTEN_FACTOR
    mentor_top = jnp.max(halved, axis=-1)
    mentor_sum = jnp.sum(jnp.exp(halved - mentor_top[:, None]), axis=-1)
    pairs = join_heads(jnp.stack([mentor_top, mentor_sum]), h, m)
    top = jnp.max(pairs[:, 0], axis=0)
    log_total = top + jnp.log(jnp.sum(pairs[:, 1] * jnp.exp(pairs[:, 0] - top), axis=0))
    part_a = log_total.astype(BF16)
    part_b = (log_total - part_a.astype(F32)).astype(BF16)
    part_c = (log_total - part_a.astype(F32) - part_b.astype(F32)).astype(BF16)
    log_parts = own_row(jnp.stack([part_a, part_b, part_c], axis=-1).reshape(m, masks, 3))

    teacher_weight = join_heads(teacher_qk, h, m)
    states = own_row(teacher_states)
    teacher_proj = dot("hdce,ld->chel", teacher_weight, states).astype(BF16)
    teacher_proj = teacher_proj.reshape(2, HEADS, THD, LEN)

    back, tail_own, teacher_proj, log_parts, blocks = lax.optimization_barrier(
        (back, tail_own, teacher_proj, log_parts, blocks)
    )
    mentor_a = send_mentor(blocks[0])
    tail_other = [swap(part, "head", 1, 2) if m == 2 else part for part in tail_own]
    weights = unpack_tail(plan, place, tail_own, tail_other)

    ends = jnp.cumsum(sizes)
    passed = (order[:, None] >= ends[None, :]).astype(jnp.int32)
    sentence = jnp.sum(passed, axis=-1)
    within = order - jnp.sum(passed * sizes[None, :], axis=-1)
    valid = (sentence < sizes.shape[0] - 1).astype(jnp.int32)

    pick_sentence = jnp.sum(jnp.where(pos[:, None] == order[None, :], sentence[None, :], 0), 1)
    picked_any = jnp.sum((pos[:, None] == order[None, :]).astype(jnp.int32), axis=0) > 0
    columns = [within, types, sentence, valid, 1 - picked_any.astype(jnp.int32), token_slots(0)]
    columns = jnp.stack(columns + [order, order], axis=1)
    pick_columns = jnp.stack([pos, pick_sentence], axis=1)
    attn_in, attn_out, ffn_in, ffn_out, shared_half, qv_bias, up_bias = weights
    shape = jax.ShapeDtypeStruct
    chosen_own, *saved = call(
        forward_kernel,
        [
            shape((masks, 3 * LANES), BF16),
            shape((LEN, D), F32),
            shape((LEN, 1), F32),
            shape((3, HEADS, HP, LEN), BF16),
            shape((HEADS, masks, LEN), F32),
            shape((m, masks, plan.width // HD * HP), BF16),
            shape((masks, D), F32),
            shape((masks, 1), F32),
            shape((masks, D), BF16),
            shape((m, masks, plan.units), F32),
            shape((m, masks, plan.units), BF16),
            shape((masks, D), F32),
            shape((masks, 1), F32),
        ],
        back,
        more_words,
        columns,
        pick_columns,
        sentence[None],
        log_parts,
        *weights,
        scratch=[pltpu.VMEM((SROWS, D), F32)],
    )
    proj = saved[2]

    halves = [
        map_attention(first, HEADS // 2, proj, teacher_proj, columns, sentence[None])
        for first in (0, HEADS // 2)
    ]

    chosen_own, mentor_a = lax.optimization_barrier((chosen_own, mentor_a))
    chosen = join_heads(gather_to_all(chosen_own, plan), h, m)
    chosen = jnp.swapaxes(chosen, 0, 1).reshape(picks, 3 * LANES)
    chosen, last_block = lax.optimization_barrier((chosen, blocks[1]))
    mentor_b = send_mentor(last_block)
    stats = merge_stats(logits_stats(plan, place, chosen, words_own)[:2], plan)
    halves[0], mentor_b, stats = lax.optimization_barrier((halves[0], mentor_b, stats))
    mentor_here = jnp.concatenate([mentor_a, mentor_b], axis=1).reshape(picks, room)
    grad_logits, grad_chosen, losses = grad_logits_call(
        plan, place, chosen, words_own, mentor_here, stats
    )
    map_rows = halves[0][2] + halves[1][2]
    loss_local = jnp.sum(map_rows) + losses[1, 0] / devices - losses[0, 0]
    grad_chosen = grad_chosen.reshape(n, m, masks, D)
    if m == 2:
        mine = lax.dynamic_index_in_dim(grad_chosen, h, 1, keepdims=False)
        other = lax.dynamic_index_in_dim(grad_chosen, 1 - h, 1, keepdims=False)
        mine = mine + swap(other.astype(BF16), "head", 1, 2).astype(F32)
    else:
        mine = lax.psum_scatter(grad_chosen, "head", scatter_dimension=1, tiled=False)
    grad_pick = jnp.sum(
        lax.all_to_all(mine.astype(BF16), "dp", 0, 0, tiled=False).astype(F32), axis=0
    )

    *piece_grads, word_grads, slot_grads = call(
        backward_kernel,
        [
            shape((m, 3, D, plan.width), F32),
            shape((m, plan.width, D), F32),
            shape((m, D, plan.units), F32),
            shape((m, plan.units, D), F32),
            shape((m, SROWS, plan.width), F32),
            shape((m, 2, plan.width), F32),
            shape((m, 1, plan.units), F32),
            shape((LEN, D), BF16),
            shape((devices * slots, D), BF16),
        ],
        jnp.array([sizes.shape[0] - 1], jnp.int32),
        grad_pick,
        columns,
        pick_columns,
        pos[None],
        sentence[None],
        attn_in,
        attn_out,
        ffn_in,
        ffn_out,
        shared_half,
        *saved,
        teacher_proj,
        *halves[0][:2],
        *halves[1][:2],
        scratch=[
            pltpu.VMEM((SROWS - LEN, D), F32),
            pltpu.VMEM((3, HEADS * HP, LEN), BF16),
            pltpu.VMEM((m, plan.width // HD * HP, D), BF16),
        ],
        smem=1,
    )

    def give(slot_grads):
        return lax.all_to_all(
            slot_grads.reshape(devices, slots, D), BOTH, 0, 0, tiled=True
        ).reshape(-1, D)

    def give_more(turn):
        hot = one_hot(token_slots(turn), devices * slots)
        return give(dot("ts,td->sd", hot, word_grads).astype(BF16))

    given = give(slot_grads)
    if m == 2:
        tail_got = swap(pack_tail(plan, 1 - h, piece_grads), "head", 1, 2)
        tail_kept = pack_tail(plan, h, piece_grads)
        tail_got, tail_kept, given = lax.optimization_barrier((tail_got, tail_kept, given))
    else:
        tail_kept = pack_tail(plan, h, piece_grads)
        tail_got = jnp.zeros_like(tail_kept)
    tail_grad = reduce_tail(plan, tail_kept, tail_got)

    grad_table = call(
        rows_grad_kernel,
        jax.ShapeDtypeStruct((plan.rows, D), F32),
        place,
        grad_logits,
        chosen,
        own_index(asked_first)[:, None],
        given,
        smem=1,
    )
    grad_table = lax.while_loop(
        lambda state: state[0] < rounds,
        lambda state: (
            state[0] + 1,
            add_rows(
                TN,
                own_index(ask(slots_sent(state[0], rounds_here))[0]),
                give_more(state[0]),
                state[1],
            ),
        ),
        (jnp.int32(1), grad_table),
    )[1]
    last_row = lax.dynamic_slice_in_dim(grad_table, jnp.maximum(row_count - 1, 0), 1)
    before = lax.ppermute(
        jnp.broadcast_to(last_row, (8, D)), "dp", [(i, i + 1) for i in range(n - 1)]
    )
    table_lines = table_pack(plan, place, grad_table, before)

    gradient, numbers = merge(
        plan, place, loss_local.reshape(1), table_lines, tail_grad
    )

    numbers = total_all(numbers, plan)
    loss_sum, grad_norm = numbers[1, 0], jnp.sqrt(numbers[0, 0])
    scale = CLIP_NORM / jnp.maximum(grad_norm, CLIP_NORM)
    vector_start = plan.table + plan.width * D * 4 + 2 * D * plan.units + (LEN + 2) * plan.width
    whole = jax.ShapeDtypeStruct((1, share_len), F32)
    updated = call(
        functools.partial(adam_kernel, plan, vector_start),
        [whole, whole, whole, jax.ShapeDtypeStruct((1, share_len), BF16)],
        place,
        scale.reshape(1),
        master,
        gradient.reshape(1, share_len),
        first_moment,
        second_moment,
        smem=2,
    )
    return (loss_sum, grad_norm, *updated)


def solution(mesh):
    return jax.shard_map(
        local,
        mesh=mesh,
        in_specs=(
            P("head", "dp"),
            P("head", "dp"),
            P("head", "dp"),
            P("dp", None),
            P("dp", None),
            P("dp", None),
            P("dp", None),
            P("dp", None, None),
            P(None, None, "head"),
            P("dp", None, "head"),
        ),
        out_specs=(P(), P(), P("head", "dp"), P("head", "dp"), P("head", "dp"), P("head", "dp")),
        check_vma=False,
    )
```

```python
import functools

import jax
import jax.numpy as jnp
from jax import lax
from jax.experimental import pallas as pl
from jax.experimental.pallas import tpu as pltpu
from jax.sharding import PartitionSpec as P

D = 312
HEADS = 12
HD = 26
HP = 32
FF = 1200
VOCAB = 30522
THD = 64
LEN = 512
STEP = 10
SROWS = 522

ATT_WEIGHT = 1.0
SOFTEN_FACTOR = 2.0
CLIP_NORM = 1.0
BETA_ONE = 0.9
BETA_TWO = 0.999
RATE_MATRIX = 0.06
RATE_VECTOR = 0.6
WEIGHT_DECAY = 0.01
ADAM_EPS = 1e-08
NORM_EPS = 1e-12
MASKED = -1000000000.0

F32 = jnp.float32
BF16 = jnp.bfloat16
LANES = 128
BOTH = ("dp", "head")
VMEM_BYTES = 56 * 1024 * 1024


def ceil_to(value, unit):
    return -(-value // unit) * unit


def call(kernel, out_shape, *args, scratch=(), smem=0, hbm=(), hbm_out=()):
    space = lambda index: pltpu.SMEM if index < smem else pl.ANY if index in hbm else pltpu.VMEM
    in_specs = [pl.BlockSpec(memory_space=space(index)) for index in range(len(args))]
    outs = out_shape if isinstance(out_shape, list) else [out_shape]
    out_specs = [
        pl.BlockSpec(memory_space=pl.ANY if index in hbm_out else pltpu.VMEM)
        for index in range(len(outs))
    ]
    out_specs = out_specs if isinstance(out_shape, list) else out_specs[0]
    return pl.pallas_call(
        kernel,
        out_shape=out_shape,
        in_specs=in_specs,
        out_specs=out_specs,
        scratch_shapes=list(scratch),
        compiler_params=pltpu.CompilerParams(vmem_limit_bytes=VMEM_BYTES),
    )(*args)


class Plan:
    def __init__(self, n, m, share):
        self.n, self.m, self.share = n, m, share
        self.rows_share = share // LANES
        self.vocab = VOCAB // m
        self.width = D // m
        self.units = FF // m
        self.first = [min(-(-d * share // D), self.vocab) for d in range(n + 1)]
        widest = -(-share // D)
        self.rows = ceil_to(widest + 3, 16)
        table = self.vocab * D
        self.table = table
        self.tail_row = table // LANES
        self.tail_off = table % LANES
        self.tail_rows = n * self.rows_share - self.tail_row
        self.tail_pad = ceil_to(self.tail_rows + 40, 16)
        w, u = self.width, self.units
        self.pieces = []
        base = self.tail_off
        for rows, wide in ((3 * D, w), (w, D), (D, u), (u, D), (SROWS, w), (2, w), (1, u)):
            self.pieces.append((base, wide, rows))
            base += rows * wide
        self.special = n == 16 and self.tail_row // self.rows_share == n - 2
        if self.special:
            self.low_rows = (n - 1) * self.rows_share - self.tail_row
            self.slice_rows = ceil_to(-(-self.rows_share // 8), 16)
            self.half_rows = 4 * self.slice_rows


def period(width):
    step = 16
    while step * width % LANES:
        step *= 2
    return step, step * width // LANES


def rows_at(start, count, stride):
    return pl.ds(start, count) if count == 1 else pl.ds(start, count, stride=stride)


def spread_rows(src, dst, base, width, rows):
    step, lane_rows = period(width)
    tiles = -(-width // LANES)
    for phase in range(min(step, rows)):
        count = len(range(phase, rows, step))
        line, off = divmod(base + phase * width, LANES)
        loaded = [
            src[rows_at(line + j, count, lane_rows), :] for j in range(tiles + (1 if off else 0))
        ]
        lane = lax.broadcasted_iota(jnp.int32, (count, LANES), 1)
        for tile in range(tiles):
            value = loaded[tile]
            if off:
                value = jnp.where(
                    lane < LANES - off,
                    pltpu.roll(value, LANES - off, 1),
                    pltpu.roll(loaded[tile + 1], LANES - off, 1),
                )
            dst[tile, rows_at(phase, count, step), :] = value


def pack_rows(src, dst, base, width, rows):
    step, lane_rows = period(width)
    tiles = -(-width // LANES)
    for phase in range(min(step, rows)):
        count = len(range(phase, rows, step))
        line, off = divmod(base + phase * width, LANES)
        loaded = [
            src[tile, rows_at(phase, count, step), :] for tile in range(tiles)
        ]
        lane = lax.broadcasted_iota(jnp.int32, (count, LANES), 1)
        rolled = [pltpu.roll(value, off, 1) if off else value for value in loaded]
        for j in range(-(-(off + width) // LANES)):
            value = jnp.zeros((count, LANES), F32)
            if j < tiles:
                value = jnp.where(lane >= off, rolled[j], value)
            if off and j > 0:
                value = jnp.where(lane < off, rolled[j - 1], value)
            at = rows_at(line + j, count, lane_rows)
            dst[at, :] = dst[at, :] + value


def column_tiles(width):
    return [(t, t * LANES, min(LANES, width - t * LANES)) for t in range(-(-width // LANES))]


def shift_lines(source, count, start, max_line):
    low, high = start // LANES, lax.rem(start, LANES)
    first = source[0:count, :]
    second = source[1 : count + 1, :]
    for line in range(1, max_line + 1):
        first = jnp.where(low == line, source[line : count + line, :], first)
        second = jnp.where(low == line, source[line + 1 : count + line + 1, :], second)
    lane = lax.broadcasted_iota(jnp.int32, (count, LANES), 1)
    back = lax.rem(LANES - high, LANES)
    return jnp.where(lane < LANES - high, pltpu.roll(first, back, 1), pltpu.roll(second, back, 1))


def bring(source, target, sem):
    copy = pltpu.make_async_copy(source, target, sem)
    copy.start()
    copy.wait()


def share_rows_kernel(plan, place, chunk, out, lines, sem):
    share, low = plan.rows_share, plan.low_rows
    lines[share & -8 :, :] = jnp.zeros((lines.shape[0] - (share & -8), LANES), F32)
    bring(chunk.at[:, 0, :], lines.at[0:share], sem)
    count = out.shape[0]
    begins_late = place[2] == plan.n - 2
    first = share - low
    out[...] = jnp.where(
        begins_late, lines[first : first + count, :], lines[0:count, :]
    ).astype(BF16)


def share_rows(plan, place, chunk):
    count = 8 * plan.slice_rows
    return call(
        functools.partial(share_rows_kernel, plan),
        jax.ShapeDtypeStruct((count, LANES), BF16),
        place,
        chunk,
        scratch=[
            pltpu.VMEM((ceil_to(count + plan.rows_share - plan.low_rows, 8), LANES), F32),
            pltpu.SemaphoreType.DMA,
        ],
        smem=1,
        hbm=(1,),
    )


def table_rows_kernel(plan, place, chunk, after, out, joined, shifted, rows, sem):
    share = plan.rows_share
    lines = joined.shape[0]
    joined[share & -8 :, :] = jnp.zeros((lines - (share & -8), LANES), F32)
    bring(chunk.at[:, 0, :], joined.at[0:share], sem)
    joined[share : share + 8, :] = after[...]
    shifted[...] = jnp.zeros_like(shifted)
    shifted[0 : share + 2, :] = shift_lines(joined, share + 2, place[0], 2)
    spread_rows(shifted, rows, 0, D, plan.rows)
    row = lax.broadcasted_iota(jnp.int32, (plan.rows, LANES), 0)
    for tile, left, wide in column_tiles(D):
        value = jnp.where(row < place[1], rows[tile], 0.0).astype(BF16)
        out[:, left : left + wide] = value[:, 0:wide]


def table_rows(plan, place, chunk, after):
    lines = ceil_to(max(plan.rows_share + 16, plan.rows // 16 * 39 + 2), 8)
    return call(
        functools.partial(table_rows_kernel, plan),
        jax.ShapeDtypeStruct((plan.rows, D), BF16),
        place,
        chunk,
        after,
        scratch=[
            pltpu.VMEM((lines, LANES), F32),
            pltpu.VMEM((lines, LANES), F32),
            pltpu.VMEM((3, plan.rows, LANES), F32),
            pltpu.SemaphoreType.DMA,
        ],
        smem=1,
        hbm=(1,),
    )


def table_pack_kernel(plan, place, grads, out, rows, lines):
    rows[...] = jnp.zeros_like(rows)
    for tile, left, wide in column_tiles(D):
        rows[tile, 16 : 16 + plan.rows, 0:wide] = grads[:, left : left + wide]
    lines[...] = jnp.zeros_like(lines)
    pack_rows(rows, lines, 0, D, plan.rows + 16)
    count = plan.rows_share + 8
    start = 39 * LANES - place[0]
    low, high = start // LANES - 36, lax.rem(start, LANES)
    first = lines[36 : 36 + count, :]
    second = lines[37 : 37 + count, :]
    for line in range(1, 4):
        first = jnp.where(low == line, lines[36 + line : 36 + line + count, :], first)
        second = jnp.where(low == line, lines[37 + line : 37 + line + count, :], second)
    lane = lax.broadcasted_iota(jnp.int32, (count, LANES), 1)
    back = lax.rem(LANES - high, LANES)
    value = jnp.where(
        lane < LANES - high, pltpu.roll(first, back, 1), pltpu.roll(second, back, 1)
    )
    line = lax.broadcasted_iota(jnp.int32, (count, LANES), 0)
    index = (line + place[2] * plan.rows_share) * LANES + lane
    out[...] = jnp.where(index < plan.table, value, 0.0)


def merge_kernel(plan, place, loss, table, before, *refs):
    extra, (out, numbers, whole, sem) = refs[:-4], refs[-4:]
    share = plan.rows_share
    whole[...] = table[0:share, :]
    whole[0:8, :] = whole[0:8, :] + before[...]
    if plan.special:
        d, low = place[2], plan.low_rows
        for owner, first, count in ((plan.n - 2, share - low, low), (plan.n - 1, 0, share)):

            @pl.when(d == owner)
            def _(first=first, count=count):
                whole[first : first + count, :] = (
                    whole[first : first + count, :] + extra[0][0:count, :]
                )
    else:
        whole[...] = whole[...] + extra[0][...]
    copy = pltpu.make_async_copy(whole, out.at[:, 0, :], sem)
    copy.start()
    value = whole[...]
    squares = jnp.sum(jnp.sum(value * value, axis=0, keepdims=True), axis=1, keepdims=True)
    line = lax.broadcasted_iota(jnp.int32, (8, LANES), 0)
    numbers[...] = jnp.where(
        line == 0, jnp.broadcast_to(squares, (8, LANES)), jnp.where(line == 1, loss[0], 0.0)
    )
    copy.wait()


def merge(plan, place, loss, table, before, extra):
    return call(
        functools.partial(merge_kernel, plan),
        [
            jax.ShapeDtypeStruct((plan.rows_share, 1, LANES), F32),
            jax.ShapeDtypeStruct((8, LANES), F32),
        ],
        place,
        loss,
        table,
        before,
        extra,
        scratch=[pltpu.VMEM((plan.rows_share, LANES), F32), pltpu.SemaphoreType.DMA],
        smem=2,
        hbm_out=(0,),
    )


def adam_kernel(plan, edge, place, scale, master, gradient, first, second, *outs):
    new_master, new_first, new_second, new_weights = outs
    clipped = gradient[...] * scale[0]
    moment = BETA_ONE * first[...] + (1.0 - BETA_ONE) * clipped
    spread = BETA_TWO * second[...] + (1.0 - BETA_TWO) * clipped * clipped
    step = (
        moment
        / (1.0 - BETA_ONE**STEP)
        / (jnp.sqrt(spread / (1.0 - BETA_TWO**STEP)) + ADAM_EPS)
    )
    index = lax.broadcasted_iota(jnp.int32, step.shape, 1) + place[2] * plan.share
    matrix_part = index < edge
    rate = jnp.where(matrix_part, RATE_MATRIX, RATE_VECTOR)
    decay = jnp.where(matrix_part, WEIGHT_DECAY, 0.0)
    value = master[...] - rate * (step + decay * master[...])
    new_master[...] = value
    new_first[...] = moment
    new_second[...] = spread
    new_weights[...] = value.astype(BF16)


def mentor_kernel(plan, room, cuts, mentor, *refs):
    outs, stats = refs[:-1], refs[-1]
    m, masks, vocab = mentor.shape
    wide = 16 * LANES
    columns = []
    for part in range(m):
        pieces = [
            mentor[part, :, left : min(left + wide, vocab)].astype(F32) * (1.0 / SOFTEN_FACTOR)
            for left in range(0, vocab, wide)
        ]
        top = pieces[0]
        for piece in pieces[1:-1]:
            top = jnp.maximum(top, piece)
        top = jnp.maximum(
            jnp.max(top, axis=-1, keepdims=True), jnp.max(pieces[-1], axis=-1, keepdims=True)
        )
        total = jnp.exp(pieces[0] - top)
        for piece in pieces[1:-1]:
            total = total + jnp.exp(piece - top)
        total = jnp.sum(total, axis=-1, keepdims=True) + jnp.sum(
            jnp.exp(pieces[-1] - top), axis=-1, keepdims=True
        )
        columns.append((top, total))
    lane = lax.broadcasted_iota(jnp.int32, (m * masks, LANES), 1)
    top, total = (jnp.concatenate([column[k] for column in columns]) for k in range(2))
    both = jnp.where(lane == 0, top, jnp.where(lane == 1, total, 0.0))
    both = jnp.concatenate([both, jnp.zeros((LANES - m * masks, LANES), F32)])
    stats[...] = jnp.transpose(both)[0:8, :]
    for owner in range(plan.n):
        low = plan.first[owner]
        high = min(low + room, vocab)
        if high <= low:
            for out in outs:
                out[owner] = jnp.zeros(out.shape[1:], BF16)
            continue
        left = low // LANES * LANES
        right = min(ceil_to(high, LANES), vocab)
        for part in range(m):
            value = mentor[part, :, left:right].astype(F32)
            value = jnp.pad(value, ((0, 0), (0, ceil_to(high, LANES) + LANES - right)))
            if low > left:
                value = pltpu.roll(value, value.shape[1] - (low - left), 1)
            if high - low < room:
                value = jnp.pad(value[:, : high - low], ((0, 0), (0, room - (high - low))))
            value = value[:, 0:room].astype(BF16)
            for out, start in zip(outs, cuts):
                first = max(start, part * masks)
                last = min(start + out.shape[1], (part + 1) * masks)
                if first < last:
                    out[owner, first - start : last - start, :] = value[
                        first - part * masks : last - part * masks, :
                    ]


def table_pack(plan, place, grads):
    lines = ceil_to(max(plan.rows_share + 48, (plan.rows // 16 + 1) * 39 + 2), 8)
    return call(
        functools.partial(table_pack_kernel, plan),
        jax.ShapeDtypeStruct((plan.rows_share + 8, LANES), F32),
        place,
        grads,
        scratch=[
            pltpu.VMEM((3, plan.rows + 16, LANES), F32),
            pltpu.VMEM((lines, LANES), F32),
        ],
        smem=1,
    )


def unpack_kernel(plan, place, *refs):
    count = 4 if plan.special else 1
    own, other, refs = refs[:count], refs[count : 2 * count], refs[2 * count :]
    outs, (lines, wide) = refs[:-2], refs[-2:]
    share = plan.rows_share

    def load(tails):
        if not plan.special:
            lines[...] = tails[0][...].astype(F32)
            return
        half = plan.half_rows
        for quarter in range(4):
            y, x = divmod(quarter, 2)
            first = y * half
            end = min(first + half, share if x else plan.low_rows)
            at = first + (plan.low_rows if x else 0)
            for k in range(4):

                @pl.when(lax.rem(place[2], 4) == quarter ^ k)
                def _(k=k, at=at, length=end - first):
                    lines[at : at + length, :] = tails[k][...].astype(F32)[0:length]

    mine = place[3] == pl.program_id(0)
    pl.when(mine)(lambda: load(own))
    pl.when(jnp.logical_not(mine))(lambda: load(other))
    for out, (base, width, rows) in zip(outs, plan.pieces):
        spread_rows(lines, wide, base, width, rows)
        for tile, left, part in column_tiles(width):
            if len(out.shape) == 4:
                for kind in range(3):
                    value = wide[tile, kind * D : (kind + 1) * D, 0:part]
                    out[0, kind, :, left : left + part] = value.astype(BF16)
            else:
                out[0, :, left : left + part] = wide[tile, 0:rows, 0:part].astype(BF16)


def leading_block(value):
    rest = value.shape[1:]
    return pl.BlockSpec((1,) + rest, lambda i, *_: (i,) + (0,) * len(rest))


def unpack_tail(plan, place, own, other):
    m = plan.m
    shapes = [jax.ShapeDtypeStruct((m, rows, width), BF16) for _, width, rows in plan.pieces]
    shapes[0] = jax.ShapeDtypeStruct((m, 3, D, plan.width), BF16)
    tallest = max(rows for _, _, rows in plan.pieces)
    widest = max(-(-width // LANES) for _, width, _ in plan.pieces)
    return pl.pallas_call(
        functools.partial(unpack_kernel, plan),
        out_shape=shapes,
        grid=(m,),
        in_specs=[pl.BlockSpec(memory_space=pltpu.SMEM)]
        + [pl.BlockSpec(memory_space=pltpu.VMEM)] * (len(own) + len(other)),
        out_specs=[leading_block(shape) for shape in shapes],
        scratch_shapes=[
            pltpu.VMEM((plan.tail_pad, LANES), F32),
            pltpu.VMEM((widest, tallest, LANES), F32),
        ],
        compiler_params=pltpu.CompilerParams(vmem_limit_bytes=VMEM_BYTES),
    )(place, *own, *other)


def pack_kernel(plan, part_index, *refs):
    folding = plan.special and len(refs) == len(plan.pieces) + 4
    ins, refs = refs[: len(plan.pieces)], refs[len(plan.pieces) :]
    out, wide, lines = refs[-3:]
    lines[...] = refs[0][...] if len(refs) == 4 else jnp.zeros_like(lines)
    for source, (base, width, rows) in zip(ins, plan.pieces):
        for tile, left, part in column_tiles(width):
            if part < LANES:
                wide[tile, 0:rows, :] = jnp.zeros((rows, LANES), F32)
            if len(source.shape) == 4:
                for kind in range(3):
                    wide[tile, kind * D : (kind + 1) * D, 0:part] = source[
                        0, kind, :, left : left + part
                    ]
            else:
                wide[tile, 0:rows, 0:part] = source[0, :, left : left + part]
        pack_rows(wide, lines, base, width, rows)
    if not folding:
        out[...] = lines[...]
        return
    size, low, share = plan.slice_rows, plan.low_rows, plan.rows_share
    for index in range(8):
        for side, base, end in ((0, 0, low), (1, low, low + share)):
            first = base + index * size
            count = min(size, end - first)
            value = jnp.pad(lines[first : first + count, :], ((0, size - count), (0, 0)))
            out[2 * index + side] = value.astype(BF16)


def pack_tail(plan, part, pieces, *added):
    tallest = max(rows for _, _, rows in plan.pieces)
    widest = max(-(-width // LANES) for _, width, _ in plan.pieces)

    def chosen_block(value):
        rest = value.shape[1:]
        return pl.BlockSpec((1,) + rest, lambda i, part: (part[0],) + (0,) * len(rest))

    shape = jax.ShapeDtypeStruct((plan.tail_pad, LANES), F32)
    if plan.special and added:
        shape = jax.ShapeDtypeStruct((plan.n, plan.slice_rows, LANES), BF16)
    zeros = (0,) * len(shape.shape)
    return pl.pallas_call(
        functools.partial(pack_kernel, plan),
        out_shape=shape,
        grid_spec=pltpu.PrefetchScalarGridSpec(
            num_scalar_prefetch=1,
            grid=(1,),
            in_specs=[chosen_block(piece) for piece in pieces]
            + [pl.BlockSpec((plan.tail_pad, LANES), lambda i, part: (0, 0)) for _ in added],
            out_specs=pl.BlockSpec(shape.shape, lambda i, part: zeros),
            scratch_shapes=[
                pltpu.VMEM((widest, tallest, LANES), F32),
                pltpu.VMEM((plan.tail_pad, LANES), F32),
            ],
        ),
        compiler_params=pltpu.CompilerParams(vmem_limit_bytes=VMEM_BYTES),
    )(part.reshape(1).astype(jnp.int32), *pieces, *added)


def slots_kernel(plan, slots, turn, ids, sent, slot_col):
    vocab, m = plan.vocab, plan.m

    def parts(value):
        head = jnp.zeros(value.shape, jnp.int32)
        for index in range(1, m):
            head = head + jnp.where(value >= index * vocab, 1, 0)
        row = value - head * vocab
        owner = jnp.zeros(value.shape, jnp.int32)
        for first in plan.first[1 : plan.n]:
            owner = owner + jnp.where(row >= first, 1, 0)
        return row, owner * m + head

    ids_row = ids[0:1, :]
    ids_col = jnp.transpose(jnp.broadcast_to(ids_row.astype(F32), (LANES, LEN)))[:, 0:1]
    ids_col = ids_col.astype(jnp.int32)
    row_row, owner_row = parts(ids_row)
    row_col, owner_col = parts(ids_col)
    same = ids_col == ids_row
    along = lax.broadcasted_iota(jnp.int32, (LEN, LEN), 1)
    down = lax.broadcasted_iota(jnp.int32, (LEN, LEN), 0)
    leader = jnp.min(jnp.where(same, along, LEN).astype(F32), axis=1, keepdims=True)
    lead_row = jnp.min(jnp.where(same, down, LEN).astype(F32), axis=0, keepdims=True)
    leads = lead_row == along[0:1, :].astype(F32)
    ahead = (owner_col == owner_row) & leads & (along.astype(F32) < leader)
    rank = jnp.sum(jnp.where(ahead, 1.0, 0.0), axis=1, keepdims=True).astype(jnp.int32)
    place = rank - turn[0] * slots
    slot = jnp.where((place >= 0) & (place < slots), owner_col * slots + place, -1)
    slot_col[...] = slot
    lane = lax.broadcasted_iota(jnp.int32, (LEN, LANES), 1)
    most = jnp.max(jnp.max(rank.astype(F32), axis=0, keepdims=True), axis=1, keepdims=True)
    needed = jnp.ones((1, 1), F32)
    for turn in range(1, LEN // slots):
        needed = needed + jnp.where(most >= turn * slots, 1.0, 0.0)
    lane_row = lax.broadcasted_iota(jnp.int32, (1, LANES), 1)
    inside = jnp.where(lane < slots, lane, -LEN * LEN)
    row_value = row_col.astype(F32)
    for device in range(sent.shape[0]):
        hit = slot - device * slots == inside
        asked = jnp.max(jnp.where(hit, row_value, -1.0), axis=0, keepdims=True)
        asked = jnp.where(lane_row == slots, needed, asked)
        sent[device : device + 1, :] = asked.astype(jnp.int32)


def add_rows_kernel(over, index, rows, total, out):
    size = rows.shape[0] if over == NN else out.shape[0]
    out[...] = total[...] + mm(hot_rows(index[...], size), rows[...], over)


def add_rows(over, index, rows, total):
    return call(
        functools.partial(add_rows_kernel, over),
        jax.ShapeDtypeStruct(total.shape, F32),
        index,
        rows,
        total,
    )


def rows_grad_kernel(place, grads, chosen, asked, got, out):
    rows = out.shape[0]
    hot = hot_rows(asked[...], rows)
    out[...] = mm(grads[...], chosen[...], TN) + mm(hot, got[...], TN)


def swap(value, axis, bit, size):
    return lax.ppermute(value, axis, [(i, i ^ bit) for i in range(size)])


def gather_to_all(value, plan):
    return lax.all_to_all(
        jnp.broadcast_to(value[None], (plan.n,) + value.shape), "dp", 0, 0, tiled=False
    )


def join_heads(value, head, m):
    if m != 2:
        return lax.all_gather(value, "head", axis=0, tiled=False)
    other = swap(value, "head", 1, m)
    mine_first = head == 0
    return jnp.stack([jnp.where(mine_first, value, other), jnp.where(mine_first, other, value)])


def total_all(value, plan):
    if plan.m == 2:
        value = value + swap(value, "head", 1, 2)
    else:
        value = lax.psum(value, "head")
    return jnp.sum(gather_to_all(value, plan), axis=0)


def tail_to_plane(plan, own):
    half = plan.half_rows
    d = lax.axis_index("dp")
    part = lax.ppermute(own[:half], "dp", [(14, 12), (15, 13)])
    return jnp.where(d >= 14, own[half:], part)


def tail_along_z(part, step):
    pairs = [[(12, 4)], [(12, 8), (4, 0)]][step]
    got = lax.ppermute(part, "dp", [(a + p, b + p) for a, b in pairs for p in range(4)])
    z = lax.axis_index("dp") // 4
    return jnp.where(z == 1 if step == 0 else (z == 0) | (z == 2), got, part)


def tail_in_plane(part, n):
    return [part] + [swap(part, "dp", k, n) for k in (1, 2, 3)]


def merge_stats(value, beside, plan):
    steps = [("head", 1 << bit, plan.m) for bit in range(plan.m.bit_length() - 1)]
    steps += [("dp", 1 << bit, plan.n) for bit in range(plan.n.bit_length() - 1)]
    for index, (axis, bit, size) in enumerate(steps):
        if index == 3:
            value, beside = lax.optimization_barrier((value, beside))
        other = swap(value, axis, bit, size)
        top = jnp.maximum(value[:2], other[:2])
        total = value[2:] * jnp.exp(value[:2] - top) + other[2:] * jnp.exp(other[:2] - top)
        value = jnp.concatenate([top, total])
    return value, beside


def gather_tail(plan, value):
    whole = lax.all_gather(value, "dp", axis=0, tiled=True)
    return jnp.pad(whole[plan.tail_row :], ((0, plan.tail_pad - plan.tail_rows), (0, 0)))


def reduce_tail(plan, tail):
    n, share = plan.n, plan.rows_share
    if not plan.special:
        total = lax.psum(tail, "dp")
        front = jnp.zeros((share, LANES), F32)
        start = lax.axis_index("dp") * share - plan.tail_row + share
        start = jnp.clip(start, 0, plan.tail_pad)
        return lax.dynamic_slice_in_dim(
            jnp.concatenate([front, total[: plan.tail_rows], front]), start, share
        )
    mine = jnp.sum(tail.astype(F32), axis=0)
    whole = []
    for k in range(7):
        whole.append(lax.ppermute(mine, "dp", [(2 * k, n - 2), (2 * k + 1, n - 1)]))
    return jnp.concatenate(whole + [mine])


def attention_kernel(proj, teacher, columns, sent_row, grad_q, grad_k, loss):
    @pl.when(pl.program_id(0) == 0)
    def _():
        loss[...] = jnp.zeros_like(loss)

    allowed = columns[:, 2:3] == sent_row[...]
    weight = columns[:, 3:4].astype(F32)
    plain = columns[:, 4:5].astype(F32)

    def probs(queries, key_heads, scale):
        scores = lax.dot_general(
            queries, key_heads, (((0,), (0,)), ((), ())), preferred_element_type=F32
        )
        scores = jnp.where(allowed, scores * scale, MASKED)
        exponent = jnp.exp(scores - jnp.max(scores, axis=-1, keepdims=True))
        return exponent * (1.0 / jnp.sum(exponent, axis=-1, keepdims=True))

    teacher_prob = probs(teacher[0, 0], teacher[1, 0], THD ** (-0.5))
    queries, key_heads = proj[0, 0], proj[1, 0]
    prob = probs(queries, key_heads, HD ** (-0.5))
    gap = (prob - teacher_prob) * weight
    loss[...] += jnp.sum(gap * gap, axis=0, keepdims=True) * ATT_WEIGHT
    pulled = prob * gap
    inner = jnp.sum(pulled, axis=-1, keepdims=True)
    grad_scores = (
        (pulled - prob * inner) * (plain * (2.0 * ATT_WEIGHT))
    ).astype(BF16)
    grad_q[0] = lax.dot_general(
        key_heads, grad_scores, (((1,), (1,)), ((), ())), preferred_element_type=F32
    )
    grad_k[0] = lax.dot_general(
        queries, grad_scores, (((1,), (0,)), ((), ())), preferred_element_type=F32
    )


def map_attention(first, heads, proj, teacher, columns, sent_row):
    whole = lambda i: (0, 0)
    return pl.pallas_call(
        attention_kernel,
        out_shape=[
            jax.ShapeDtypeStruct((heads, HP, LEN), F32),
            jax.ShapeDtypeStruct((heads, HP, LEN), F32),
            jax.ShapeDtypeStruct((1, LEN), F32),
        ],
        grid=(heads,),
        in_specs=[
            pl.BlockSpec((3, 1, HP, LEN), lambda i: (0, first + i, 0, 0)),
            pl.BlockSpec((2, 1, THD, LEN), lambda i: (0, first + i, 0, 0)),
            pl.BlockSpec(columns.shape, whole),
            pl.BlockSpec((1, LEN), whole),
        ],
        out_specs=[
            pl.BlockSpec((1, HP, LEN), lambda i: (i, 0, 0)),
            pl.BlockSpec((1, HP, LEN), lambda i: (i, 0, 0)),
            pl.BlockSpec((1, LEN), whole),
        ],
        compiler_params=pltpu.CompilerParams(vmem_limit_bytes=VMEM_BYTES),
    )(proj, teacher, columns, sent_row)


def mm(left, right, over):
    return lax.dot_general(left, right, (over, ((), ())), preferred_element_type=F32)


NN, NT, TN = ((1,), (0,)), ((1,), (1,)), ((0,), (0,))


def exact(hot, value, over, parts=3):
    total = None
    for _ in range(parts):
        piece = value.astype(BF16)
        value = value - piece.astype(F32)
        term = mm(hot, piece, over)
        total = term if total is None else total + term
    return total


def head_spread(width, per_head):
    row = lax.broadcasted_iota(jnp.int32, (width, per_head * HP), 0)
    column = lax.broadcasted_iota(jnp.int32, (width, per_head * HP), 1)
    for head in range(1, per_head):
        column = column - jnp.where(row >= head * HD, HP - HD, 0)
    return jnp.where(row == column, 1.0, 0.0).astype(BF16)


def hot_rows(index, size):
    column = lax.broadcasted_iota(jnp.int32, (index.shape[0], size), 1)
    return jnp.where(index == column, 1.0, 0.0).astype(BF16)


def softmax_rows(scores, allowed):
    scores = jnp.where(allowed, scores, MASKED)
    exponent = jnp.exp(scores - jnp.max(scores, axis=-1, keepdims=True))
    return exponent * (1.0 / jnp.sum(exponent, axis=-1, keepdims=True))


def norm_pull(gradient, normed, inverse, gain_row):
    scaled = gradient * gain_row
    inner_part = (
        scaled
        - jnp.mean(scaled, -1, keepdims=True)
        - normed * jnp.mean(scaled * normed, -1, keepdims=True)
    )
    return (
        inner_part * inverse,
        jnp.sum(gradient * normed, 0, keepdims=True),
        jnp.sum(gradient, 0, keepdims=True),
    )


ROOT_HALF = 0.5**0.5
BELL = (2.0 * 3.141592653589793) ** -0.5


def forward_kernel(
    back,
    more_words,
    slot_col,
    columns,
    pick_columns,
    sent_row,
    attn_in,
    attn_out,
    ffn_in,
    ffn_out,
    shared_half,
    qv_bias,
    up_bias,
    chosen,
    normed_zero,
    inverse_zero,
    proj,
    prob,
    mixed,
    normed_one,
    inverse_one,
    state_low,
    pre_act,
    hidden_act,
    normed_two,
    inverse_two,
    shared,
):
    m, _, _, width = attn_in.shape
    per_head = width // HD
    for part in range(m):
        shared[:, part * width : (part + 1) * width] = shared_half[part].astype(F32)
    position_hot = hot_rows(columns[:, 0:1], LEN)
    state = mm(hot_rows(slot_col[...], back.shape[0]), back[...], NN) + more_words[...]
    state = state + mm(position_hot, shared[0:LEN, :].astype(BF16), NN)
    state = state + jnp.where(columns[:, 1:2] == 0, shared[LEN : LEN + 1, :], shared[LEN + 1 : LEN + 2, :])
    state, (normed, inverse) = norm_forward(
        state, shared[LEN + 2 : LEN + 3, :], shared[LEN + 3 : LEN + 4, :]
    )
    normed_zero[...] = normed
    inverse_zero[...] = inverse
    gathered = state.astype(BF16)
    base = LEN + 4
    row = lambda index: shared[base + index : base + index + 1, :]

    spread = head_spread(width, per_head)
    for part in range(m):
        for kind in range(3):
            wide = mm(attn_in[part, kind], spread, NN).astype(BF16)
            value = mm(wide, gathered, ((0,), (1,)))
            if kind != 1:
                bias_row = qv_bias[part, kind // 2 : kind // 2 + 1, :]
                bias = mm(spread, jnp.broadcast_to(bias_row, (8, width)), ((0,), (1,)))
                value = value + bias[:, 0:1]
            value = value.astype(BF16).reshape(per_head, HP, LEN)
            proj[kind, part * per_head : (part + 1) * per_head] = value

    pick_hot = hot_rows(pick_columns[:, 0:1], LEN)
    allowed = pick_columns[:, 1:2] == sent_row[...]
    masks = pick_columns.shape[0]
    branch = jnp.zeros((masks, D), F32)
    for part in range(m):
        wide_out = mm(spread, attn_out[part], TN).astype(BF16)
        for index in range(per_head):
            head = part * per_head + index
            query = mm(pick_hot, proj[0, head], NT).astype(BF16)
            value = softmax_rows(mm(query, proj[1, head], NN) * HD ** (-0.5), allowed)
            prob[head] = value
            mix = mm(value.astype(BF16), proj[2, head], NT).astype(BF16)
            mixed[part, :, index * HP : (index + 1) * HP] = mix
            branch = branch + mm(mix, wide_out[index * HP : (index + 1) * HP, :], NN)
    state_one, (normed, inverse) = norm_forward(
        exact(pick_hot, state, NN) + branch + row(4), row(0), row(1)
    )
    normed_one[...] = normed
    inverse_one[...] = inverse
    low = state_one.astype(BF16)
    state_low[...] = low
    branch = jnp.zeros((masks, D), F32)
    for part in range(m):
        pre = mm(low, ffn_in[part], NN) + up_bias[part].astype(F32)
        pre_act[part] = pre
        act = (0.5 * pre * (1.0 + lax.erf(pre * ROOT_HALF))).astype(BF16)
        hidden_act[part] = act
        branch = branch + mm(act, ffn_out[part], NN)
    state_two, (normed, inverse) = norm_forward(state_one + branch + row(5), row(2), row(3))
    normed_two[...] = normed
    inverse_two[...] = inverse
    chosen[...] = state_two.astype(BF16)


def backward_kernel(
    last_sentence,
    grad_pick,
    slot_col,
    columns,
    pick_columns,
    pos_row,
    sent_row,
    attn_in,
    attn_out,
    ffn_in,
    ffn_out,
    shared_half,
    normed_zero,
    inverse_zero,
    proj,
    prob,
    mixed,
    normed_one,
    inverse_one,
    state_low,
    pre_act,
    hidden_act,
    normed_two,
    inverse_two,
    teacher,
    map_q_low,
    map_k_low,
    map_q_high,
    map_k_high,
    grad_attn_in,
    grad_attn_out,
    grad_ffn_in,
    grad_ffn_out,
    grad_shared,
    grad_qv,
    grad_up,
    word_grads,
    slot_grads,
    shared,
    grad_proj,
    wide_out,
):
    m, _, _, width = attn_in.shape
    per_head = width // HD
    pos = pick_columns[:, 0:1]
    pick_sentence = pick_columns[:, 1:2]
    masks = pos.shape[0]
    for part in range(m):
        shared[:, part * width : (part + 1) * width] = shared_half[part, LEN:, :].astype(F32)
    row = lambda index: shared[index : index + 1, :]
    spread = head_spread(width, per_head)
    score_scale = HD ** (-0.5)

    repeats = pos == pos_row[...]
    order = lax.broadcasted_iota(jnp.int32, (masks, masks), 1)
    lead = jnp.min(jnp.where(repeats, order, masks).astype(F32), axis=1, keepdims=True)
    leads = lead == lax.broadcasted_iota(jnp.int32, (masks, 1), 0).astype(F32)
    gradient = exact(jnp.where(repeats, 1.0, 0.0).astype(BF16), grad_pick[...], NN)
    gradient = jnp.where(leads, gradient, 0.0)

    grad_res, gain_two, bias_two = norm_pull(
        gradient, normed_two[...], inverse_two[...], row(6)
    )
    grad_branch = grad_res.astype(BF16)
    grad_one = grad_res
    for part in range(m):
        pre = pre_act[part]
        grad_hidden = mm(grad_branch, ffn_out[part], NT)
        slope = 0.5 * (1.0 + lax.erf(pre * ROOT_HALF)) + pre * jnp.exp(-0.5 * pre * pre) * BELL
        grad_pre = (grad_hidden * slope).astype(BF16)
        grad_ffn_out[part] = mm(hidden_act[part], grad_branch, TN)
        grad_ffn_in[part] = mm(state_low[...], grad_pre, TN)
        grad_up[part] = jnp.sum(grad_pre.astype(F32), 0, keepdims=True)
        grad_one = grad_one + mm(grad_pre, ffn_in[part], NT)
    grad_mid, gain_one, bias_one = norm_pull(grad_one, normed_one[...], inverse_one[...], row(4))
    grad_attended = grad_mid.astype(BF16)

    pick_hot = hot_rows(pos, LEN)
    allowed = pick_sentence == sent_row[...]
    weight = jnp.where(pick_sentence < last_sentence[0], 2.0 * ATT_WEIGHT, 0.0)
    for part in range(m):
        narrow = mm(mixed[part], spread, NT).astype(BF16)
        grad_attn_out[part] = mm(narrow, grad_attended, TN)
        wide_out[part] = mm(spread, attn_out[part], TN).astype(BF16)
        for index in range(per_head):
            head = part * per_head + index
            at = slice(head * HP, (head + 1) * HP)
            map_q, map_k = (map_q_low, map_k_low) if head < HEADS // 2 else (map_q_high, map_k_high)
            grad_mixed = mm(
                grad_attended, wide_out[part, index * HP : (index + 1) * HP, :], NT
            ).astype(BF16)
            value = prob[head]
            teacher_query = mm(pick_hot, teacher[0, head], NT).astype(BF16)
            teacher_prob = softmax_rows(
                mm(teacher_query, teacher[1, head], NN) * THD ** (-0.5), allowed
            )
            grad_prob = mm(grad_mixed, proj[2, head], NN) + (value - teacher_prob) * weight
            grad_proj[2, at, :] = mm(grad_mixed, value.astype(BF16), TN).astype(BF16)
            grad_scores = value * (
                grad_prob - jnp.sum(value * grad_prob, axis=-1, keepdims=True)
            )
            grad_scores = jnp.where(leads, grad_scores, 0.0).astype(BF16)
            grad_query = (mm(grad_scores, proj[1, head], NT) * score_scale).astype(BF16)
            grad_proj[0, at, :] = (
                map_q[head % (HEADS // 2)] * score_scale + mm(grad_query, pick_hot, TN)
            ).astype(BF16)
            query = mm(pick_hot, proj[0, head], NT).astype(BF16)
            grad_proj[1, at, :] = (
                (map_k[head % (HEADS // 2)] + mm(query, grad_scores, TN)) * score_scale
            ).astype(BF16)

    normed = normed_zero[...]
    gathered = (normed * row(2) + row(3)).astype(BF16)
    grad_in = exact(pick_hot, grad_mid, TN)
    ones = jnp.ones((8, LEN), BF16)
    for part in range(m):
        for kind in range(3):
            first = part * per_head * HP
            narrow = mm(spread, grad_proj[kind, first : first + per_head * HP, :], NN).astype(BF16)
            grad_attn_in[part, kind] = mm(gathered, narrow, ((0,), (1,)))
            grad_in = grad_in + mm(narrow, attn_in[part, kind], ((0,), (1,)))
            if kind != 1:
                sums = mm(ones, narrow, NT)
                grad_qv[part, kind // 2 : kind // 2 + 1, :] = sums[0:1, :]
    grad_embed, gain_zero, bias_zero = norm_pull(grad_in, normed, inverse_zero[...], row(2))
    low = grad_embed.astype(BF16)
    word_grads[...] = low
    slot_grads[...] = mm(hot_rows(slot_col[...], slot_grads.shape[0]), low, TN).astype(BF16)
    positions = exact(hot_rows(columns[:, 0:1], LEN), grad_embed, TN, 2)
    ones_type = columns[:, 1:2] == 1
    rows = [
        jnp.sum(jnp.where(ones_type, 0.0, grad_embed), axis=0, keepdims=True),
        jnp.sum(jnp.where(ones_type, grad_embed, 0.0), axis=0, keepdims=True),
        gain_zero,
        bias_zero,
        gain_one,
        bias_one,
        gain_two,
        bias_two,
        jnp.sum(grad_mid, axis=0, keepdims=True),
        jnp.sum(grad_res, axis=0, keepdims=True),
    ]
    for part in range(m):
        at = slice(part * width, (part + 1) * width)
        grad_shared[part, 0:LEN, :] = positions[:, at]
        for index, value in enumerate(rows):
            grad_shared[part, LEN + index : LEN + index + 1, :] = value[:, at]


def logits_kernel(block, places, chosen, words, out):
    logits = mm(chosen[...], words[...], NT) * (1.0 / SOFTEN_FACTOR)
    column = lax.broadcasted_iota(jnp.int32, logits.shape, 1)
    own = column < places[1]
    logits = jnp.where(own, logits, -1e30)
    top = jnp.max(logits, axis=-1, keepdims=True)
    total = jnp.sum(jnp.where(own, jnp.exp(logits - top), 0.0), axis=-1, keepdims=True)
    lane = lax.broadcasted_iota(jnp.int32, (block, LANES), 1)
    both = jnp.where(lane == 0, top, jnp.where(lane == 1, total, 0.0))
    out[...] = jnp.transpose(both)[0:8, :]


def logits_stats(plan, place, chosen, words):
    picks = chosen.shape[0]
    block = 256
    return pl.pallas_call(
        functools.partial(logits_kernel, block),
        out_shape=jax.ShapeDtypeStruct((8, picks), F32),
        grid=(picks // block,),
        in_specs=[
            pl.BlockSpec(memory_space=pltpu.SMEM),
            pl.BlockSpec((block, chosen.shape[1]), lambda i: (i, 0)),
            pl.BlockSpec(words.shape, lambda i: (0, 0)),
        ],
        out_specs=pl.BlockSpec((8, block), lambda i: (0, i)),
        compiler_params=pltpu.CompilerParams(vmem_limit_bytes=VMEM_BYTES),
    )(place, chosen, words)


def grad_logits_kernel(block, places, chosen, words, *refs):
    parts_in, (stats, grads, pulled, losses, mentor) = refs[:-5], refs[-5:]
    first = 0
    size = sum(part.shape[1] for part in parts_in)
    for part in parts_in:
        for source in range(part.shape[0]):
            begin = source * size + first
            mentor[begin : begin + part.shape[1], :] = part[source]
        first += part.shape[1]
    step = pl.program_id(0)
    log_total = stats[0:1, :] + jnp.log(stats[2:3, :])
    log_mentor = stats[1:2, :] + jnp.log(stats[3:4, :])
    line = lax.broadcasted_iota(jnp.int32, (LANES, block), 0)
    both = jnp.transpose(jnp.where(line == 0, log_total, log_mentor))
    column_total, mentor_total = both[:, 0:1], both[:, 1:2]
    logits = mm(chosen[...], words[...], NT) * (1.0 / SOFTEN_FACTOR)
    column = lax.broadcasted_iota(jnp.int32, logits.shape, 1)
    own = column < places[1]
    target = jnp.exp(mentor[...].astype(F32) * (1.0 / SOFTEN_FACTOR) - mentor_total)
    target = jnp.where(own, target, 0.0)
    student = jnp.where(own, jnp.exp(jnp.where(own, logits, -1e30) - column_total), 0.0)
    value = ((student - target) * (1.0 / SOFTEN_FACTOR)).astype(BF16)
    grads[...] = value
    pulled[...] = mm(value, words[...], NN)

    @pl.when(step == 0)
    def _():
        losses[...] = jnp.zeros_like(losses)

    cross = jnp.sum(jnp.sum(target * logits, axis=0, keepdims=True), axis=1, keepdims=True)
    own_share = jnp.sum(log_total, axis=1, keepdims=True)
    row = lax.broadcasted_iota(jnp.int32, (8, LANES), 0)
    losses[...] += jnp.where(row == 0, cross, jnp.where(row == 1, own_share, 0.0))


def grad_logits_call(plan, place, chosen, words, mentor, stats):
    picks = chosen.shape[0]
    sources = 8
    block = picks // plan.n * sources
    rows = words.shape[0]
    return pl.pallas_call(
        functools.partial(grad_logits_kernel, block),
        out_shape=[
            jax.ShapeDtypeStruct((picks, rows), BF16),
            jax.ShapeDtypeStruct((picks, D), F32),
            jax.ShapeDtypeStruct((8, LANES), F32),
        ],
        grid=(picks // block,),
        in_specs=[
            pl.BlockSpec(memory_space=pltpu.SMEM),
            pl.BlockSpec((block, chosen.shape[1]), lambda i: (i, 0)),
            pl.BlockSpec(words.shape, lambda i: (0, 0)),
        ]
        + [pl.BlockSpec((sources,) + part.shape[1:], lambda i: (i, 0, 0)) for part in mentor]
        + [pl.BlockSpec((4, block), lambda i: (0, i))],
        out_specs=[
            pl.BlockSpec((block, rows), lambda i: (i, 0)),
            pl.BlockSpec((block, D), lambda i: (i, 0)),
            pl.BlockSpec((8, LANES), lambda i: (0, 0)),
        ],
        scratch_shapes=[pltpu.VMEM((block, rows), BF16)],
        compiler_params=pltpu.CompilerParams(vmem_limit_bytes=VMEM_BYTES),
    )(place, chosen, words, *mentor, stats)


def dot(spec, left, right, **options):
    return jnp.einsum(spec, left, right, preferred_element_type=F32, **options)


def one_hot(index, size):
    return (index[:, None] == jnp.arange(size, dtype=jnp.int32)[None, :]).astype(BF16)


def norm_forward(value, gain_row, bias_row):
    centred = value - jnp.mean(value, axis=-1, keepdims=True)
    inverse = lax.rsqrt(jnp.mean(centred * centred, axis=-1, keepdims=True) + NORM_EPS)
    normed = centred * inverse
    return (normed * gain_row + bias_row, (normed, inverse))


def local(
    master,
    first_moment,
    second_moment,
    token_ids,
    token_types,
    counts,
    mask_pos,
    teacher_states,
    teacher_qk,
    mentor_logits,
):
    n, m = lax.axis_size("dp"), lax.axis_size("head")
    d, h = lax.axis_index("dp"), lax.axis_index("head")
    share_len = master.shape[1]
    assert share_len % LANES == 0 and token_ids.shape[0] == m == 2
    plan = Plan(n, m, share_len)
    share = plan.rows_share
    devices = n * m
    slots = max(8, 1024 // devices)
    masks = mask_pos.shape[1]
    picks = devices * masks

    own_row = lambda value: lax.dynamic_index_in_dim(value, h, 0, keepdims=False)
    ids, types, sizes, pos = (own_row(v) for v in (token_ids, token_types, counts, mask_pos))

    order = jnp.arange(LEN, dtype=jnp.int32)

    def token_slots(turn):
        return call(
            functools.partial(slots_kernel, plan, slots),
            [
                jax.ShapeDtypeStruct((devices, LANES), jnp.int32),
                jax.ShapeDtypeStruct((LEN, 1), jnp.int32),
            ],
            jnp.reshape(turn, (1,)).astype(jnp.int32),
            jnp.broadcast_to(ids[None], (8, LEN)),
            smem=1,
        )

    sent_first, slot_col = token_slots(jnp.int32(0))

    def ask(sent):
        got = lax.all_to_all(sent, BOTH, 0, 0, tiled=True)
        asked = got[:, :slots].reshape(-1)
        return asked, got[:, slots]

    first_row = jnp.minimum((d * share_len + D - 1) // D, plan.vocab)
    row_count = jnp.minimum(((d + 1) * share_len + D - 1) // D, plan.vocab) - first_row

    chunk = master.reshape(share, 1, LANES)
    after = lax.ppermute(
        master[0, : 8 * LANES].reshape(8, LANES), "dp", [(i + 1, i) for i in range(n - 1)]
    )
    shift = jnp.where(row_count > 0, first_row * D - d * share_len, 0)
    place = jnp.stack([shift, row_count, d, h]).astype(jnp.int32)
    if plan.special:
        tail_part = share_rows(plan, place, chunk)
    else:
        tail_part = chunk.reshape(share, LANES).astype(BF16)

    words_own = table_rows(plan, place, chunk, after)

    own_index = lambda asked: jnp.where(asked >= 0, asked - first_row, -1)

    def fetch(asked):
        rows = dot(
            "sv,vd->sd", one_hot(own_index(asked), plan.rows), words_own
        ).astype(BF16)
        return lax.all_to_all(
            rows.reshape(devices, slots, D), BOTH, 0, 0, tiled=True
        ).reshape(-1, D)

    asked_first, needs = ask(sent_first)
    if plan.special:
        tail_part = tail_along_z(tail_to_plane(plan, tail_part), 0)
        asked_first, tail_part, words_own = lax.optimization_barrier(
            (asked_first, tail_part, words_own)
        )

    rounds = jnp.max(needs)
    back = fetch(asked_first)

    room = plan.rows

    send_mentor = lambda block: lax.all_to_all(block, "dp", 0, 0, tiled=False)
    cut = 32
    block_first, block_second, mentor_stats = call(
        functools.partial(mentor_kernel, plan, room, (0, cut)),
        [
            jax.ShapeDtypeStruct((n, cut, room), BF16),
            jax.ShapeDtypeStruct((n, m * masks - cut, room), BF16),
            jax.ShapeDtypeStruct((8, LANES), F32),
        ],
        mentor_logits,
    )

    teacher_weight = join_heads(teacher_qk, h, m)
    states = own_row(teacher_states)
    teacher_proj = dot("hdce,ld->chel", teacher_weight, states).astype(BF16)
    teacher_proj = teacher_proj.reshape(2, HEADS, THD, LEN)

    if plan.special:
        tail_part = tail_along_z(tail_part, 1)

    def more_words(state):
        sent, slot = token_slots(state[0])
        return state[0] + 1, add_rows(NN, slot, fetch(ask(sent)[0]), state[1])

    more_words = lax.while_loop(
        lambda state: state[0] < rounds, more_words, (jnp.int32(1), jnp.zeros((LEN, D), F32))
    )[1]
    tail_own = tail_in_plane(tail_part, n) if plan.special else [gather_tail(plan, tail_part)]


    back, tail_own, block_first, teacher_proj = lax.optimization_barrier(
        (back, tail_own, block_first, teacher_proj)
    )
    mentor_first = send_mentor(block_first)
    tail_other = [swap(part, "head", 1, 2) if m == 2 else part for part in tail_own]
    weights = unpack_tail(plan, place, tail_own, tail_other)

    ends = jnp.cumsum(sizes)
    passed = (order[:, None] >= ends[None, :]).astype(jnp.int32)
    sentence = jnp.sum(passed, axis=-1)
    within = order - jnp.sum(passed * sizes[None, :], axis=-1)
    valid = (sentence < sizes.shape[0] - 1).astype(jnp.int32)

    pick_sentence = jnp.sum(jnp.where(pos[:, None] == order[None, :], sentence[None, :], 0), 1)
    picked_any = jnp.sum((pos[:, None] == order[None, :]).astype(jnp.int32), axis=0) > 0
    columns = [within, types, sentence, valid, 1 - picked_any.astype(jnp.int32)]
    columns = jnp.stack(columns + [order] * 3, axis=1)
    pick_columns = jnp.stack([pos, pick_sentence], axis=1)
    attn_in, attn_out, ffn_in, ffn_out, shared_half, qv_bias, up_bias = weights
    shape = jax.ShapeDtypeStruct
    chosen_own, *saved = call(
        forward_kernel,
        [
            shape((masks, D), BF16),
            shape((LEN, D), F32),
            shape((LEN, 1), F32),
            shape((3, HEADS, HP, LEN), BF16),
            shape((HEADS, masks, LEN), F32),
            shape((m, masks, plan.width // HD * HP), BF16),
            shape((masks, D), F32),
            shape((masks, 1), F32),
            shape((masks, D), BF16),
            shape((m, masks, plan.units), F32),
            shape((m, masks, plan.units), BF16),
            shape((masks, D), F32),
            shape((masks, 1), F32),
        ],
        back,
        more_words,
        slot_col,
        columns,
        pick_columns,
        sentence[None],
        *weights,
        scratch=[pltpu.VMEM((SROWS, D), F32)],
    )
    proj = saved[2]

    chosen_own, mentor_first = lax.optimization_barrier((chosen_own, mentor_first))
    chosen = gather_to_all(chosen_own, plan)
    halves = [
        map_attention(first, HEADS // 2, proj, teacher_proj, columns, sentence[None])
        for first in (0, HEADS // 2)
    ]
    chosen = join_heads(chosen, h, m)
    chosen = jnp.swapaxes(chosen, 0, 1).reshape(picks, D)
    chosen, block_second = lax.optimization_barrier((chosen, block_second))
    mentor_second = send_mentor(block_second)
    student = logits_stats(plan, place, chosen, words_own)
    nothing = jnp.concatenate([jnp.full((1, picks), -1e30, F32), jnp.zeros((1, picks), F32)])
    at = (0, d * m * masks)
    mentor_all = lax.dynamic_update_slice(nothing, mentor_stats[:2, : m * masks], at)
    stats = jnp.concatenate([student[:1], mentor_all[:1], student[1:2], mentor_all[1:]])
    stats, halves[0] = merge_stats(stats, halves[0], plan)
    mentor_here = [mentor_first, mentor_second]
    grad_logits, grad_chosen, losses = grad_logits_call(
        plan, place, chosen, words_own, mentor_here, stats
    )
    map_rows = halves[0][2] + halves[1][2]
    loss_local = jnp.sum(map_rows) + losses[1, 0] / devices - losses[0, 0]
    grad_chosen = grad_chosen.reshape(n, m, masks, D)
    if m == 2:
        mine = lax.dynamic_index_in_dim(grad_chosen, h, 1, keepdims=False)
        other = lax.dynamic_index_in_dim(grad_chosen, 1 - h, 1, keepdims=False)
        mine = mine + swap(other.astype(BF16), "head", 1, 2).astype(F32)
    else:
        mine = lax.psum_scatter(grad_chosen, "head", scatter_dimension=1, tiled=False)
    grad_pick = jnp.sum(
        lax.all_to_all(mine.astype(BF16), "dp", 0, 0, tiled=False).astype(F32), axis=0
    )

    *piece_grads, word_grads, slot_grads = call(
        backward_kernel,
        [
            shape((m, 3, D, plan.width), F32),
            shape((m, plan.width, D), F32),
            shape((m, D, plan.units), F32),
            shape((m, plan.units, D), F32),
            shape((m, SROWS, plan.width), F32),
            shape((m, 2, plan.width), F32),
            shape((m, 1, plan.units), F32),
            shape((LEN, D), BF16),
            shape((devices * slots, D), BF16),
        ],
        jnp.array([sizes.shape[0] - 1], jnp.int32),
        grad_pick,
        slot_col,
        columns,
        pick_columns,
        pos[None],
        sentence[None],
        attn_in,
        attn_out,
        ffn_in,
        ffn_out,
        shared_half,
        *saved,
        teacher_proj,
        *halves[0][:2],
        *halves[1][:2],
        scratch=[
            pltpu.VMEM((SROWS - LEN, D), F32),
            pltpu.VMEM((3, HEADS * HP, LEN), BF16),
            pltpu.VMEM((m, plan.width // HD * HP, D), BF16),
        ],
        smem=1,
    )

    def give(slot_grads):
        return lax.all_to_all(
            slot_grads.reshape(devices, slots, D), BOTH, 0, 0, tiled=True
        ).reshape(-1, D)

    def more_grads(state):
        sent, slot = token_slots(state[0])
        asked = own_index(ask(sent)[0])[:, None]
        hot = one_hot(slot[:, 0], devices * slots)
        got = give(dot("ts,td->sd", hot, word_grads).astype(BF16))
        return state[0] + 1, add_rows(TN, asked, got, state[1])

    given = give(slot_grads)
    tail_sent = pack_tail(plan, 1 - h, piece_grads)
    tail = pack_tail(plan, h, piece_grads, swap(tail_sent, "head", 1, 2))
    tail, given = lax.optimization_barrier((tail, given))
    if plan.special:
        tail = lax.all_to_all(tail, "dp", 0, 0, tiled=False)

    grad_table = call(
        rows_grad_kernel,
        jax.ShapeDtypeStruct((plan.rows, D), F32),
        place,
        grad_logits,
        chosen,
        own_index(asked_first)[:, None],
        given,
        smem=1,
    )
    grad_table = lax.while_loop(
        lambda state: state[0] < rounds, more_grads, (jnp.int32(1), grad_table)
    )[1]
    table_lines = table_pack(plan, place, grad_table)
    before = lax.ppermute(table_lines[share:], "dp", [(i, i + 1) for i in range(n - 1)])

    tail, table_lines, loss_local = lax.optimization_barrier((tail, table_lines, loss_local))
    gradient, numbers = merge(
        plan, place, loss_local.reshape(1), table_lines, before, reduce_tail(plan, tail)
    )

    numbers = total_all(numbers, plan)
    loss_sum, grad_norm = numbers[1, 0], jnp.sqrt(numbers[0, 0])
    scale = CLIP_NORM / jnp.maximum(grad_norm, CLIP_NORM)
    vector_start = plan.table + plan.width * D * 4 + 2 * D * plan.units + (LEN + 2) * plan.width
    whole = jax.ShapeDtypeStruct((1, share_len), F32)
    updated = call(
        functools.partial(adam_kernel, plan, vector_start),
        [whole, whole, whole, jax.ShapeDtypeStruct((1, share_len), BF16)],
        place,
        scale.reshape(1),
        master,
        gradient.reshape(1, share_len),
        first_moment,
        second_moment,
        smem=2,
    )
    return (loss_sum, grad_norm, *updated)


def solution(mesh):
    return jax.shard_map(
        local,
        mesh=mesh,
        in_specs=(
            P("head", "dp"),
            P("head", "dp"),
            P("head", "dp"),
            P("dp", None),
            P("dp", None),
            P("dp", None),
            P("dp", None),
            P("dp", None, None),
            P(None, None, "head"),
            P("dp", None, "head"),
        ),
        out_specs=(P(), P(), P("head", "dp"), P("head", "dp"), P("head", "dp"), P("head", "dp")),
        check_vma=False,
    )
```

```python
import functools

import jax
import jax.numpy as jnp
from jax import lax
from jax.experimental import pallas as pl
from jax.experimental.pallas import tpu as pltpu
from jax.sharding import PartitionSpec as P

D = 312
HEADS = 12
HD = 26
HP = 32
FF = 1200
VOCAB = 30522
THD = 64
LEN = 512
STEP = 10
SROWS = 522

ATT_WEIGHT = 1.0
SOFTEN_FACTOR = 2.0
CLIP_NORM = 1.0
BETA_ONE = 0.9
BETA_TWO = 0.999
RATE_MATRIX = 0.06
RATE_VECTOR = 0.6
WEIGHT_DECAY = 0.01
ADAM_EPS = 1e-08
NORM_EPS = 1e-12
MASKED = -1000000000.0

F32 = jnp.float32
BF16 = jnp.bfloat16
LANES = 128
BOTH = ("dp", "head")
VMEM_BYTES = 56 * 1024 * 1024


def ceil_to(value, unit):
    return -(-value // unit) * unit


def call(kernel, out_shape, *args, scratch=(), smem=0, hbm=(), hbm_out=(), smem_out=()):
    space = lambda index: pltpu.SMEM if index < smem else pl.ANY if index in hbm else pltpu.VMEM
    in_specs = [pl.BlockSpec(memory_space=space(index)) for index in range(len(args))]
    outs = out_shape if isinstance(out_shape, list) else [out_shape]
    out_specs = [
        pl.BlockSpec(
            memory_space=pl.ANY
            if index in hbm_out
            else pltpu.SMEM
            if index in smem_out
            else pltpu.VMEM
        )
        for index in range(len(outs))
    ]
    out_specs = out_specs if isinstance(out_shape, list) else out_specs[0]
    return pl.pallas_call(
        kernel,
        out_shape=out_shape,
        in_specs=in_specs,
        out_specs=out_specs,
        scratch_shapes=list(scratch),
        compiler_params=pltpu.CompilerParams(vmem_limit_bytes=VMEM_BYTES),
    )(*args)


class Plan:
    def __init__(self, n, m, share):
        self.n, self.m, self.share = n, m, share
        self.rows_share = share // LANES
        self.vocab = VOCAB // m
        self.width = D // m
        self.units = FF // m
        self.first = [min(-(-d * share // D), self.vocab) for d in range(n + 1)]
        widest = -(-share // D)
        self.rows = ceil_to(widest + 3, 16)
        table = self.vocab * D
        self.table = table
        self.tail_row = table // LANES
        self.tail_off = table % LANES
        self.tail_rows = n * self.rows_share - self.tail_row
        self.tail_pad = ceil_to(self.tail_rows + 40, 16)
        w, u = self.width, self.units
        self.pieces = []
        base = self.tail_off
        for rows, wide in ((3 * D, w), (w, D), (D, u), (u, D), (SROWS, w), (2, w), (1, u)):
            self.pieces.append((base, wide, rows))
            base += rows * wide
        self.special = n == 16 and self.tail_row // self.rows_share == n - 2
        if self.special:
            self.low_rows = (n - 1) * self.rows_share - self.tail_row
            self.slice_rows = ceil_to(-(-self.rows_share // 8), 16)
            self.half_rows = 4 * self.slice_rows


def period(width):
    step = 16
    while step * width % LANES:
        step *= 2
    return step, step * width // LANES


def rows_at(start, count, stride):
    return pl.ds(start, count) if count == 1 else pl.ds(start, count, stride=stride)


def spread_rows(src, dst, base, width, rows):
    step, lane_rows = period(width)
    tiles = -(-width // LANES)
    for phase in range(min(step, rows)):
        count = len(range(phase, rows, step))
        line, off = divmod(base + phase * width, LANES)
        loaded = [
            src[rows_at(line + j, count, lane_rows), :] for j in range(tiles + (1 if off else 0))
        ]
        lane = lax.broadcasted_iota(jnp.int32, (count, LANES), 1)
        for tile in range(tiles):
            value = loaded[tile]
            if off:
                value = jnp.where(
                    lane < LANES - off,
                    pltpu.roll(value, LANES - off, 1),
                    pltpu.roll(loaded[tile + 1], LANES - off, 1),
                )
            dst[tile, rows_at(phase, count, step), :] = value


def pack_rows(src, dst, base, width, rows):
    step, lane_rows = period(width)
    tiles = -(-width // LANES)
    for phase in range(min(step, rows)):
        count = len(range(phase, rows, step))
        line, off = divmod(base + phase * width, LANES)
        loaded = [
            src[tile, rows_at(phase, count, step), :] for tile in range(tiles)
        ]
        lane = lax.broadcasted_iota(jnp.int32, (count, LANES), 1)
        rolled = [pltpu.roll(value, off, 1) if off else value for value in loaded]
        for j in range(-(-(off + width) // LANES)):
            value = jnp.zeros((count, LANES), F32)
            if j < tiles:
                value = jnp.where(lane >= off, rolled[j], value)
            if off and j > 0:
                value = jnp.where(lane < off, rolled[j - 1], value)
            at = rows_at(line + j, count, lane_rows)
            dst[at, :] = dst[at, :] + value


def column_tiles(width):
    return [(t, t * LANES, min(LANES, width - t * LANES)) for t in range(-(-width // LANES))]


def shift_lines(source, count, start, max_line):
    low, high = start // LANES, lax.rem(start, LANES)
    first = source[0:count, :]
    second = source[1 : count + 1, :]
    for line in range(1, max_line + 1):
        first = jnp.where(low == line, source[line : count + line, :], first)
        second = jnp.where(low == line, source[line + 1 : count + line + 1, :], second)
    lane = lax.broadcasted_iota(jnp.int32, (count, LANES), 1)
    back = lax.rem(LANES - high, LANES)
    return jnp.where(lane < LANES - high, pltpu.roll(first, back, 1), pltpu.roll(second, back, 1))


def bring(source, target, sem):
    copy = pltpu.make_async_copy(source, target, sem)
    copy.start()
    copy.wait()


def share_rows_kernel(plan, place, chunk, out, lines, sem):
    share, low = plan.rows_share, plan.low_rows
    lines[share & -8 :, :] = jnp.zeros((lines.shape[0] - (share & -8), LANES), F32)
    bring(chunk.at[:, 0, :], lines.at[0:share], sem)
    count = out.shape[0]
    begins_late = place[2] == plan.n - 2
    first = share - low
    out[...] = jnp.where(
        begins_late, lines[first : first + count, :], lines[0:count, :]
    ).astype(BF16)


def share_rows(plan, place, chunk):
    count = 8 * plan.slice_rows
    return call(
        functools.partial(share_rows_kernel, plan),
        jax.ShapeDtypeStruct((count, LANES), BF16),
        place,
        chunk,
        scratch=[
            pltpu.VMEM((ceil_to(count + plan.rows_share - plan.low_rows, 8), LANES), F32),
            pltpu.SemaphoreType.DMA,
        ],
        smem=1,
        hbm=(1,),
    )


def table_rows_kernel(plan, place, chunk, after, out, joined, shifted, rows, sem):
    share = plan.rows_share
    lines = joined.shape[0]
    joined[share & -8 :, :] = jnp.zeros((lines - (share & -8), LANES), F32)
    bring(chunk.at[:, 0, :], joined.at[0:share], sem)
    joined[share : share + 8, :] = after[...]
    shifted[...] = jnp.zeros_like(shifted)
    shifted[0 : share + 2, :] = shift_lines(joined, share + 2, place[0], 2)
    spread_rows(shifted, rows, 0, D, plan.rows)
    row = lax.broadcasted_iota(jnp.int32, (plan.rows, LANES), 0)
    for tile, left, wide in column_tiles(D):
        value = jnp.where(row < place[1], rows[tile], 0.0).astype(BF16)
        out[:, left : left + wide] = value[:, 0:wide]


def table_rows(plan, place, chunk, after):
    lines = ceil_to(max(plan.rows_share + 16, plan.rows // 16 * 39 + 2), 8)
    return call(
        functools.partial(table_rows_kernel, plan),
        jax.ShapeDtypeStruct((plan.rows, D), BF16),
        place,
        chunk,
        after,
        scratch=[
            pltpu.VMEM((lines, LANES), F32),
            pltpu.VMEM((lines, LANES), F32),
            pltpu.VMEM((3, plan.rows, LANES), F32),
            pltpu.SemaphoreType.DMA,
        ],
        smem=1,
        hbm=(1,),
    )


def table_pack_kernel(plan, place, grads, out, rows, lines):
    rows[...] = jnp.zeros_like(rows)
    for tile, left, wide in column_tiles(D):
        rows[tile, 16 : 16 + plan.rows, 0:wide] = grads[:, left : left + wide]
    lines[...] = jnp.zeros_like(lines)
    pack_rows(rows, lines, 0, D, plan.rows + 16)
    count = plan.rows_share + 8
    start = 39 * LANES - place[0]
    low, high = start // LANES - 36, lax.rem(start, LANES)
    first = lines[36 : 36 + count, :]
    second = lines[37 : 37 + count, :]
    for line in range(1, 4):
        first = jnp.where(low == line, lines[36 + line : 36 + line + count, :], first)
        second = jnp.where(low == line, lines[37 + line : 37 + line + count, :], second)
    lane = lax.broadcasted_iota(jnp.int32, (count, LANES), 1)
    back = lax.rem(LANES - high, LANES)
    value = jnp.where(
        lane < LANES - high, pltpu.roll(first, back, 1), pltpu.roll(second, back, 1)
    )
    line = lax.broadcasted_iota(jnp.int32, (count, LANES), 0)
    index = (line + place[2] * plan.rows_share) * LANES + lane
    out[...] = jnp.where(index < plan.table, value, 0.0)


def merge_kernel(plan, place, loss, table, before, *refs):
    extra, (out, numbers, whole, sem) = refs[:-4], refs[-4:]
    share = plan.rows_share
    whole[...] = table[0:share, :]
    whole[0:8, :] = whole[0:8, :] + before[...]
    if plan.special:
        d, low = place[2], plan.low_rows
        for owner, first, count in ((plan.n - 2, share - low, low), (plan.n - 1, 0, share)):

            @pl.when(d == owner)
            def _(first=first, count=count):
                whole[first : first + count, :] = (
                    whole[first : first + count, :] + extra[0][0:count, :]
                )
    else:
        whole[...] = whole[...] + extra[0][...]
    copy = pltpu.make_async_copy(whole, out.at[:, 0, :], sem)
    copy.start()
    value = whole[...]
    squares = jnp.sum(jnp.sum(value * value, axis=0, keepdims=True), axis=1, keepdims=True)
    line = lax.broadcasted_iota(jnp.int32, (8, LANES), 0)
    numbers[...] = jnp.where(
        line == 0, jnp.broadcast_to(squares, (8, LANES)), jnp.where(line == 1, loss[0], 0.0)
    )
    copy.wait()


def merge(plan, place, loss, table, before, extra):
    return call(
        functools.partial(merge_kernel, plan),
        [
            jax.ShapeDtypeStruct((plan.rows_share, 1, LANES), F32),
            jax.ShapeDtypeStruct((8, LANES), F32),
        ],
        place,
        loss,
        table,
        before,
        extra,
        scratch=[pltpu.VMEM((plan.rows_share, LANES), F32), pltpu.SemaphoreType.DMA],
        smem=2,
        hbm_out=(0,),
    )


def adam_kernel(plan, edge, place, totals, *refs):
    ins, outs, refs = refs[:4], refs[4:7], refs[7:]
    norm_out, loss_out, held, sems = refs[0], refs[1], refs[2:9], refs[9]
    share, parts = plan.rows_share, sems.shape[1]
    size = ceil_to(-(-share // parts), 8)
    spans = [(part * size, min(size, share - part * size)) for part in range(parts)]

    def copies(part, arrays, scratch, first, outward):
        begin, count = spans[part]
        made = []
        for index, (array, kept) in enumerate(zip(arrays, scratch)):
            near = kept.at[pl.ds(begin, count)]
            far = array.at[pl.ds(begin, count), 0, :]
            pair = (near, far) if outward else (far, near)
            made.append(pltpu.make_async_copy(*pair, sems.at[first + index, part]))
        for copy in made:
            copy.start()
        return made

    coming = [copies(part, ins, held[:4], 0, False) for part in range(parts)]
    total = jnp.sum(totals[...], axis=0)
    norm = jnp.sqrt(total[0:1, :])
    norm_out[0] = jnp.max(norm)
    loss_out[0] = jnp.max(total[1:2, :])
    scale = CLIP_NORM / jnp.maximum(norm, CLIP_NORM)
    going = []
    for part in range(parts):
        begin, count = spans[part]
        for copy in coming[part]:
            copy.wait()
        at = slice(begin, begin + count)
        master, gradient, first, second = (kept[at, :] for kept in held[:4])
        clipped = gradient * scale
        moment = BETA_ONE * first + (1.0 - BETA_ONE) * clipped
        spread = BETA_TWO * second + (1.0 - BETA_TWO) * clipped * clipped
        step = (moment * (1.0 / (1.0 - BETA_ONE**STEP))) / (
            jnp.sqrt(spread * (1.0 / (1.0 - BETA_TWO**STEP))) + ADAM_EPS
        )
        lines = lax.broadcasted_iota(jnp.int32, (count, LANES), 0) + begin
        lane = lax.broadcasted_iota(jnp.int32, (count, LANES), 1)
        matrix_part = (lines + place[2] * share) * LANES + lane < edge
        rate = jnp.where(matrix_part, RATE_MATRIX, RATE_VECTOR)
        decay = jnp.where(matrix_part, WEIGHT_DECAY, 0.0)
        held[4][at, :] = master - rate * (step + decay * master)
        held[5][at, :] = moment
        held[6][at, :] = spread
        going.append(copies(part, outs, held[4:], 4, True))
    for made in going:
        for copy in made:
            copy.wait()


def round_kernel(value, out):
    out[...] = value[...].astype(BF16)


def mentor_kernel(plan, room, cuts, mentor, *refs):
    outs, stats = refs[:-1], refs[-1]
    m, masks, vocab = mentor.shape
    wide = 16 * LANES
    columns = []
    for part in range(m):
        pieces = [
            mentor[part, :, left : min(left + wide, vocab)].astype(F32) * (1.0 / SOFTEN_FACTOR)
            for left in range(0, vocab, wide)
        ]
        top = pieces[0]
        for piece in pieces[1:-1]:
            top = jnp.maximum(top, piece)
        top = jnp.maximum(
            jnp.max(top, axis=-1, keepdims=True), jnp.max(pieces[-1], axis=-1, keepdims=True)
        )
        total = jnp.exp(pieces[0] - top)
        for piece in pieces[1:-1]:
            total = total + jnp.exp(piece - top)
        total = jnp.sum(total, axis=-1, keepdims=True) + jnp.sum(
            jnp.exp(pieces[-1] - top), axis=-1, keepdims=True
        )
        columns.append((top, total))
    lane = lax.broadcasted_iota(jnp.int32, (m * masks, LANES), 1)
    top, total = (jnp.concatenate([column[k] for column in columns]) for k in range(2))
    both = jnp.where(lane == 0, top, jnp.where(lane == 1, total, 0.0))
    both = jnp.concatenate([both, jnp.zeros((LANES - m * masks, LANES), F32)])
    stats[...] = jnp.transpose(both)[0:8, :]
    for owner in range(plan.n):
        low = plan.first[owner]
        high = min(low + room, vocab)
        if high <= low:
            for out in outs:
                out[owner] = jnp.zeros(out.shape[1:], BF16)
            continue
        left = low // LANES * LANES
        right = min(ceil_to(high, LANES), vocab)
        for part in range(m):
            value = mentor[part, :, left:right].astype(F32)
            value = jnp.pad(value, ((0, 0), (0, ceil_to(high, LANES) + LANES - right)))
            if low > left:
                value = pltpu.roll(value, value.shape[1] - (low - left), 1)
            if high - low < room:
                value = jnp.pad(value[:, : high - low], ((0, 0), (0, room - (high - low))))
            value = value[:, 0:room].astype(BF16)
            for out, start in zip(outs, cuts):
                first = max(start, part * masks)
                last = min(start + out.shape[1], (part + 1) * masks)
                if first < last:
                    out[owner, first - start : last - start, :] = value[
                        first - part * masks : last - part * masks, :
                    ]


def table_pack(plan, place, grads):
    lines = ceil_to(max(plan.rows_share + 48, (plan.rows // 16 + 1) * 39 + 2), 8)
    return call(
        functools.partial(table_pack_kernel, plan),
        jax.ShapeDtypeStruct((plan.rows_share + 8, LANES), F32),
        place,
        grads,
        scratch=[
            pltpu.VMEM((3, plan.rows + 16, LANES), F32),
            pltpu.VMEM((lines, LANES), F32),
        ],
        smem=1,
    )


def unpack(plan, place, own, other, outs, lines, wide):
    share = plan.rows_share

    def load(tails):
        if not plan.special:
            lines[...] = tails[0][...].astype(F32)
            return
        half = plan.half_rows
        for quarter in range(4):
            y, x = divmod(quarter, 2)
            first = y * half
            end = min(first + half, share if x else plan.low_rows)
            at = first + (plan.low_rows if x else 0)
            size = half // CHUNKS
            for k in range(4):

                @pl.when(lax.rem(place[2], 4) == quarter ^ k)
                def _(k=k, at=at, length=end - first):
                    for chunk in range(CHUNKS):
                        rows = min(size, length - chunk * size)
                        lines[at + chunk * size : at + chunk * size + rows, :] = tails[
                            4 * chunk + k
                        ][...].astype(F32)[0:rows]

    for head in range(plan.m):
        mine = place[3] == head
        pl.when(mine)(lambda: load(own))
        pl.when(jnp.logical_not(mine))(lambda: load(other))
        for out, (base, width, rows) in zip(outs, plan.pieces):
            spread_rows(lines, wide, base, width, rows)
            for tile, left, part in column_tiles(width):
                if len(out.shape) == 4:
                    for kind in range(3):
                        value = wide[tile, kind * D : (kind + 1) * D, 0:part]
                        out[head, kind, :, left : left + part] = value.astype(BF16)
                else:
                    out[head, :, left : left + part] = wide[tile, 0:rows, 0:part].astype(BF16)


def piece_shapes(plan):
    shapes = [jax.ShapeDtypeStruct((plan.m, rows, width), BF16) for _, width, rows in plan.pieces]
    shapes[0] = jax.ShapeDtypeStruct((plan.m, 3, D, plan.width), BF16)
    return shapes


def piece_scratch(plan):
    tallest = max(rows for _, _, rows in plan.pieces)
    widest = max(-(-width // LANES) for _, width, _ in plan.pieces)
    return [pltpu.VMEM((plan.tail_pad, LANES), F32), pltpu.VMEM((widest, tallest, LANES), F32)]


def pack_kernel(plan, part_index, *refs):
    folding = plan.special and len(refs) == len(plan.pieces) + 4
    ins, refs = refs[: len(plan.pieces)], refs[len(plan.pieces) :]
    out, lines, wide = refs[-3:]
    lines[...] = refs[0][...] if len(refs) == 4 else jnp.zeros_like(lines)
    for source, (base, width, rows) in zip(ins, plan.pieces):
        for tile, left, part in column_tiles(width):
            if part < LANES:
                wide[tile, 0:rows, :] = jnp.zeros((rows, LANES), F32)
            if len(source.shape) == 4:
                for kind in range(3):
                    wide[tile, kind * D : (kind + 1) * D, 0:part] = source[
                        0, kind, :, left : left + part
                    ]
            else:
                wide[tile, 0:rows, 0:part] = source[0, :, left : left + part]
        pack_rows(wide, lines, base, width, rows)
    if not folding:
        out[...] = lines[...]
        return
    size, low, share = plan.slice_rows, plan.low_rows, plan.rows_share
    for index in range(8):
        for side, base, end in ((0, 0, low), (1, low, low + share)):
            first = base + index * size
            count = min(size, end - first)
            value = jnp.pad(lines[first : first + count, :], ((0, size - count), (0, 0)))
            out[2 * index + side] = value.astype(BF16)


def pack_tail(plan, part, pieces, *added):
    def chosen_block(value):
        rest = value.shape[1:]
        return pl.BlockSpec((1,) + rest, lambda i, part: (part[0],) + (0,) * len(rest))

    shape = jax.ShapeDtypeStruct((plan.tail_pad, LANES), F32)
    if plan.special and added:
        shape = jax.ShapeDtypeStruct((plan.n, plan.slice_rows, LANES), BF16)
    zeros = (0,) * len(shape.shape)
    return pl.pallas_call(
        functools.partial(pack_kernel, plan),
        out_shape=shape,
        grid_spec=pltpu.PrefetchScalarGridSpec(
            num_scalar_prefetch=1,
            grid=(1,),
            in_specs=[chosen_block(piece) for piece in pieces]
            + [pl.BlockSpec((plan.tail_pad, LANES), lambda i, part: (0, 0)) for _ in added],
            out_specs=pl.BlockSpec(shape.shape, lambda i, part: zeros),
            scratch_shapes=piece_scratch(plan),
        ),
        compiler_params=pltpu.CompilerParams(vmem_limit_bytes=VMEM_BYTES),
    )(part.reshape(1).astype(jnp.int32), *pieces, *added)


def slots_kernel(plan, slots, turn, ids, sent, slot_col):
    vocab, m = plan.vocab, plan.m

    def parts(value):
        head = jnp.zeros(value.shape, jnp.int32)
        for index in range(1, m):
            head = head + jnp.where(value >= index * vocab, 1, 0)
        row = value - head * vocab
        owner = jnp.zeros(value.shape, jnp.int32)
        for first in plan.first[1 : plan.n]:
            owner = owner + jnp.where(row >= first, 1, 0)
        return row, owner * m + head

    ids_row = ids[0:1, :]
    ids_col = jnp.transpose(jnp.broadcast_to(ids_row.astype(F32), (LANES, LEN)))[:, 0:1]
    ids_col = ids_col.astype(jnp.int32)
    row_row, owner_row = parts(ids_row)
    row_col, owner_col = parts(ids_col)
    same = ids_col == ids_row
    along = lax.broadcasted_iota(jnp.int32, (LEN, LEN), 1)
    down = lax.broadcasted_iota(jnp.int32, (LEN, LEN), 0)
    leader = jnp.min(jnp.where(same, along, LEN).astype(F32), axis=1, keepdims=True)
    lead_row = jnp.min(jnp.where(same, down, LEN).astype(F32), axis=0, keepdims=True)
    leads = lead_row == along[0:1, :].astype(F32)
    ahead = (owner_col == owner_row) & leads & (along.astype(F32) < leader)
    rank = jnp.sum(jnp.where(ahead, 1.0, 0.0), axis=1, keepdims=True).astype(jnp.int32)
    place = rank - turn[0] * slots
    slot = jnp.where((place >= 0) & (place < slots), owner_col * slots + place, -1)
    slot_col[...] = slot
    lane = lax.broadcasted_iota(jnp.int32, (LEN, LANES), 1)
    most = jnp.max(jnp.max(rank.astype(F32), axis=0, keepdims=True), axis=1, keepdims=True)
    needed = jnp.ones((1, 1), F32)
    for turn in range(1, LEN // slots):
        needed = needed + jnp.where(most >= turn * slots, 1.0, 0.0)
    lane_row = lax.broadcasted_iota(jnp.int32, (1, LANES), 1)
    inside = jnp.where(lane < slots, lane, -LEN * LEN)
    row_value = row_col.astype(F32)
    for device in range(sent.shape[0]):
        hit = slot - device * slots == inside
        asked = jnp.max(jnp.where(hit, row_value, -1.0), axis=0, keepdims=True)
        asked = jnp.where(lane_row == slots, needed, asked)
        sent[device : device + 1, :] = asked.astype(jnp.int32)


def add_rows_kernel(over, index, rows, total, out):
    size = rows.shape[0] if over == NN else out.shape[0]
    out[...] = total[...] + mm(hot_rows(index[...], size), rows[...], over)


def add_rows(over, index, rows, total):
    return call(
        functools.partial(add_rows_kernel, over),
        jax.ShapeDtypeStruct(total.shape, F32),
        index,
        rows,
        total,
    )


def rows_grad_kernel(grads, chosen, out):
    out[...] = mm(grads[...], chosen[...], TN)


def swap(value, axis, bit, size):
    return lax.ppermute(value, axis, [(i, i ^ bit) for i in range(size)])


def gather_to_all(value, plan):
    return lax.all_to_all(
        jnp.broadcast_to(value[None], (plan.n,) + value.shape), "dp", 0, 0, tiled=False
    )


def join_heads(value, head, m):
    if m != 2:
        return lax.all_gather(value, "head", axis=0, tiled=False)
    other = swap(value, "head", 1, m)
    mine_first = head == 0
    return jnp.stack([jnp.where(mine_first, value, other), jnp.where(mine_first, other, value)])


CHUNKS = 1


def tail_to_plane(plan, own):
    half = plan.half_rows
    size = half // CHUNKS
    d = lax.axis_index("dp")
    parts = []
    for first in range(0, half, size):
        part = lax.ppermute(own[first : first + size], "dp", [(14, 12), (15, 13)])
        parts.append(jnp.where(d >= 14, own[half + first : half + first + size], part))
    return parts


def tail_along_z(parts, step):
    pairs = [[(12, 4)], [(12, 8), (4, 0)]][step]
    perm = [(a + p, b + p) for a, b in pairs for p in range(4)]
    z = lax.axis_index("dp") // 4
    here = z == 1 if step == 0 else (z == 0) | (z == 2)
    return [jnp.where(here, lax.ppermute(part, "dp", perm), part) for part in parts]


def tail_in_plane(parts, n):
    return [one for part in parts for one in [part] + [swap(part, "dp", k, n) for k in (1, 2, 3)]]


def merge_stats(value, beside, plan):
    steps = [("head", 1 << bit, plan.m) for bit in range(plan.m.bit_length() - 1)]
    steps += [("dp", 1 << bit, plan.n) for bit in range(plan.n.bit_length() - 1)]
    for index, (axis, bit, size) in enumerate(steps):
        if index == 3:
            value, beside = lax.optimization_barrier((value, beside))
        other = swap(value, axis, bit, size)
        top = jnp.maximum(value[:2], other[:2])
        total = value[2:] * jnp.exp(value[:2] - top) + other[2:] * jnp.exp(other[:2] - top)
        value = jnp.concatenate([top, total])
    return value, beside


def gather_tail(plan, value):
    whole = lax.all_gather(value, "dp", axis=0, tiled=True)
    return jnp.pad(whole[plan.tail_row :], ((0, plan.tail_pad - plan.tail_rows), (0, 0)))


def reduce_tail(plan, tail):
    n, share = plan.n, plan.rows_share
    if not plan.special:
        total = lax.psum(tail, "dp")
        front = jnp.zeros((share, LANES), F32)
        start = lax.axis_index("dp") * share - plan.tail_row + share
        start = jnp.clip(start, 0, plan.tail_pad)
        return lax.dynamic_slice_in_dim(
            jnp.concatenate([front, total[: plan.tail_rows], front]), start, share
        )
    mine = jnp.sum(tail.astype(F32), axis=0)
    whole = []
    for k in range(7):
        whole.append(lax.ppermute(mine, "dp", [(2 * k, n - 2), (2 * k + 1, n - 1)]))
    return jnp.concatenate(whole + [mine])


def attention_kernel(proj, teacher, columns, sent_row, grad_q, grad_k, loss):
    @pl.when(pl.program_id(0) == 0)
    def _():
        loss[...] = jnp.zeros_like(loss)

    allowed = columns[:, 2:3] == sent_row[...]
    weight = columns[:, 3:4].astype(F32)
    plain = columns[:, 4:5].astype(F32)

    def probs(queries, key_heads, scale):
        scores = lax.dot_general(
            queries, key_heads, (((0,), (0,)), ((), ())), preferred_element_type=F32
        )
        scores = jnp.where(allowed, scores * scale, MASKED)
        exponent = jnp.exp(scores - jnp.max(scores, axis=-1, keepdims=True))
        return exponent * (1.0 / jnp.sum(exponent, axis=-1, keepdims=True))

    teacher_prob = probs(teacher[0, 0], teacher[1, 0], THD ** (-0.5))
    queries, key_heads = proj[0, 0], proj[1, 0]
    prob = probs(queries, key_heads, HD ** (-0.5))
    gap = (prob - teacher_prob) * weight
    loss[...] += jnp.sum(gap * gap, axis=0, keepdims=True) * ATT_WEIGHT
    pulled = prob * gap
    inner = jnp.sum(pulled, axis=-1, keepdims=True)
    grad_scores = (
        (pulled - prob * inner) * (plain * (2.0 * ATT_WEIGHT))
    ).astype(BF16)
    grad_q[0] = lax.dot_general(
        key_heads, grad_scores, (((1,), (1,)), ((), ())), preferred_element_type=F32
    )
    grad_k[0] = lax.dot_general(
        queries, grad_scores, (((1,), (0,)), ((), ())), preferred_element_type=F32
    )


def map_attention(first, heads, proj, teacher, columns, sent_row):
    whole = lambda i: (0, 0)
    return pl.pallas_call(
        attention_kernel,
        out_shape=[
            jax.ShapeDtypeStruct((heads, HP, LEN), F32),
            jax.ShapeDtypeStruct((heads, HP, LEN), F32),
            jax.ShapeDtypeStruct((1, LEN), F32),
        ],
        grid=(heads,),
        in_specs=[
            pl.BlockSpec((3, 1, HP, LEN), lambda i: (0, first + i, 0, 0)),
            pl.BlockSpec((2, 1, THD, LEN), lambda i: (0, first + i, 0, 0)),
            pl.BlockSpec(columns.shape, whole),
            pl.BlockSpec((1, LEN), whole),
        ],
        out_specs=[
            pl.BlockSpec((1, HP, LEN), lambda i: (i, 0, 0)),
            pl.BlockSpec((1, HP, LEN), lambda i: (i, 0, 0)),
            pl.BlockSpec((1, LEN), whole),
        ],
        compiler_params=pltpu.CompilerParams(vmem_limit_bytes=VMEM_BYTES),
    )(proj, teacher, columns, sent_row)


def mm(left, right, over):
    return lax.dot_general(left, right, (over, ((), ())), preferred_element_type=F32)


NN, NT, TN = ((1,), (0,)), ((1,), (1,)), ((0,), (0,))


def exact(hot, value, over, parts=3):
    total = None
    for _ in range(parts):
        piece = value.astype(BF16)
        value = value - piece.astype(F32)
        term = mm(hot, piece, over)
        total = term if total is None else total + term
    return total


def head_spread(width, per_head):
    row = lax.broadcasted_iota(jnp.int32, (width, per_head * HP), 0)
    column = lax.broadcasted_iota(jnp.int32, (width, per_head * HP), 1)
    for head in range(1, per_head):
        column = column - jnp.where(row >= head * HD, HP - HD, 0)
    return jnp.where(row == column, 1.0, 0.0).astype(BF16)


def hot_rows(index, size):
    column = lax.broadcasted_iota(jnp.int32, (index.shape[0], size), 1)
    return jnp.where(index == column, 1.0, 0.0).astype(BF16)


def softmax_rows(scores, allowed):
    scores = jnp.where(allowed, scores, MASKED)
    exponent = jnp.exp(scores - jnp.max(scores, axis=-1, keepdims=True))
    return exponent * (1.0 / jnp.sum(exponent, axis=-1, keepdims=True))


def norm_pull(gradient, normed, inverse, gain_row):
    scaled = gradient * gain_row
    inner_part = (
        scaled
        - jnp.mean(scaled, -1, keepdims=True)
        - normed * jnp.mean(scaled * normed, -1, keepdims=True)
    )
    return (
        inner_part * inverse,
        jnp.sum(gradient * normed, 0, keepdims=True),
        jnp.sum(gradient, 0, keepdims=True),
    )


ROOT_HALF = 0.5**0.5
BELL = (2.0 * 3.141592653589793) ** -0.5


def forward_kernel(plan, place, *refs):
    tails = len(refs) - 29
    own, other, refs = refs[: tails // 2], refs[tails // 2 : tails], refs[tails:]
    back, more_words, slot_col, columns, pick_columns, sent_row, *refs = refs
    attn_in, attn_out, ffn_in, ffn_out, shared_half, qv_bias, up_bias = refs[:7]
    (
        chosen,
        normed_zero,
        inverse_zero,
        proj,
        prob,
        mixed,
        normed_one,
        inverse_one,
        state_low,
        pre_act,
        hidden_act,
        normed_two,
        inverse_two,
        shared,
        lines,
        wide_rows,
    ) = refs[7:]
    unpack(plan, place, own, other, refs[:7], lines, wide_rows)
    m, _, _, width = attn_in.shape
    per_head = width // HD
    for part in range(m):
        shared[:, part * width : (part + 1) * width] = shared_half[part].astype(F32)
    position_hot = hot_rows(columns[:, 0:1], LEN)
    state = mm(hot_rows(slot_col[...], back.shape[0]), back[...], NN) + more_words[...]
    state = state + mm(position_hot, shared[0:LEN, :].astype(BF16), NN)
    state = state + jnp.where(columns[:, 1:2] == 0, shared[LEN : LEN + 1, :], shared[LEN + 1 : LEN + 2, :])
    state, (normed, inverse) = norm_forward(
        state, shared[LEN + 2 : LEN + 3, :], shared[LEN + 3 : LEN + 4, :]
    )
    normed_zero[...] = normed
    inverse_zero[...] = inverse
    gathered = state.astype(BF16)
    base = LEN + 4
    row = lambda index: shared[base + index : base + index + 1, :]

    spread = head_spread(width, per_head)
    for part in range(m):
        for kind in range(3):
            wide = mm(attn_in[part, kind], spread, NN).astype(BF16)
            value = mm(wide, gathered, ((0,), (1,)))
            if kind != 1:
                bias_row = qv_bias[part, kind // 2 : kind // 2 + 1, :]
                bias = mm(spread, jnp.broadcast_to(bias_row, (8, width)), ((0,), (1,)))
                value = value + bias[:, 0:1]
            value = value.astype(BF16).reshape(per_head, HP, LEN)
            proj[kind, part * per_head : (part + 1) * per_head] = value

    pick_hot = hot_rows(pick_columns[:, 0:1], LEN)
    allowed = pick_columns[:, 1:2] == sent_row[...]
    masks = pick_columns.shape[0]
    branch = jnp.zeros((masks, D), F32)
    for part in range(m):
        wide_out = mm(spread, attn_out[part], TN).astype(BF16)
        for index in range(per_head):
            head = part * per_head + index
            query = mm(pick_hot, proj[0, head], NT).astype(BF16)
            value = softmax_rows(mm(query, proj[1, head], NN) * HD ** (-0.5), allowed)
            prob[head] = value
            mix = mm(value.astype(BF16), proj[2, head], NT).astype(BF16)
            mixed[part, :, index * HP : (index + 1) * HP] = mix
            branch = branch + mm(mix, wide_out[index * HP : (index + 1) * HP, :], NN)
    state_one, (normed, inverse) = norm_forward(
        exact(pick_hot, state, NN) + branch + row(4), row(0), row(1)
    )
    normed_one[...] = normed
    inverse_one[...] = inverse
    low = state_one.astype(BF16)
    state_low[...] = low
    branch = jnp.zeros((masks, D), F32)
    for part in range(m):
        pre = mm(low, ffn_in[part], NN) + up_bias[part].astype(F32)
        pre_act[part] = pre
        act = (0.5 * pre * (1.0 + lax.erf(pre * ROOT_HALF))).astype(BF16)
        hidden_act[part] = act
        branch = branch + mm(act, ffn_out[part], NN)
    state_two, (normed, inverse) = norm_forward(state_one + branch + row(5), row(2), row(3))
    normed_two[...] = normed
    inverse_two[...] = inverse
    low = state_two.astype(BF16)
    for index in range(chosen.shape[0]):
        chosen[index] = low


def pick_gap_kernel(last_sentence, teacher, prob, pick_columns, sent_row, out):
    pick_hot = hot_rows(pick_columns[:, 0:1], LEN)
    pick_sentence = pick_columns[:, 1:2]
    allowed = pick_sentence == sent_row[...]
    weight = jnp.where(pick_sentence < last_sentence[0], 2.0 * ATT_WEIGHT, 0.0)
    for head in range(prob.shape[0]):
        query = mm(pick_hot, teacher[0, head], NT).astype(BF16)
        value = softmax_rows(mm(query, teacher[1, head], NN) * THD ** (-0.5), allowed)
        out[head] = (prob[head] - value) * weight


def backward_kernel(
    grad_pick,
    slot_col,
    columns,
    pick_columns,
    pos_row,
    attn_in,
    attn_out,
    ffn_in,
    ffn_out,
    shared_half,
    normed_zero,
    inverse_zero,
    proj,
    prob,
    mixed,
    normed_one,
    inverse_one,
    state_low,
    pre_act,
    hidden_act,
    normed_two,
    inverse_two,
    gap,
    map_q_low,
    map_k_low,
    map_q_high,
    map_k_high,
    grad_attn_in,
    grad_attn_out,
    grad_ffn_in,
    grad_ffn_out,
    grad_shared,
    grad_qv,
    grad_up,
    word_grads,
    slot_grads,
    shared,
    grad_proj,
    wide_out,
):
    m, _, _, width = attn_in.shape
    per_head = width // HD
    pos = pick_columns[:, 0:1]
    masks = pos.shape[0]
    for part in range(m):
        shared[:, part * width : (part + 1) * width] = shared_half[part, LEN:, :].astype(F32)
    row = lambda index: shared[index : index + 1, :]
    spread = head_spread(width, per_head)
    score_scale = HD ** (-0.5)

    repeats = pos == pos_row[...]
    order = lax.broadcasted_iota(jnp.int32, (masks, masks), 1)
    lead = jnp.min(jnp.where(repeats, order, masks).astype(F32), axis=1, keepdims=True)
    leads = lead == lax.broadcasted_iota(jnp.int32, (masks, 1), 0).astype(F32)
    gradient = exact(jnp.where(repeats, 1.0, 0.0).astype(BF16), grad_pick[...], NN)
    gradient = jnp.where(leads, gradient, 0.0)

    grad_res, gain_two, bias_two = norm_pull(
        gradient, normed_two[...], inverse_two[...], row(6)
    )
    grad_branch = grad_res.astype(BF16)
    grad_one = grad_res
    for part in range(m):
        pre = pre_act[part]
        grad_hidden = mm(grad_branch, ffn_out[part], NT)
        slope = 0.5 * (1.0 + lax.erf(pre * ROOT_HALF)) + pre * jnp.exp(-0.5 * pre * pre) * BELL
        grad_pre = (grad_hidden * slope).astype(BF16)
        grad_ffn_out[part] = mm(hidden_act[part], grad_branch, TN)
        grad_ffn_in[part] = mm(state_low[...], grad_pre, TN)
        grad_up[part] = jnp.sum(grad_pre.astype(F32), 0, keepdims=True)
        grad_one = grad_one + mm(grad_pre, ffn_in[part], NT)
    grad_mid, gain_one, bias_one = norm_pull(grad_one, normed_one[...], inverse_one[...], row(4))
    grad_attended = grad_mid.astype(BF16)

    pick_hot = hot_rows(pos, LEN)
    for part in range(m):
        narrow = mm(mixed[part], spread, NT).astype(BF16)
        grad_attn_out[part] = mm(narrow, grad_attended, TN)
        wide_out[part] = mm(spread, attn_out[part], TN).astype(BF16)
        for index in range(per_head):
            head = part * per_head + index
            at = slice(head * HP, (head + 1) * HP)
            map_q, map_k = (map_q_low, map_k_low) if head < HEADS // 2 else (map_q_high, map_k_high)
            grad_mixed = mm(
                grad_attended, wide_out[part, index * HP : (index + 1) * HP, :], NT
            ).astype(BF16)
            value = prob[head]
            grad_prob = mm(grad_mixed, proj[2, head], NN) + gap[head]
            grad_proj[2, at, :] = mm(grad_mixed, value.astype(BF16), TN).astype(BF16)
            grad_scores = value * (
                grad_prob - jnp.sum(value * grad_prob, axis=-1, keepdims=True)
            )
            grad_scores = jnp.where(leads, grad_scores, 0.0).astype(BF16)
            grad_query = (mm(grad_scores, proj[1, head], NT) * score_scale).astype(BF16)
            grad_proj[0, at, :] = (
                map_q[head % (HEADS // 2)] * score_scale + mm(grad_query, pick_hot, TN)
            ).astype(BF16)
            query = mm(pick_hot, proj[0, head], NT).astype(BF16)
            grad_proj[1, at, :] = (
                (map_k[head % (HEADS // 2)] + mm(query, grad_scores, TN)) * score_scale
            ).astype(BF16)

    normed = normed_zero[...]
    gathered = (normed * row(2) + row(3)).astype(BF16)
    grad_in = exact(pick_hot, grad_mid, TN)
    ones = jnp.ones((8, LEN), BF16)
    for part in range(m):
        for kind in range(3):
            first = part * per_head * HP
            narrow = mm(spread, grad_proj[kind, first : first + per_head * HP, :], NN).astype(BF16)
            grad_attn_in[part, kind] = mm(gathered, narrow, ((0,), (1,)))
            grad_in = grad_in + mm(narrow, attn_in[part, kind], ((0,), (1,)))
            if kind != 1:
                sums = mm(ones, narrow, NT)
                grad_qv[part, kind // 2 : kind // 2 + 1, :] = sums[0:1, :]
    grad_embed, gain_zero, bias_zero = norm_pull(grad_in, normed, inverse_zero[...], row(2))
    low = grad_embed.astype(BF16)
    word_grads[...] = low
    slot_grads[...] = mm(hot_rows(slot_col[...], slot_grads.shape[0]), low, TN).astype(BF16)
    positions = exact(hot_rows(columns[:, 0:1], LEN), grad_embed, TN, 2)
    ones_type = columns[:, 1:2] == 1
    rows = [
        jnp.sum(jnp.where(ones_type, 0.0, grad_embed), axis=0, keepdims=True),
        jnp.sum(jnp.where(ones_type, grad_embed, 0.0), axis=0, keepdims=True),
        gain_zero,
        bias_zero,
        gain_one,
        bias_one,
        gain_two,
        bias_two,
        jnp.sum(grad_mid, axis=0, keepdims=True),
        jnp.sum(grad_res, axis=0, keepdims=True),
    ]
    for part in range(m):
        at = slice(part * width, (part + 1) * width)
        grad_shared[part, 0:LEN, :] = positions[:, at]
        for index, value in enumerate(rows):
            grad_shared[part, LEN + index : LEN + index + 1, :] = value[:, at]


def masked_logits(places, chosen, words):
    soft = (chosen[...] * (1.0 / SOFTEN_FACTOR)).astype(BF16)
    column = lax.broadcasted_iota(jnp.int32, (1, words.shape[0]), 1)
    mask = jnp.where(column < places[1], 0.0, -1e30)
    return mm(soft, words[...], NT) + mask, mask


def logits_kernel(block, places, chosen, words, out):
    logits, _ = masked_logits(places, chosen, words)
    top = jnp.max(logits, axis=-1, keepdims=True)
    total = jnp.sum(jnp.exp(logits - top), axis=-1, keepdims=True)
    total = jnp.where(places[1] > 0, total, 0.0)
    lane = lax.broadcasted_iota(jnp.int32, (block, LANES), 1)
    both = jnp.where(lane == 0, top, jnp.where(lane == 1, total, 0.0))
    out[...] = jnp.transpose(both)[0:8, :]


def logits_stats(plan, place, chosen, words):
    picks = chosen.shape[0]
    block = 640
    return pl.pallas_call(
        functools.partial(logits_kernel, block),
        out_shape=jax.ShapeDtypeStruct((8, picks), F32),
        grid=(picks // block,),
        in_specs=[
            pl.BlockSpec(memory_space=pltpu.SMEM),
            pl.BlockSpec((block, chosen.shape[1]), lambda i: (i, 0)),
            pl.BlockSpec(words.shape, lambda i: (0, 0)),
        ],
        out_specs=pl.BlockSpec((8, block), lambda i: (0, i)),
        compiler_params=pltpu.CompilerParams(vmem_limit_bytes=VMEM_BYTES),
    )(place, chosen, words)


def grad_logits_kernel(block, places, chosen, words, *refs):
    parts_in, (stats, grads, own_pull, other_pull, losses, mentor) = refs[:-6], refs[-6:]
    first = 0
    size = sum(part.shape[1] for part in parts_in)
    for part in parts_in:
        for source in range(part.shape[0]):
            begin = source * size + first
            mentor[begin : begin + part.shape[1], :] = part[source]
        first += part.shape[1]
    step = pl.program_id(0)
    log_total = stats[0:1, :] + jnp.log(stats[2:3, :])
    log_mentor = stats[1:2, :] + jnp.log(stats[3:4, :])
    line = lax.broadcasted_iota(jnp.int32, (LANES, block), 0)
    both = jnp.transpose(jnp.where(line == 0, log_total, log_mentor))
    column_total, mentor_total = both[:, 0:1], both[:, 1:2]
    logits, mask = masked_logits(places, chosen, words)
    target = jnp.exp(mentor[...].astype(F32) * (1.0 / SOFTEN_FACTOR) + (mask - mentor_total))
    student = jnp.exp(logits - column_total)
    value = ((student - target) * (1.0 / SOFTEN_FACTOR)).astype(BF16)
    grads[...] = value
    sources, masks = own_pull.shape[:2]
    pulled = mm(value, words[...], NN).reshape(sources, 2, masks, D)
    first_head = places[3] == 0
    own_pull[...] = jnp.where(first_head, pulled[:, 0], pulled[:, 1])
    other_pull[...] = jnp.where(first_head, pulled[:, 1], pulled[:, 0]).astype(BF16)

    @pl.when(step == 0)
    def _():
        losses[...] = jnp.zeros_like(losses)

    cross = jnp.sum(jnp.sum(target * logits, axis=0, keepdims=True), axis=1, keepdims=True)
    own_share = jnp.sum(log_total, axis=1, keepdims=True)
    row = lax.broadcasted_iota(jnp.int32, (8, LANES), 0)
    losses[...] += jnp.where(row == 0, cross, jnp.where(row == 1, own_share, 0.0))


def grad_logits_call(plan, place, chosen, words, mentor, stats):
    picks = chosen.shape[0]
    sources = 8
    block = picks // plan.n * sources
    masks = picks // plan.n // plan.m
    rows = words.shape[0]
    return pl.pallas_call(
        functools.partial(grad_logits_kernel, block),
        out_shape=[
            jax.ShapeDtypeStruct((picks, rows), BF16),
            jax.ShapeDtypeStruct((plan.n, masks, D), F32),
            jax.ShapeDtypeStruct((plan.n, masks, D), BF16),
            jax.ShapeDtypeStruct((8, LANES), F32),
        ],
        grid=(picks // block,),
        in_specs=[
            pl.BlockSpec(memory_space=pltpu.SMEM),
            pl.BlockSpec((block, chosen.shape[1]), lambda i: (i, 0)),
            pl.BlockSpec(words.shape, lambda i: (0, 0)),
        ]
        + [pl.BlockSpec((sources,) + part.shape[1:], lambda i: (i, 0, 0)) for part in mentor]
        + [pl.BlockSpec((4, block), lambda i: (0, i))],
        out_specs=[
            pl.BlockSpec((block, rows), lambda i: (i, 0)),
            pl.BlockSpec((sources, masks, D), lambda i: (i, 0, 0)),
            pl.BlockSpec((sources, masks, D), lambda i: (i, 0, 0)),
            pl.BlockSpec((8, LANES), lambda i: (0, 0)),
        ],
        scratch_shapes=[pltpu.VMEM((block, rows), BF16)],
        compiler_params=pltpu.CompilerParams(vmem_limit_bytes=VMEM_BYTES),
    )(place, chosen, words, *mentor, stats)


def dot(spec, left, right, **options):
    return jnp.einsum(spec, left, right, preferred_element_type=F32, **options)


def one_hot(index, size):
    return (index[:, None] == jnp.arange(size, dtype=jnp.int32)[None, :]).astype(BF16)


def norm_forward(value, gain_row, bias_row):
    centred = value - jnp.mean(value, axis=-1, keepdims=True)
    inverse = lax.rsqrt(jnp.mean(centred * centred, axis=-1, keepdims=True) + NORM_EPS)
    normed = centred * inverse
    return (normed * gain_row + bias_row, (normed, inverse))


def local(
    master,
    first_moment,
    second_moment,
    token_ids,
    token_types,
    counts,
    mask_pos,
    teacher_states,
    teacher_qk,
    mentor_logits,
):
    n, m = lax.axis_size("dp"), lax.axis_size("head")
    d, h = lax.axis_index("dp"), lax.axis_index("head")
    share_len = master.shape[1]
    assert share_len % LANES == 0 and token_ids.shape[0] == m == 2
    plan = Plan(n, m, share_len)
    share = plan.rows_share
    devices = n * m
    slots = max(8, 1024 // devices)
    masks = mask_pos.shape[1]
    picks = devices * masks

    own_row = lambda value: lax.dynamic_index_in_dim(value, h, 0, keepdims=False)
    ids, types, sizes, pos = (own_row(v) for v in (token_ids, token_types, counts, mask_pos))

    order = jnp.arange(LEN, dtype=jnp.int32)

    def token_slots(turn):
        return call(
            functools.partial(slots_kernel, plan, slots),
            [
                jax.ShapeDtypeStruct((devices, LANES), jnp.int32),
                jax.ShapeDtypeStruct((LEN, 1), jnp.int32),
            ],
            jnp.reshape(turn, (1,)).astype(jnp.int32),
            jnp.broadcast_to(ids[None], (8, LEN)),
            smem=1,
        )

    sent_first, slot_col = token_slots(jnp.int32(0))

    def ask(sent):
        got = lax.all_to_all(sent, BOTH, 0, 0, tiled=True)
        asked = got[:, :slots].reshape(-1)
        return asked, got[:, slots]

    first_row = jnp.minimum((d * share_len + D - 1) // D, plan.vocab)
    row_count = jnp.minimum(((d + 1) * share_len + D - 1) // D, plan.vocab) - first_row

    chunk = master.reshape(share, 1, LANES)
    after = lax.ppermute(
        master[0, : 8 * LANES].reshape(8, LANES), "dp", [(i + 1, i) for i in range(n - 1)]
    )
    shift = jnp.where(row_count > 0, first_row * D - d * share_len, 0)
    place = jnp.stack([shift, row_count, d, h]).astype(jnp.int32)
    if plan.special:
        tail_part = share_rows(plan, place, chunk)
    else:
        tail_part = chunk.reshape(share, LANES).astype(BF16)

    words_own = table_rows(plan, place, chunk, after)

    own_index = lambda asked: jnp.where(asked >= 0, asked - first_row, -1)

    def fetch(asked):
        rows = dot(
            "sv,vd->sd", one_hot(own_index(asked), plan.rows), words_own
        ).astype(BF16)
        return lax.all_to_all(
            rows.reshape(devices, slots, D), BOTH, 0, 0, tiled=True
        ).reshape(-1, D)

    asked_first, needs = ask(sent_first)
    if plan.special:
        tail_part = tail_along_z(tail_to_plane(plan, tail_part), 0)
        asked_first, tail_part, words_own = lax.optimization_barrier(
            (asked_first, tail_part, words_own)
        )

    rounds = jnp.max(needs)
    back = fetch(asked_first)

    room = plan.rows

    send_mentor = lambda block: lax.all_to_all(block, "dp", 0, 0, tiled=False)
    cut = 32
    block_first, block_second, mentor_stats = call(
        functools.partial(mentor_kernel, plan, room, (0, cut)),
        [
            jax.ShapeDtypeStruct((n, cut, room), BF16),
            jax.ShapeDtypeStruct((n, m * masks - cut, room), BF16),
            jax.ShapeDtypeStruct((8, LANES), F32),
        ],
        mentor_logits,
    )

    teacher_weight = join_heads(teacher_qk, h, m)
    states = own_row(teacher_states)
    teacher_proj = dot("hdce,ld->chel", teacher_weight, states).astype(BF16)
    teacher_proj = teacher_proj.reshape(2, HEADS, THD, LEN)

    if plan.special:
        tail_part = tail_along_z(tail_part, 1)

    def more_words(state):
        sent, slot = token_slots(state[0])
        return state[0] + 1, add_rows(NN, slot, fetch(ask(sent)[0]), state[1])

    more_words = lax.while_loop(
        lambda state: state[0] < rounds, more_words, (jnp.int32(1), jnp.zeros((LEN, D), F32))
    )[1]
    tail_own = tail_in_plane(tail_part, n) if plan.special else [gather_tail(plan, tail_part)]


    ends = jnp.cumsum(sizes)
    passed = (order[:, None] >= ends[None, :]).astype(jnp.int32)
    sentence = jnp.sum(passed, axis=-1)
    within = order - jnp.sum(passed * sizes[None, :], axis=-1)
    valid = (sentence < sizes.shape[0] - 1).astype(jnp.int32)

    pick_sentence = jnp.sum(jnp.where(pos[:, None] == order[None, :], sentence[None, :], 0), 1)
    picked_any = jnp.sum((pos[:, None] == order[None, :]).astype(jnp.int32), axis=0) > 0
    columns = [within, types, sentence, valid, 1 - picked_any.astype(jnp.int32)]
    columns = jnp.stack(columns + [order] * 3, axis=1)
    pick_columns = jnp.stack([pos, pick_sentence], axis=1)

    tail_other = [swap(part, "head", 1, 2) for part in tail_own]
    back, tail_own, tail_other, block_first, teacher_proj, columns, pick_columns = (
        lax.optimization_barrier(
            (back, tail_own, tail_other, block_first, teacher_proj, columns, pick_columns)
        )
    )
    mentor_first = send_mentor(block_first)

    shape = jax.ShapeDtypeStruct
    attn_in, attn_out, ffn_in, ffn_out, shared_half, _, _, chosen_own, *saved = call(
        functools.partial(forward_kernel, plan),
        piece_shapes(plan)
        + [
            shape((n, masks, D), BF16),
            shape((LEN, D), F32),
            shape((LEN, 1), F32),
            shape((3, HEADS, HP, LEN), BF16),
            shape((HEADS, masks, LEN), F32),
            shape((m, masks, plan.width // HD * HP), BF16),
            shape((masks, D), F32),
            shape((masks, 1), F32),
            shape((masks, D), BF16),
            shape((m, masks, plan.units), F32),
            shape((m, masks, plan.units), BF16),
            shape((masks, D), F32),
            shape((masks, 1), F32),
        ],
        place,
        *tail_own,
        *tail_other,
        back,
        more_words,
        slot_col,
        columns,
        pick_columns,
        sentence[None],
        scratch=[pltpu.VMEM((SROWS, D), F32)] + piece_scratch(plan),
        smem=1,
    )
    proj = saved[2]

    chosen_own, mentor_first = lax.optimization_barrier((chosen_own, mentor_first))
    gap = call(
        pick_gap_kernel,
        shape((HEADS, masks, LEN), F32),
        jnp.array([sizes.shape[0] - 1], jnp.int32),
        teacher_proj,
        saved[3],
        pick_columns,
        sentence[None],
        smem=1,
    )
    chosen = lax.all_to_all(chosen_own, "dp", 0, 0, tiled=False)
    chosen, gap = lax.optimization_barrier((chosen, gap))
    halves = [
        map_attention(first, HEADS // 2, proj, teacher_proj, columns, sentence[None])
        for first in (0, HEADS // 2)
    ]
    chosen = join_heads(chosen, h, m)
    chosen = jnp.swapaxes(chosen, 0, 1).reshape(picks, D)
    chosen, block_second = lax.optimization_barrier((chosen, block_second))
    mentor_second = send_mentor(block_second)
    student = logits_stats(plan, place, chosen, words_own)
    nothing = jnp.concatenate([jnp.full((1, picks), -1e30, F32), jnp.zeros((1, picks), F32)])
    at = (0, d * m * masks)
    mentor_all = lax.dynamic_update_slice(nothing, mentor_stats[:2, : m * masks], at)
    stats = jnp.concatenate([student[:1], mentor_all[:1], student[1:2], mentor_all[1:]])
    stats, halves[0] = merge_stats(stats, halves[0], plan)
    mentor_here = [mentor_first, mentor_second]
    grad_logits, own_pull, other_pull, losses = grad_logits_call(
        plan, place, chosen, words_own, mentor_here, stats
    )
    map_rows = halves[0][2] + halves[1][2]
    loss_local = jnp.sum(map_rows) + losses[1, 0] / devices - losses[0, 0]
    mine = own_pull + swap(other_pull, "head", 1, 2).astype(F32)
    grad_pick = jnp.sum(
        lax.all_to_all(mine.astype(BF16), "dp", 0, 0, tiled=False).astype(F32), axis=0
    )

    *piece_grads, word_grads, slot_grads = call(
        backward_kernel,
        [
            shape((m, 3, D, plan.width), F32),
            shape((m, plan.width, D), F32),
            shape((m, D, plan.units), F32),
            shape((m, plan.units, D), F32),
            shape((m, SROWS, plan.width), F32),
            shape((m, 2, plan.width), F32),
            shape((m, 1, plan.units), F32),
            shape((LEN, D), BF16),
            shape((devices * slots, D), BF16),
        ],
        grad_pick,
        slot_col,
        columns,
        pick_columns,
        pos[None],
        attn_in,
        attn_out,
        ffn_in,
        ffn_out,
        shared_half,
        *saved,
        gap,
        *halves[0][:2],
        *halves[1][:2],
        scratch=[
            pltpu.VMEM((SROWS - LEN, D), F32),
            pltpu.VMEM((3, HEADS * HP, LEN), BF16),
            pltpu.VMEM((m, plan.width // HD * HP, D), BF16),
        ],
    )

    def give(slot_grads):
        return lax.all_to_all(
            slot_grads.reshape(devices, slots, D), BOTH, 0, 0, tiled=True
        ).reshape(-1, D)

    def more_grads(state):
        sent, slot = token_slots(state[0])
        asked = own_index(ask(sent)[0])[:, None]
        hot = one_hot(slot[:, 0], devices * slots)
        got = give(dot("ts,td->sd", hot, word_grads).astype(BF16))
        return state[0] + 1, add_rows(TN, asked, got, state[1])

    given = give(slot_grads)
    tail_sent = pack_tail(plan, 1 - h, piece_grads)
    tail = pack_tail(plan, h, piece_grads, swap(tail_sent, "head", 1, 2))
    grad_table = call(
        rows_grad_kernel, jax.ShapeDtypeStruct((plan.rows, D), F32), grad_logits, chosen
    )
    tail, given, grad_table = lax.optimization_barrier((tail, given, grad_table))
    if plan.special:
        tail = lax.all_to_all(tail, "dp", 0, 0, tiled=False)

    grad_table = add_rows(TN, own_index(asked_first)[:, None], given, grad_table)
    grad_table = lax.while_loop(
        lambda state: state[0] < rounds, more_grads, (jnp.int32(1), grad_table)
    )[1]
    table_lines = table_pack(plan, place, grad_table)
    before = lax.ppermute(table_lines[share:], "dp", [(i, i + 1) for i in range(n - 1)])

    tail, table_lines, loss_local = lax.optimization_barrier((tail, table_lines, loss_local))
    gradient, numbers = merge(
        plan, place, loss_local.reshape(1), table_lines, before, reduce_tail(plan, tail)
    )

    numbers = numbers + swap(numbers, "head", 1, 2)
    totals = gather_to_all(numbers, plan)
    vector_start = plan.table + plan.width * D * 4 + 2 * D * plan.units + (LEN + 2) * plan.width
    lines = jax.ShapeDtypeStruct((share, 1, LANES), F32)
    *updated, norm, loss_sum = call(
        functools.partial(adam_kernel, plan, vector_start),
        [lines, lines, lines] + [jax.ShapeDtypeStruct((1,), F32)] * 2,
        place,
        totals,
        chunk,
        gradient,
        first_moment.reshape(share, 1, LANES),
        second_moment.reshape(share, 1, LANES),
        scratch=[pltpu.VMEM((share, LANES), F32)] * 7 + [pltpu.SemaphoreType.DMA((7, 4))],
        smem=1,
        hbm=(2, 3, 4, 5),
        hbm_out=(0, 1, 2),
        smem_out=(3, 4),
    )
    updated = [value.reshape(1, share_len) for value in updated]
    weights = call(round_kernel, jax.ShapeDtypeStruct((1, share_len), BF16), updated[0])
    return (loss_sum.reshape(()), norm.reshape(()), *updated, weights)


def solution(mesh):
    return jax.shard_map(
        local,
        mesh=mesh,
        in_specs=(
            P("head", "dp"),
            P("head", "dp"),
            P("head", "dp"),
            P("dp", None),
            P("dp", None),
            P("dp", None),
            P("dp", None),
            P("dp", None, None),
            P(None, None, "head"),
            P("dp", None, "head"),
        ),
        out_specs=(P(), P(), P("head", "dp"), P("head", "dp"), P("head", "dp"), P("head", "dp")),
        check_vma=False,
    )
```

```python
import functools

import jax
import jax.numpy as jnp
from jax import lax
from jax.experimental import pallas as pl
from jax.experimental.pallas import tpu as pltpu
from jax.sharding import PartitionSpec as P

D = 312
HEADS = 12
HD = 26
HP = 32
FF = 1200
VOCAB = 30522
THD = 64
LEN = 512
STEP = 10
SROWS = 522

ATT_WEIGHT = 1.0
SOFTEN_FACTOR = 2.0
CLIP_NORM = 1.0
BETA_ONE = 0.9
BETA_TWO = 0.999
RATE_MATRIX = 0.06
RATE_VECTOR = 0.6
WEIGHT_DECAY = 0.01
ADAM_EPS = 1e-08
NORM_EPS = 1e-12
MASKED = -1000000000.0

F32 = jnp.float32
BF16 = jnp.bfloat16
LANES = 128
BOTH = ("dp", "head")
VMEM_BYTES = 56 * 1024 * 1024


def ceil_to(value, unit):
    return -(-value // unit) * unit


def call(kernel, out_shape, *args, scratch=(), smem=0, hbm=(), hbm_out=(), smem_out=()):
    space = lambda index: pltpu.SMEM if index < smem else pl.ANY if index in hbm else pltpu.VMEM
    in_specs = [pl.BlockSpec(memory_space=space(index)) for index in range(len(args))]
    outs = out_shape if isinstance(out_shape, list) else [out_shape]
    out_specs = [
        pl.BlockSpec(
            memory_space=pl.ANY
            if index in hbm_out
            else pltpu.SMEM
            if index in smem_out
            else pltpu.VMEM
        )
        for index in range(len(outs))
    ]
    out_specs = out_specs if isinstance(out_shape, list) else out_specs[0]
    return pl.pallas_call(
        kernel,
        out_shape=out_shape,
        in_specs=in_specs,
        out_specs=out_specs,
        scratch_shapes=list(scratch),
        compiler_params=pltpu.CompilerParams(vmem_limit_bytes=VMEM_BYTES),
    )(*args)


class Plan:
    def __init__(self, n, m, share):
        self.n, self.m, self.share = n, m, share
        self.rows_share = share // LANES
        self.vocab = VOCAB // m
        self.width = D // m
        self.units = FF // m
        self.first = [min(-(-d * share // D), self.vocab) for d in range(n + 1)]
        widest = -(-share // D)
        self.rows = ceil_to(widest + 3, 16)
        table = self.vocab * D
        self.table = table
        self.tail_row = table // LANES
        self.tail_off = table % LANES
        self.tail_rows = n * self.rows_share - self.tail_row
        self.tail_pad = ceil_to(self.tail_rows + 40, 16)
        w, u = self.width, self.units
        self.pieces = []
        base = self.tail_off
        for rows, wide in ((3 * D, w), (w, D), (D, u), (u, D), (SROWS, w), (2, w), (1, u)):
            self.pieces.append((base, wide, rows))
            base += rows * wide
        self.special = n == 16 and self.tail_row // self.rows_share == n - 2
        if self.special:
            self.low_rows = (n - 1) * self.rows_share - self.tail_row
            self.slice_rows = ceil_to(-(-self.rows_share // 8), 16)
            self.half_rows = 4 * self.slice_rows


def period(width):
    step = 16
    while step * width % LANES:
        step *= 2
    return step, step * width // LANES


def rows_at(start, count, stride):
    return pl.ds(start, count) if count == 1 else pl.ds(start, count, stride=stride)


def spread_rows(src, dst, base, width, rows):
    step, lane_rows = period(width)
    tiles = -(-width // LANES)
    for phase in range(min(step, rows)):
        count = len(range(phase, rows, step))
        line, off = divmod(base + phase * width, LANES)
        loaded = [
            src[rows_at(line + j, count, lane_rows), :] for j in range(tiles + (1 if off else 0))
        ]
        lane = lax.broadcasted_iota(jnp.int32, (count, LANES), 1)
        for tile in range(tiles):
            value = loaded[tile]
            if off:
                value = jnp.where(
                    lane < LANES - off,
                    pltpu.roll(value, LANES - off, 1),
                    pltpu.roll(loaded[tile + 1], LANES - off, 1),
                )
            dst[tile, rows_at(phase, count, step), :] = value


def pack_rows(src, dst, base, width, rows):
    step, lane_rows = period(width)
    tiles = -(-width // LANES)
    for phase in range(min(step, rows)):
        count = len(range(phase, rows, step))
        line, off = divmod(base + phase * width, LANES)
        loaded = [
            src[tile, rows_at(phase, count, step), :] for tile in range(tiles)
        ]
        lane = lax.broadcasted_iota(jnp.int32, (count, LANES), 1)
        rolled = [pltpu.roll(value, off, 1) if off else value for value in loaded]
        for j in range(-(-(off + width) // LANES)):
            value = jnp.zeros((count, LANES), F32)
            if j < tiles:
                value = jnp.where(lane >= off, rolled[j], value)
            if off and j > 0:
                value = jnp.where(lane < off, rolled[j - 1], value)
            at = rows_at(line + j, count, lane_rows)
            dst[at, :] = dst[at, :] + value


def column_tiles(width):
    return [(t, t * LANES, min(LANES, width - t * LANES)) for t in range(-(-width // LANES))]


def shift_lines(source, count, start, max_line):
    low, high = start // LANES, lax.rem(start, LANES)
    first = source[0:count, :]
    second = source[1 : count + 1, :]
    for line in range(1, max_line + 1):
        first = jnp.where(low == line, source[line : count + line, :], first)
        second = jnp.where(low == line, source[line + 1 : count + line + 1, :], second)
    lane = lax.broadcasted_iota(jnp.int32, (count, LANES), 1)
    back = lax.rem(LANES - high, LANES)
    return jnp.where(lane < LANES - high, pltpu.roll(first, back, 1), pltpu.roll(second, back, 1))


def bring(source, target, sem):
    copy = pltpu.make_async_copy(source, target, sem)
    copy.start()
    copy.wait()


def share_rows_kernel(plan, place, chunk, out, lines, sem):
    share, low = plan.rows_share, plan.low_rows
    lines[share & -8 :, :] = jnp.zeros((lines.shape[0] - (share & -8), LANES), F32)
    bring(chunk.at[:, 0, :], lines.at[0:share], sem)
    count = out.shape[0]
    begins_late = place[2] == plan.n - 2
    first = share - low
    out[...] = jnp.where(
        begins_late, lines[first : first + count, :], lines[0:count, :]
    ).astype(BF16)


def share_rows(plan, place, chunk):
    count = 8 * plan.slice_rows
    return call(
        functools.partial(share_rows_kernel, plan),
        jax.ShapeDtypeStruct((count, LANES), BF16),
        place,
        chunk,
        scratch=[
            pltpu.VMEM((ceil_to(count + plan.rows_share - plan.low_rows, 8), LANES), F32),
            pltpu.SemaphoreType.DMA,
        ],
        smem=1,
        hbm=(1,),
    )


def table_rows_kernel(plan, place, chunk, after, out, joined, shifted, rows, sem):
    share = plan.rows_share
    lines = joined.shape[0]
    joined[share & -8 :, :] = jnp.zeros((lines - (share & -8), LANES), F32)
    bring(chunk.at[:, 0, :], joined.at[0:share], sem)
    joined[share : share + 8, :] = after[...]
    shifted[...] = jnp.zeros_like(shifted)
    shifted[0 : share + 2, :] = shift_lines(joined, share + 2, place[0], 2)
    spread_rows(shifted, rows, 0, D, plan.rows)
    row = lax.broadcasted_iota(jnp.int32, (plan.rows, LANES), 0)
    for tile, left, wide in column_tiles(D):
        value = jnp.where(row < place[1], rows[tile], 0.0).astype(BF16)
        out[:, left : left + wide] = value[:, 0:wide]


def table_rows(plan, place, chunk, after):
    lines = ceil_to(max(plan.rows_share + 16, plan.rows // 16 * 39 + 2), 8)
    return call(
        functools.partial(table_rows_kernel, plan),
        jax.ShapeDtypeStruct((plan.rows, D), BF16),
        place,
        chunk,
        after,
        scratch=[
            pltpu.VMEM((lines, LANES), F32),
            pltpu.VMEM((lines, LANES), F32),
            pltpu.VMEM((3, plan.rows, LANES), F32),
            pltpu.SemaphoreType.DMA,
        ],
        smem=1,
        hbm=(1,),
    )


def table_pack_kernel(plan, place, index, given, grads, out, rows, lines):
    total = grads[...] + mm(hot_rows(index[...], plan.rows), given[...], TN)
    rows[...] = jnp.zeros_like(rows)
    for tile, left, wide in column_tiles(D):
        rows[tile, 16 : 16 + plan.rows, 0:wide] = total[:, left : left + wide]
    lines[...] = jnp.zeros_like(lines)
    pack_rows(rows, lines, 0, D, plan.rows + 16)
    count = plan.rows_share + 8
    start = 39 * LANES - place[0]
    low, high = start // LANES - 36, lax.rem(start, LANES)
    first = lines[36 : 36 + count, :]
    second = lines[37 : 37 + count, :]
    for line in range(1, 4):
        first = jnp.where(low == line, lines[36 + line : 36 + line + count, :], first)
        second = jnp.where(low == line, lines[37 + line : 37 + line + count, :], second)
    lane = lax.broadcasted_iota(jnp.int32, (count, LANES), 1)
    back = lax.rem(LANES - high, LANES)
    value = jnp.where(
        lane < LANES - high, pltpu.roll(first, back, 1), pltpu.roll(second, back, 1)
    )
    line = lax.broadcasted_iota(jnp.int32, (count, LANES), 0)
    index = (line + place[2] * plan.rows_share) * LANES + lane
    out[...] = jnp.where(index < plan.table, value, 0.0)


def merge_kernel(plan, place, loss, table, before, *refs):
    extra, (out, numbers, whole, sem) = refs[:-4], refs[-4:]
    size = plan.slice_rows if plan.special else plan.rows_share
    share = plan.rows_share
    whole[...] = table[0:share, :]
    whole[0:8, :] = whole[0:8, :] + before[...]
    if plan.special:
        d, low = place[2], plan.low_rows
        for owner, first, count in ((plan.n - 2, share - low, low), (plan.n - 1, 0, share)):

            @pl.when(d == owner)
            def _(first=first, count=count):
                for index, part in enumerate(extra):
                    begin = first + index * size
                    end = min(begin + size, first + count)
                    whole[begin:end, :] = whole[begin:end, :] + part[0 : end - begin, :]

    else:
        whole[...] = whole[...] + extra[0][...]
    copy = pltpu.make_async_copy(whole, out.at[:, 0, :], sem)
    copy.start()
    value = whole[...]
    squares = jnp.sum(jnp.sum(value * value, axis=0, keepdims=True), axis=1, keepdims=True)
    line = lax.broadcasted_iota(jnp.int32, (8, LANES), 0)
    numbers[...] = jnp.where(
        line == 0, jnp.broadcast_to(squares, (8, LANES)), jnp.where(line == 1, loss[0], 0.0)
    )
    copy.wait()


def merge(plan, place, loss, table, before, extra):
    return call(
        functools.partial(merge_kernel, plan),
        [
            jax.ShapeDtypeStruct((plan.rows_share, 1, LANES), F32),
            jax.ShapeDtypeStruct((8, LANES), F32),
        ],
        place,
        loss,
        table,
        before,
        *extra,
        scratch=[pltpu.VMEM((plan.rows_share, LANES), F32), pltpu.SemaphoreType.DMA],
        smem=2,
        hbm_out=(0,),
    )


def adam_kernel(plan, edge, place, totals, *refs):
    ins, outs, refs = refs[:4], refs[4:7], refs[7:]
    norm_out, loss_out, held, sems = refs[0], refs[1], refs[2:9], refs[9]
    share, parts = plan.rows_share, sems.shape[1]
    size = ceil_to(-(-share // parts), 8)
    spans = [(part * size, min(size, share - part * size)) for part in range(parts)]

    def copies(part, arrays, scratch, first, outward):
        begin, count = spans[part]
        made = []
        for index, (array, kept) in enumerate(zip(arrays, scratch)):
            near = kept.at[pl.ds(begin, count)]
            far = array.at[pl.ds(begin, count), 0, :]
            pair = (near, far) if outward else (far, near)
            made.append(pltpu.make_async_copy(*pair, sems.at[first + index, part]))
        for copy in made:
            copy.start()
        return made

    coming = [copies(part, ins, held[:4], 0, False) for part in range(parts)]
    total = jnp.sum(totals[...], axis=0)
    norm = jnp.sqrt(total[0:1, :])
    norm_out[0] = jnp.max(norm)
    loss_out[0] = jnp.max(total[1:2, :])
    scale = CLIP_NORM / jnp.maximum(norm, CLIP_NORM)
    going = []
    for part in range(parts):
        begin, count = spans[part]
        for copy in coming[part]:
            copy.wait()
        at = slice(begin, begin + count)
        master, gradient, first, second = (kept[at, :] for kept in held[:4])
        clipped = gradient * scale
        moment = BETA_ONE * first + (1.0 - BETA_ONE) * clipped
        spread = BETA_TWO * second + (1.0 - BETA_TWO) * clipped * clipped
        step = (moment * (1.0 / (1.0 - BETA_ONE**STEP))) / (
            jnp.sqrt(spread * (1.0 / (1.0 - BETA_TWO**STEP))) + ADAM_EPS
        )
        lines = lax.broadcasted_iota(jnp.int32, (count, LANES), 0) + begin
        lane = lax.broadcasted_iota(jnp.int32, (count, LANES), 1)
        matrix_part = (lines + place[2] * share) * LANES + lane < edge
        rate = jnp.where(matrix_part, RATE_MATRIX, RATE_VECTOR)
        decay = jnp.where(matrix_part, WEIGHT_DECAY, 0.0)
        held[4][at, :] = master - rate * (step + decay * master)
        held[5][at, :] = moment
        held[6][at, :] = spread
        going.append(copies(part, outs, held[4:], 4, True))
    for made in going:
        for copy in made:
            copy.wait()


def round_kernel(value, out):
    out[...] = value[...].astype(BF16)


def mentor_kernel(plan, room, cuts, mentor, *refs):
    outs, stats = refs[:-1], refs[-1]
    m, masks, vocab = mentor.shape
    wide = 16 * LANES
    columns = []
    for part in range(m):
        pieces = [
            mentor[part, :, left : min(left + wide, vocab)].astype(F32) * (1.0 / SOFTEN_FACTOR)
            for left in range(0, vocab, wide)
        ]
        top = pieces[0]
        for piece in pieces[1:-1]:
            top = jnp.maximum(top, piece)
        top = jnp.maximum(
            jnp.max(top, axis=-1, keepdims=True), jnp.max(pieces[-1], axis=-1, keepdims=True)
        )
        total = jnp.exp(pieces[0] - top)
        for piece in pieces[1:-1]:
            total = total + jnp.exp(piece - top)
        total = jnp.sum(total, axis=-1, keepdims=True) + jnp.sum(
            jnp.exp(pieces[-1] - top), axis=-1, keepdims=True
        )
        columns.append((top, total))
    lane = lax.broadcasted_iota(jnp.int32, (m * masks, LANES), 1)
    top, total = (jnp.concatenate([column[k] for column in columns]) for k in range(2))
    both = jnp.where(lane == 0, top, jnp.where(lane == 1, total, 0.0))
    both = jnp.concatenate([both, jnp.zeros((LANES - m * masks, LANES), F32)])
    stats[...] = jnp.transpose(both)[0:8, :]
    for owner in range(plan.n):
        low = plan.first[owner]
        high = min(low + room, vocab)
        if high <= low:
            for out in outs:
                out[owner] = jnp.zeros(out.shape[1:], BF16)
            continue
        left = low // LANES * LANES
        right = min(ceil_to(high, LANES), vocab)
        for part in range(m):
            value = mentor[part, :, left:right].astype(F32)
            value = jnp.pad(value, ((0, 0), (0, ceil_to(high, LANES) + LANES - right)))
            if low > left:
                value = pltpu.roll(value, value.shape[1] - (low - left), 1)
            if high - low < room:
                value = jnp.pad(value[:, : high - low], ((0, 0), (0, room - (high - low))))
            value = value[:, 0:room].astype(BF16)
            for out, start in zip(outs, cuts):
                first = max(start, part * masks)
                last = min(start + out.shape[1], (part + 1) * masks)
                if first < last:
                    out[owner, first - start : last - start, :] = value[
                        first - part * masks : last - part * masks, :
                    ]


def table_pack(plan, place, index, given, grads):
    lines = ceil_to(max(plan.rows_share + 48, (plan.rows // 16 + 1) * 39 + 2), 8)
    return call(
        functools.partial(table_pack_kernel, plan),
        jax.ShapeDtypeStruct((plan.rows_share + 8, LANES), F32),
        place,
        index[:, None],
        given,
        grads,
        scratch=[
            pltpu.VMEM((3, plan.rows + 16, LANES), F32),
            pltpu.VMEM((lines, LANES), F32),
        ],
        smem=1,
    )


def unpack(plan, place, own, other, outs, lines, wide):
    share = plan.rows_share

    def load(tails):
        if not plan.special:
            lines[...] = tails[0][...].astype(F32)
            return
        half = plan.half_rows
        for quarter in range(4):
            y, x = divmod(quarter, 2)
            first = y * half
            end = min(first + half, share if x else plan.low_rows)
            at = first + (plan.low_rows if x else 0)
            size = half // CHUNKS
            for k in range(4):

                @pl.when(lax.rem(place[2], 4) == quarter ^ k)
                def _(k=k, at=at, length=end - first):
                    for chunk in range(CHUNKS):
                        rows = min(size, length - chunk * size)
                        lines[at + chunk * size : at + chunk * size + rows, :] = tails[
                            4 * chunk + k
                        ][...].astype(F32)[0:rows]

    for head in range(plan.m):
        mine = place[3] == head
        pl.when(mine)(lambda: load(own))
        pl.when(jnp.logical_not(mine))(lambda: load(other))
        for out, (base, width, rows) in zip(outs, plan.pieces):
            spread_rows(lines, wide, base, width, rows)
            for tile, left, part in column_tiles(width):
                if len(out.shape) == 4:
                    for kind in range(3):
                        value = wide[tile, kind * D : (kind + 1) * D, 0:part]
                        out[head, kind, :, left : left + part] = value.astype(BF16)
                else:
                    out[head, :, left : left + part] = wide[tile, 0:rows, 0:part].astype(BF16)


def piece_shapes(plan):
    shapes = [jax.ShapeDtypeStruct((plan.m, rows, width), BF16) for _, width, rows in plan.pieces]
    shapes[0] = jax.ShapeDtypeStruct((plan.m, 3, D, plan.width), BF16)
    return shapes


def piece_scratch(plan):
    tallest = max(rows for _, _, rows in plan.pieces)
    widest = max(-(-width // LANES) for _, width, _ in plan.pieces)
    return [pltpu.VMEM((plan.tail_pad, LANES), F32), pltpu.VMEM((widest, tallest, LANES), F32)]


def pack_kernel(plan, part_index, *refs):
    folding = plan.special and len(refs) == len(plan.pieces) + 4
    ins, refs = refs[: len(plan.pieces)], refs[len(plan.pieces) :]
    out, lines, wide = refs[-3:]
    lines[...] = refs[0][...] if len(refs) == 4 else jnp.zeros_like(lines)
    for source, (base, width, rows) in zip(ins, plan.pieces):
        for tile, left, part in column_tiles(width):
            if part < LANES:
                wide[tile, 0:rows, :] = jnp.zeros((rows, LANES), F32)
            if len(source.shape) == 4:
                for kind in range(3):
                    wide[tile, kind * D : (kind + 1) * D, 0:part] = source[
                        0, kind, :, left : left + part
                    ]
            else:
                wide[tile, 0:rows, 0:part] = source[0, :, left : left + part]
        pack_rows(wide, lines, base, width, rows)
    if not folding:
        out[...] = lines[...]
        return
    size, low, share = plan.slice_rows, plan.low_rows, plan.rows_share
    for index in range(8):
        for side, base, end in ((0, 0, low), (1, low, low + share)):
            first = base + index * size
            count = min(size, end - first)
            value = jnp.pad(lines[first : first + count, :], ((0, size - count), (0, 0)))
            out[2 * index + side] = value.astype(BF16)


def pack_tail(plan, part, pieces, *added):
    def chosen_block(value):
        rest = value.shape[1:]
        return pl.BlockSpec((1,) + rest, lambda i, part: (part[0],) + (0,) * len(rest))

    shape = jax.ShapeDtypeStruct((plan.tail_pad, LANES), F32)
    if plan.special and added:
        shape = jax.ShapeDtypeStruct((plan.n, plan.slice_rows, LANES), BF16)
    zeros = (0,) * len(shape.shape)
    return pl.pallas_call(
        functools.partial(pack_kernel, plan),
        out_shape=shape,
        grid_spec=pltpu.PrefetchScalarGridSpec(
            num_scalar_prefetch=1,
            grid=(1,),
            in_specs=[chosen_block(piece) for piece in pieces]
            + [pl.BlockSpec((plan.tail_pad, LANES), lambda i, part: (0, 0)) for _ in added],
            out_specs=pl.BlockSpec(shape.shape, lambda i, part: zeros),
            scratch_shapes=piece_scratch(plan),
        ),
        compiler_params=pltpu.CompilerParams(vmem_limit_bytes=VMEM_BYTES),
    )(part.reshape(1).astype(jnp.int32), *pieces, *added)


def slots_kernel(plan, slots, turn, ids, sent, slot_col):
    vocab, m = plan.vocab, plan.m

    def parts(value):
        head = jnp.zeros(value.shape, jnp.int32)
        for index in range(1, m):
            head = head + jnp.where(value >= index * vocab, 1, 0)
        row = value - head * vocab
        owner = jnp.zeros(value.shape, jnp.int32)
        for first in plan.first[1 : plan.n]:
            owner = owner + jnp.where(row >= first, 1, 0)
        return row, owner * m + head

    ids_row = ids[0:1, :]
    ids_col = jnp.transpose(jnp.broadcast_to(ids_row.astype(F32), (LANES, LEN)))[:, 0:1]
    ids_col = ids_col.astype(jnp.int32)
    row_row, owner_row = parts(ids_row)
    row_col, owner_col = parts(ids_col)
    same = ids_col == ids_row
    along = lax.broadcasted_iota(jnp.int32, (LEN, LEN), 1)
    down = lax.broadcasted_iota(jnp.int32, (LEN, LEN), 0)
    leader = jnp.min(jnp.where(same, along, LEN).astype(F32), axis=1, keepdims=True)
    lead_row = jnp.min(jnp.where(same, down, LEN).astype(F32), axis=0, keepdims=True)
    leads = lead_row == along[0:1, :].astype(F32)
    ahead = (owner_col == owner_row) & leads & (along.astype(F32) < leader)
    rank = jnp.sum(jnp.where(ahead, 1.0, 0.0), axis=1, keepdims=True).astype(jnp.int32)
    place = rank - turn[0] * slots
    slot = jnp.where((place >= 0) & (place < slots), owner_col * slots + place, -1)
    slot_col[...] = slot
    lane = lax.broadcasted_iota(jnp.int32, (LEN, LANES), 1)
    most = jnp.max(jnp.max(rank.astype(F32), axis=0, keepdims=True), axis=1, keepdims=True)
    needed = jnp.ones((1, 1), F32)
    for turn in range(1, LEN // slots):
        needed = needed + jnp.where(most >= turn * slots, 1.0, 0.0)
    lane_row = lax.broadcasted_iota(jnp.int32, (1, LANES), 1)
    inside = jnp.where(lane < slots, lane, -LEN * LEN)
    row_value = row_col.astype(F32)
    for device in range(sent.shape[0]):
        hit = slot - device * slots == inside
        asked = jnp.max(jnp.where(hit, row_value, -1.0), axis=0, keepdims=True)
        asked = jnp.where(lane_row == slots, needed, asked)
        sent[device : device + 1, :] = asked.astype(jnp.int32)


def add_rows_kernel(over, index, rows, total, out):
    size = rows.shape[0] if over == NN else out.shape[0]
    out[...] = total[...] + mm(hot_rows(index[...], size), rows[...], over)


def add_rows(over, index, rows, total):
    return call(
        functools.partial(add_rows_kernel, over),
        jax.ShapeDtypeStruct(total.shape, F32),
        index,
        rows,
        total,
    )


def rows_grad_kernel(grads, chosen, out):
    out[...] = mm(grads[...], chosen[...], TN)


def swap(value, axis, bit, size):
    return lax.ppermute(value, axis, [(i, i ^ bit) for i in range(size)])


def gather_to_all(value, plan):
    return lax.all_to_all(
        jnp.broadcast_to(value[None], (plan.n,) + value.shape), "dp", 0, 0, tiled=False
    )


def join_heads(value, head, m):
    if m != 2:
        return lax.all_gather(value, "head", axis=0, tiled=False)
    other = swap(value, "head", 1, m)
    mine_first = head == 0
    return jnp.stack([jnp.where(mine_first, value, other), jnp.where(mine_first, other, value)])


CHUNKS = 1


def tail_to_plane(plan, own):
    half = plan.half_rows
    size = half // CHUNKS
    d = lax.axis_index("dp")
    parts = []
    for first in range(0, half, size):
        part = lax.ppermute(own[first : first + size], "dp", [(14, 12), (15, 13)])
        parts.append(jnp.where(d >= 14, own[half + first : half + first + size], part))
    return parts


def tail_along_z(parts, step):
    pairs = [[(12, 4)], [(12, 8), (4, 0)]][step]
    perm = [(a + p, b + p) for a, b in pairs for p in range(4)]
    z = lax.axis_index("dp") // 4
    here = z == 1 if step == 0 else (z == 0) | (z == 2)
    return [jnp.where(here, lax.ppermute(part, "dp", perm), part) for part in parts]


def tail_in_plane(parts, n):
    return [one for part in parts for one in [part] + [swap(part, "dp", k, n) for k in (1, 2, 3)]]


def merge_stats(value, beside, plan):
    steps = [("head", 1 << bit, plan.m) for bit in range(plan.m.bit_length() - 1)]
    steps += [("dp", 1 << bit, plan.n) for bit in range(plan.n.bit_length() - 1)]
    for index, (axis, bit, size) in enumerate(steps):
        if index == 3:
            value, beside = lax.optimization_barrier((value, beside))
        other = swap(value, axis, bit, size)
        top = jnp.maximum(value[:2], other[:2])
        total = value[2:] * jnp.exp(value[:2] - top) + other[2:] * jnp.exp(other[:2] - top)
        value = jnp.concatenate([top, total])
    return value, beside


def gather_tail(plan, value):
    whole = lax.all_gather(value, "dp", axis=0, tiled=True)
    return jnp.pad(whole[plan.tail_row :], ((0, plan.tail_pad - plan.tail_rows), (0, 0)))


def reduce_tail(plan, tail):
    n, share = plan.n, plan.rows_share
    if not plan.special:
        total = lax.psum(tail, "dp")
        front = jnp.zeros((share, LANES), F32)
        start = lax.axis_index("dp") * share - plan.tail_row + share
        start = jnp.clip(start, 0, plan.tail_pad)
        padded = jnp.concatenate([front, total[: plan.tail_rows], front])
        return [lax.dynamic_slice_in_dim(padded, start, share)]
    mine = jnp.sum(tail.astype(F32), axis=0)
    whole = []
    for k in range(7):
        whole.append(lax.ppermute(mine, "dp", [(2 * k, n - 2), (2 * k + 1, n - 1)]))
    return whole + [mine]


def attention_kernel(proj, teacher, columns, sent_row, grad_q, grad_k, loss):
    @pl.when(pl.program_id(0) == 0)
    def _():
        loss[...] = jnp.zeros_like(loss)

    allowed = columns[:, 2:3] == sent_row[...]
    weight = columns[:, 3:4].astype(F32)
    plain = columns[:, 4:5].astype(F32)

    def probs(queries, key_heads, scale):
        scores = lax.dot_general(
            queries, key_heads, (((0,), (0,)), ((), ())), preferred_element_type=F32
        )
        scores = jnp.where(allowed, scores * scale, MASKED)
        exponent = jnp.exp(scores - jnp.max(scores, axis=-1, keepdims=True))
        return exponent * (1.0 / jnp.sum(exponent, axis=-1, keepdims=True))

    teacher_prob = probs(teacher[0, 0], teacher[1, 0], THD ** (-0.5))
    queries, key_heads = proj[0, 0], proj[1, 0]
    prob = probs(queries, key_heads, HD ** (-0.5))
    gap = (prob - teacher_prob) * weight
    loss[...] += jnp.sum(gap * gap, axis=0, keepdims=True) * ATT_WEIGHT
    pulled = prob * gap
    inner = jnp.sum(pulled, axis=-1, keepdims=True)
    grad_scores = (
        (pulled - prob * inner) * (plain * (2.0 * ATT_WEIGHT))
    ).astype(BF16)
    grad_q[0] = lax.dot_general(
        key_heads, grad_scores, (((1,), (1,)), ((), ())), preferred_element_type=F32
    )
    grad_k[0] = lax.dot_general(
        queries, grad_scores, (((1,), (0,)), ((), ())), preferred_element_type=F32
    )


def map_attention(first, heads, proj, teacher, columns, sent_row):
    whole = lambda i: (0, 0)
    return pl.pallas_call(
        attention_kernel,
        out_shape=[
            jax.ShapeDtypeStruct((heads, HP, LEN), F32),
            jax.ShapeDtypeStruct((heads, HP, LEN), F32),
            jax.ShapeDtypeStruct((1, LEN), F32),
        ],
        grid=(heads,),
        in_specs=[
            pl.BlockSpec((3, 1, HP, LEN), lambda i: (0, first + i, 0, 0)),
            pl.BlockSpec((2, 1, THD, LEN), lambda i: (0, first + i, 0, 0)),
            pl.BlockSpec(columns.shape, whole),
            pl.BlockSpec((1, LEN), whole),
        ],
        out_specs=[
            pl.BlockSpec((1, HP, LEN), lambda i: (i, 0, 0)),
            pl.BlockSpec((1, HP, LEN), lambda i: (i, 0, 0)),
            pl.BlockSpec((1, LEN), whole),
        ],
        compiler_params=pltpu.CompilerParams(vmem_limit_bytes=VMEM_BYTES),
    )(proj, teacher, columns, sent_row)


def mm(left, right, over):
    return lax.dot_general(left, right, (over, ((), ())), preferred_element_type=F32)


NN, NT, TN = ((1,), (0,)), ((1,), (1,)), ((0,), (0,))


def exact(hot, value, over, parts=3):
    total = None
    for _ in range(parts):
        piece = value.astype(BF16)
        value = value - piece.astype(F32)
        term = mm(hot, piece, over)
        total = term if total is None else total + term
    return total


def head_spread(width, per_head):
    row = lax.broadcasted_iota(jnp.int32, (width, per_head * HP), 0)
    column = lax.broadcasted_iota(jnp.int32, (width, per_head * HP), 1)
    for head in range(1, per_head):
        column = column - jnp.where(row >= head * HD, HP - HD, 0)
    return jnp.where(row == column, 1.0, 0.0).astype(BF16)


def hot_rows(index, size):
    column = lax.broadcasted_iota(jnp.int32, (index.shape[0], size), 1)
    return jnp.where(index == column, 1.0, 0.0).astype(BF16)


def softmax_rows(scores, allowed):
    scores = jnp.where(allowed, scores, MASKED)
    exponent = jnp.exp(scores - jnp.max(scores, axis=-1, keepdims=True))
    return exponent * (1.0 / jnp.sum(exponent, axis=-1, keepdims=True))


def norm_pull(gradient, normed, inverse, gain_row):
    scaled = gradient * gain_row
    inner_part = (
        scaled
        - jnp.mean(scaled, -1, keepdims=True)
        - normed * jnp.mean(scaled * normed, -1, keepdims=True)
    )
    return (
        inner_part * inverse,
        jnp.sum(gradient * normed, 0, keepdims=True),
        jnp.sum(gradient, 0, keepdims=True),
    )


ROOT_HALF = 0.5**0.5
BELL = (2.0 * 3.141592653589793) ** -0.5


def forward_kernel(plan, place, *refs):
    tails = len(refs) - 29
    own, other, refs = refs[: tails // 2], refs[tails // 2 : tails], refs[tails:]
    back, more_words, slot_col, columns, pick_columns, sent_row, *refs = refs
    attn_in, attn_out, ffn_in, ffn_out, shared_half, qv_bias, up_bias = refs[:7]
    (
        chosen,
        normed_zero,
        inverse_zero,
        proj,
        prob,
        mixed,
        normed_one,
        inverse_one,
        state_low,
        pre_act,
        hidden_act,
        normed_two,
        inverse_two,
        shared,
        lines,
        wide_rows,
    ) = refs[7:]
    unpack(plan, place, own, other, refs[:7], lines, wide_rows)
    m, _, _, width = attn_in.shape
    per_head = width // HD
    for part in range(m):
        shared[:, part * width : (part + 1) * width] = shared_half[part].astype(F32)
    position_hot = hot_rows(columns[:, 0:1], LEN)
    state = mm(hot_rows(slot_col[...], back.shape[0]), back[...], NN) + more_words[...]
    state = state + mm(position_hot, shared[0:LEN, :].astype(BF16), NN)
    state = state + jnp.where(columns[:, 1:2] == 0, shared[LEN : LEN + 1, :], shared[LEN + 1 : LEN + 2, :])
    state, (normed, inverse) = norm_forward(
        state, shared[LEN + 2 : LEN + 3, :], shared[LEN + 3 : LEN + 4, :]
    )
    normed_zero[...] = normed
    inverse_zero[...] = inverse
    gathered = state.astype(BF16)
    base = LEN + 4
    row = lambda index: shared[base + index : base + index + 1, :]

    spread = head_spread(width, per_head)
    for part in range(m):
        for kind in range(3):
            wide = mm(attn_in[part, kind], spread, NN).astype(BF16)
            value = mm(wide, gathered, ((0,), (1,)))
            if kind != 1:
                bias_row = qv_bias[part, kind // 2 : kind // 2 + 1, :]
                bias = mm(spread, jnp.broadcast_to(bias_row, (8, width)), ((0,), (1,)))
                value = value + bias[:, 0:1]
            value = value.astype(BF16).reshape(per_head, HP, LEN)
            proj[kind, part * per_head : (part + 1) * per_head] = value

    pick_hot = hot_rows(pick_columns[:, 0:1], LEN)
    allowed = pick_columns[:, 1:2] == sent_row[...]
    masks = pick_columns.shape[0]
    branch = jnp.zeros((masks, D), F32)
    for part in range(m):
        wide_out = mm(spread, attn_out[part], TN).astype(BF16)
        for index in range(per_head):
            head = part * per_head + index
            query = mm(pick_hot, proj[0, head], NT).astype(BF16)
            value = softmax_rows(mm(query, proj[1, head], NN) * HD ** (-0.5), allowed)
            prob[head] = value
            mix = mm(value.astype(BF16), proj[2, head], NT).astype(BF16)
            mixed[part, :, index * HP : (index + 1) * HP] = mix
            branch = branch + mm(mix, wide_out[index * HP : (index + 1) * HP, :], NN)
    state_one, (normed, inverse) = norm_forward(
        exact(pick_hot, state, NN) + branch + row(4), row(0), row(1)
    )
    normed_one[...] = normed
    inverse_one[...] = inverse
    low = state_one.astype(BF16)
    state_low[...] = low
    branch = jnp.zeros((masks, D), F32)
    for part in range(m):
        pre = mm(low, ffn_in[part], NN) + up_bias[part].astype(F32)
        pre_act[part] = pre
        act = (0.5 * pre * (1.0 + lax.erf(pre * ROOT_HALF))).astype(BF16)
        hidden_act[part] = act
        branch = branch + mm(act, ffn_out[part], NN)
    state_two, (normed, inverse) = norm_forward(state_one + branch + row(5), row(2), row(3))
    normed_two[...] = normed
    inverse_two[...] = inverse
    low = state_two.astype(BF16)
    for index in range(chosen.shape[0]):
        chosen[index] = low


def pick_gap_kernel(last_sentence, teacher, prob, pick_columns, sent_row, out):
    pick_hot = hot_rows(pick_columns[:, 0:1], LEN)
    pick_sentence = pick_columns[:, 1:2]
    allowed = pick_sentence == sent_row[...]
    weight = jnp.where(pick_sentence < last_sentence[0], 2.0 * ATT_WEIGHT, 0.0)
    for head in range(prob.shape[0]):
        query = mm(pick_hot, teacher[0, head], NT).astype(BF16)
        value = softmax_rows(mm(query, teacher[1, head], NN) * THD ** (-0.5), allowed)
        out[head] = (prob[head] - value) * weight


def backward_kernel(
    grad_pick,
    slot_col,
    columns,
    pick_columns,
    pos_row,
    attn_in,
    attn_out,
    ffn_in,
    ffn_out,
    shared_half,
    normed_zero,
    inverse_zero,
    proj,
    prob,
    mixed,
    normed_one,
    inverse_one,
    state_low,
    pre_act,
    hidden_act,
    normed_two,
    inverse_two,
    gap,
    map_q_low,
    map_k_low,
    map_q_high,
    map_k_high,
    grad_attn_in,
    grad_attn_out,
    grad_ffn_in,
    grad_ffn_out,
    grad_shared,
    grad_qv,
    grad_up,
    word_grads,
    slot_grads,
    shared,
    grad_proj,
    wide_out,
):
    m, _, _, width = attn_in.shape
    per_head = width // HD
    pos = pick_columns[:, 0:1]
    masks = pos.shape[0]
    for part in range(m):
        shared[:, part * width : (part + 1) * width] = shared_half[part, LEN:, :].astype(F32)
    row = lambda index: shared[index : index + 1, :]
    spread = head_spread(width, per_head)
    score_scale = HD ** (-0.5)

    repeats = pos == pos_row[...]
    order = lax.broadcasted_iota(jnp.int32, (masks, masks), 1)
    lead = jnp.min(jnp.where(repeats, order, masks).astype(F32), axis=1, keepdims=True)
    leads = lead == lax.broadcasted_iota(jnp.int32, (masks, 1), 0).astype(F32)
    gradient = exact(jnp.where(repeats, 1.0, 0.0).astype(BF16), grad_pick[...], NN)
    gradient = jnp.where(leads, gradient, 0.0)

    grad_res, gain_two, bias_two = norm_pull(
        gradient, normed_two[...], inverse_two[...], row(6)
    )
    grad_branch = grad_res.astype(BF16)
    grad_one = grad_res
    for part in range(m):
        pre = pre_act[part]
        grad_hidden = mm(grad_branch, ffn_out[part], NT)
        slope = 0.5 * (1.0 + lax.erf(pre * ROOT_HALF)) + pre * jnp.exp(-0.5 * pre * pre) * BELL
        grad_pre = (grad_hidden * slope).astype(BF16)
        grad_ffn_out[part] = mm(hidden_act[part], grad_branch, TN)
        grad_ffn_in[part] = mm(state_low[...], grad_pre, TN)
        grad_up[part] = jnp.sum(grad_pre.astype(F32), 0, keepdims=True)
        grad_one = grad_one + mm(grad_pre, ffn_in[part], NT)
    grad_mid, gain_one, bias_one = norm_pull(grad_one, normed_one[...], inverse_one[...], row(4))
    grad_attended = grad_mid.astype(BF16)

    pick_hot = hot_rows(pos, LEN)
    for part in range(m):
        narrow = mm(mixed[part], spread, NT).astype(BF16)
        grad_attn_out[part] = mm(narrow, grad_attended, TN)
        wide_out[part] = mm(spread, attn_out[part], TN).astype(BF16)
        for index in range(per_head):
            head = part * per_head + index
            at = slice(head * HP, (head + 1) * HP)
            map_q, map_k = (map_q_low, map_k_low) if head < HEADS // 2 else (map_q_high, map_k_high)
            grad_mixed = mm(
                grad_attended, wide_out[part, index * HP : (index + 1) * HP, :], NT
            ).astype(BF16)
            value = prob[head]
            grad_prob = mm(grad_mixed, proj[2, head], NN) + gap[head]
            grad_proj[2, at, :] = mm(grad_mixed, value.astype(BF16), TN).astype(BF16)
            grad_scores = value * (
                grad_prob - jnp.sum(value * grad_prob, axis=-1, keepdims=True)
            )
            grad_scores = jnp.where(leads, grad_scores, 0.0).astype(BF16)
            grad_query = (mm(grad_scores, proj[1, head], NT) * score_scale).astype(BF16)
            grad_proj[0, at, :] = (
                map_q[head % (HEADS // 2)] * score_scale + mm(grad_query, pick_hot, TN)
            ).astype(BF16)
            query = mm(pick_hot, proj[0, head], NT).astype(BF16)
            grad_proj[1, at, :] = (
                (map_k[head % (HEADS // 2)] + mm(query, grad_scores, TN)) * score_scale
            ).astype(BF16)

    normed = normed_zero[...]
    gathered = (normed * row(2) + row(3)).astype(BF16)
    grad_in = exact(pick_hot, grad_mid, TN)
    ones = jnp.ones((8, LEN), BF16)
    for part in range(m):
        for kind in range(3):
            first = part * per_head * HP
            narrow = mm(spread, grad_proj[kind, first : first + per_head * HP, :], NN).astype(BF16)
            grad_attn_in[part, kind] = mm(gathered, narrow, ((0,), (1,)))
            grad_in = grad_in + mm(narrow, attn_in[part, kind], ((0,), (1,)))
            if kind != 1:
                sums = mm(ones, narrow, NT)
                grad_qv[part, kind // 2 : kind // 2 + 1, :] = sums[0:1, :]
    grad_embed, gain_zero, bias_zero = norm_pull(grad_in, normed, inverse_zero[...], row(2))
    low = grad_embed.astype(BF16)
    word_grads[...] = low
    slot_grads[...] = mm(hot_rows(slot_col[...], slot_grads.shape[0]), low, TN).astype(BF16)
    positions = exact(hot_rows(columns[:, 0:1], LEN), grad_embed, TN, 2)
    ones_type = columns[:, 1:2] == 1
    rows = [
        jnp.sum(jnp.where(ones_type, 0.0, grad_embed), axis=0, keepdims=True),
        jnp.sum(jnp.where(ones_type, grad_embed, 0.0), axis=0, keepdims=True),
        gain_zero,
        bias_zero,
        gain_one,
        bias_one,
        gain_two,
        bias_two,
        jnp.sum(grad_mid, axis=0, keepdims=True),
        jnp.sum(grad_res, axis=0, keepdims=True),
    ]
    for part in range(m):
        at = slice(part * width, (part + 1) * width)
        grad_shared[part, 0:LEN, :] = positions[:, at]
        for index, value in enumerate(rows):
            grad_shared[part, LEN + index : LEN + index + 1, :] = value[:, at]


def masked_logits(places, chosen, words):
    soft = (chosen[...] * (1.0 / SOFTEN_FACTOR)).astype(BF16)
    column = lax.broadcasted_iota(jnp.int32, (1, words.shape[0]), 1)
    mask = jnp.where(column < places[1], 0.0, -1e30)
    return mm(soft, words[...], NT) + mask, mask


def logits_kernel(block, places, chosen, words, out):
    logits, _ = masked_logits(places, chosen, words)
    top = jnp.max(logits, axis=-1, keepdims=True)
    total = jnp.sum(jnp.exp(logits - top), axis=-1, keepdims=True)
    total = jnp.where(places[1] > 0, total, 0.0)
    lane = lax.broadcasted_iota(jnp.int32, (block, LANES), 1)
    both = jnp.where(lane == 0, top, jnp.where(lane == 1, total, 0.0))
    out[...] = jnp.transpose(both)[0:8, :]


def logits_stats(plan, place, chosen, words):
    picks = chosen.shape[0]
    block = 640
    return pl.pallas_call(
        functools.partial(logits_kernel, block),
        out_shape=jax.ShapeDtypeStruct((8, picks), F32),
        grid=(picks // block,),
        in_specs=[
            pl.BlockSpec(memory_space=pltpu.SMEM),
            pl.BlockSpec((block, chosen.shape[1]), lambda i: (i, 0)),
            pl.BlockSpec(words.shape, lambda i: (0, 0)),
        ],
        out_specs=pl.BlockSpec((8, block), lambda i: (0, i)),
        compiler_params=pltpu.CompilerParams(vmem_limit_bytes=VMEM_BYTES),
    )(place, chosen, words)


def grad_logits_kernel(block, places, chosen, words, *refs):
    parts_in, (stats, grads, own_pull, other_pull, losses, mentor) = refs[:-6], refs[-6:]
    first = 0
    size = sum(part.shape[1] for part in parts_in)
    for part in parts_in:
        for source in range(part.shape[0]):
            begin = source * size + first
            mentor[begin : begin + part.shape[1], :] = part[source]
        first += part.shape[1]
    step = pl.program_id(0)
    log_total = stats[0:1, :] + jnp.log(stats[2:3, :])
    log_mentor = stats[1:2, :] + jnp.log(stats[3:4, :])
    line = lax.broadcasted_iota(jnp.int32, (LANES, block), 0)
    both = jnp.transpose(jnp.where(line == 0, log_total, log_mentor))
    column_total, mentor_total = both[:, 0:1], both[:, 1:2]
    logits, mask = masked_logits(places, chosen, words)
    target = jnp.exp(mentor[...].astype(F32) * (1.0 / SOFTEN_FACTOR) + (mask - mentor_total))
    student = jnp.exp(logits - column_total)
    value = ((student - target) * (1.0 / SOFTEN_FACTOR)).astype(BF16)
    grads[...] = value
    sources, masks = own_pull.shape[:2]
    pulled = mm(value, words[...], NN).reshape(sources, 2, masks, D)
    first_head = places[3] == 0
    own_pull[...] = jnp.where(first_head, pulled[:, 0], pulled[:, 1])
    other_pull[...] = jnp.where(first_head, pulled[:, 1], pulled[:, 0]).astype(BF16)

    @pl.when(step == 0)
    def _():
        losses[...] = jnp.zeros_like(losses)

    cross = jnp.sum(jnp.sum(target * logits, axis=0, keepdims=True), axis=1, keepdims=True)
    own_share = jnp.sum(log_total, axis=1, keepdims=True)
    row = lax.broadcasted_iota(jnp.int32, (8, LANES), 0)
    losses[...] += jnp.where(row == 0, cross, jnp.where(row == 1, own_share, 0.0))


def grad_logits_call(plan, place, chosen, words, mentor, stats):
    picks = chosen.shape[0]
    sources = 8
    block = picks // plan.n * sources
    masks = picks // plan.n // plan.m
    rows = words.shape[0]
    return pl.pallas_call(
        functools.partial(grad_logits_kernel, block),
        out_shape=[
            jax.ShapeDtypeStruct((picks, rows), BF16),
            jax.ShapeDtypeStruct((plan.n, masks, D), F32),
            jax.ShapeDtypeStruct((plan.n, masks, D), BF16),
            jax.ShapeDtypeStruct((8, LANES), F32),
        ],
        grid=(picks // block,),
        in_specs=[
            pl.BlockSpec(memory_space=pltpu.SMEM),
            pl.BlockSpec((block, chosen.shape[1]), lambda i: (i, 0)),
            pl.BlockSpec(words.shape, lambda i: (0, 0)),
        ]
        + [pl.BlockSpec((sources,) + part.shape[1:], lambda i: (i, 0, 0)) for part in mentor]
        + [pl.BlockSpec((4, block), lambda i: (0, i))],
        out_specs=[
            pl.BlockSpec((block, rows), lambda i: (i, 0)),
            pl.BlockSpec((sources, masks, D), lambda i: (i, 0, 0)),
            pl.BlockSpec((sources, masks, D), lambda i: (i, 0, 0)),
            pl.BlockSpec((8, LANES), lambda i: (0, 0)),
        ],
        scratch_shapes=[pltpu.VMEM((block, rows), BF16)],
        compiler_params=pltpu.CompilerParams(vmem_limit_bytes=VMEM_BYTES),
    )(place, chosen, words, *mentor, stats)


def dot(spec, left, right, **options):
    return jnp.einsum(spec, left, right, preferred_element_type=F32, **options)


def one_hot(index, size):
    return (index[:, None] == jnp.arange(size, dtype=jnp.int32)[None, :]).astype(BF16)


def norm_forward(value, gain_row, bias_row):
    centred = value - jnp.mean(value, axis=-1, keepdims=True)
    inverse = lax.rsqrt(jnp.mean(centred * centred, axis=-1, keepdims=True) + NORM_EPS)
    normed = centred * inverse
    return (normed * gain_row + bias_row, (normed, inverse))


def local(
    master,
    first_moment,
    second_moment,
    token_ids,
    token_types,
    counts,
    mask_pos,
    teacher_states,
    teacher_qk,
    mentor_logits,
):
    n, m = lax.axis_size("dp"), lax.axis_size("head")
    d, h = lax.axis_index("dp"), lax.axis_index("head")
    share_len = master.shape[1]
    assert share_len % LANES == 0 and token_ids.shape[0] == m == 2
    plan = Plan(n, m, share_len)
    share = plan.rows_share
    devices = n * m
    slots = max(8, 1024 // devices)
    masks = mask_pos.shape[1]
    picks = devices * masks

    own_row = lambda value: lax.dynamic_index_in_dim(value, h, 0, keepdims=False)
    ids, types, sizes, pos = (own_row(v) for v in (token_ids, token_types, counts, mask_pos))

    order = jnp.arange(LEN, dtype=jnp.int32)

    def token_slots(turn):
        return call(
            functools.partial(slots_kernel, plan, slots),
            [
                jax.ShapeDtypeStruct((devices, LANES), jnp.int32),
                jax.ShapeDtypeStruct((LEN, 1), jnp.int32),
            ],
            jnp.reshape(turn, (1,)).astype(jnp.int32),
            jnp.broadcast_to(ids[None], (8, LEN)),
            smem=1,
        )

    sent_first, slot_col = token_slots(jnp.int32(0))

    def ask(sent):
        got = lax.all_to_all(sent, BOTH, 0, 0, tiled=True)
        asked = got[:, :slots].reshape(-1)
        return asked, got[:, slots]

    first_row = jnp.minimum((d * share_len + D - 1) // D, plan.vocab)
    row_count = jnp.minimum(((d + 1) * share_len + D - 1) // D, plan.vocab) - first_row

    chunk = master.reshape(share, 1, LANES)
    after = lax.ppermute(
        master[0, : 8 * LANES].reshape(8, LANES), "dp", [(i + 1, i) for i in range(n - 1)]
    )
    shift = jnp.where(row_count > 0, first_row * D - d * share_len, 0)
    place = jnp.stack([shift, row_count, d, h]).astype(jnp.int32)
    if plan.special:
        tail_part = share_rows(plan, place, chunk)
    else:
        tail_part = chunk.reshape(share, LANES).astype(BF16)

    words_own = table_rows(plan, place, chunk, after)

    own_index = lambda asked: jnp.where(asked >= 0, asked - first_row, -1)

    def fetch(asked):
        rows = dot(
            "sv,vd->sd", one_hot(own_index(asked), plan.rows), words_own
        ).astype(BF16)
        return lax.all_to_all(
            rows.reshape(devices, slots, D), BOTH, 0, 0, tiled=True
        ).reshape(-1, D)

    asked_first, needs = ask(sent_first)
    if plan.special:
        tail_part = tail_along_z(tail_to_plane(plan, tail_part), 0)
        asked_first, tail_part, words_own = lax.optimization_barrier(
            (asked_first, tail_part, words_own)
        )

    rounds = jnp.max(needs)
    back = fetch(asked_first)

    room = plan.rows

    send_mentor = lambda block: lax.all_to_all(block, "dp", 0, 0, tiled=False)
    cut = 32
    block_first, block_second, mentor_stats = call(
        functools.partial(mentor_kernel, plan, room, (0, cut)),
        [
            jax.ShapeDtypeStruct((n, cut, room), BF16),
            jax.ShapeDtypeStruct((n, m * masks - cut, room), BF16),
            jax.ShapeDtypeStruct((8, LANES), F32),
        ],
        mentor_logits,
    )

    teacher_weight = join_heads(teacher_qk, h, m)
    states = own_row(teacher_states)
    teacher_proj = dot("hdce,ld->chel", teacher_weight, states).astype(BF16)
    teacher_proj = teacher_proj.reshape(2, HEADS, THD, LEN)

    if plan.special:
        tail_part = tail_along_z(tail_part, 1)

    def more_words(state):
        sent, slot = token_slots(state[0])
        return state[0] + 1, add_rows(NN, slot, fetch(ask(sent)[0]), state[1])

    more_words = lax.while_loop(
        lambda state: state[0] < rounds, more_words, (jnp.int32(1), jnp.zeros((LEN, D), F32))
    )[1]
    tail_own = tail_in_plane(tail_part, n) if plan.special else [gather_tail(plan, tail_part)]


    ends = jnp.cumsum(sizes)
    passed = (order[:, None] >= ends[None, :]).astype(jnp.int32)
    sentence = jnp.sum(passed, axis=-1)
    within = order - jnp.sum(passed * sizes[None, :], axis=-1)
    valid = (sentence < sizes.shape[0] - 1).astype(jnp.int32)

    pick_sentence = jnp.sum(jnp.where(pos[:, None] == order[None, :], sentence[None, :], 0), 1)
    picked_any = jnp.sum((pos[:, None] == order[None, :]).astype(jnp.int32), axis=0) > 0
    columns = [within, types, sentence, valid, 1 - picked_any.astype(jnp.int32)]
    columns = jnp.stack(columns + [order] * 3, axis=1)
    pick_columns = jnp.stack([pos, pick_sentence], axis=1)

    tail_other = [swap(part, "head", 1, 2) for part in tail_own]
    back, tail_own, tail_other, block_first, teacher_proj, columns, pick_columns = (
        lax.optimization_barrier(
            (back, tail_own, tail_other, block_first, teacher_proj, columns, pick_columns)
        )
    )
    mentor_first = send_mentor(block_first)

    shape = jax.ShapeDtypeStruct
    attn_in, attn_out, ffn_in, ffn_out, shared_half, _, _, chosen_own, *saved = call(
        functools.partial(forward_kernel, plan),
        piece_shapes(plan)
        + [
            shape((n, masks, D), BF16),
            shape((LEN, D), F32),
            shape((LEN, 1), F32),
            shape((3, HEADS, HP, LEN), BF16),
            shape((HEADS, masks, LEN), F32),
            shape((m, masks, plan.width // HD * HP), BF16),
            shape((masks, D), F32),
            shape((masks, 1), F32),
            shape((masks, D), BF16),
            shape((m, masks, plan.units), F32),
            shape((m, masks, plan.units), BF16),
            shape((masks, D), F32),
            shape((masks, 1), F32),
        ],
        place,
        *tail_own,
        *tail_other,
        back,
        more_words,
        slot_col,
        columns,
        pick_columns,
        sentence[None],
        scratch=[pltpu.VMEM((SROWS, D), F32)] + piece_scratch(plan),
        smem=1,
    )
    proj = saved[2]

    chosen_own, mentor_first = lax.optimization_barrier((chosen_own, mentor_first))
    gap = call(
        pick_gap_kernel,
        shape((HEADS, masks, LEN), F32),
        jnp.array([sizes.shape[0] - 1], jnp.int32),
        teacher_proj,
        saved[3],
        pick_columns,
        sentence[None],
        smem=1,
    )
    chosen = lax.all_to_all(chosen_own, "dp", 0, 0, tiled=False)
    chosen, gap = lax.optimization_barrier((chosen, gap))
    halves = [
        map_attention(first, HEADS // 2, proj, teacher_proj, columns, sentence[None])
        for first in (0, HEADS // 2)
    ]
    chosen = join_heads(chosen, h, m)
    chosen = jnp.swapaxes(chosen, 0, 1).reshape(picks, D)
    chosen, block_second = lax.optimization_barrier((chosen, block_second))
    mentor_second = send_mentor(block_second)
    student = logits_stats(plan, place, chosen, words_own)
    nothing = jnp.concatenate([jnp.full((1, picks), -1e30, F32), jnp.zeros((1, picks), F32)])
    at = (0, d * m * masks)
    mentor_all = lax.dynamic_update_slice(nothing, mentor_stats[:2, : m * masks], at)
    stats = jnp.concatenate([student[:1], mentor_all[:1], student[1:2], mentor_all[1:]])
    stats, halves[0] = merge_stats(stats, halves[0], plan)
    mentor_here = [mentor_first, mentor_second]
    grad_logits, own_pull, other_pull, losses = grad_logits_call(
        plan, place, chosen, words_own, mentor_here, stats
    )
    map_rows = halves[0][2] + halves[1][2]
    loss_local = jnp.sum(map_rows) + losses[1, 0] / devices - losses[0, 0]
    mine = own_pull + swap(other_pull, "head", 1, 2).astype(F32)
    grad_pick = jnp.sum(
        lax.all_to_all(mine.astype(BF16), "dp", 0, 0, tiled=False).astype(F32), axis=0
    )

    *piece_grads, word_grads, slot_grads = call(
        backward_kernel,
        [
            shape((m, 3, D, plan.width), F32),
            shape((m, plan.width, D), F32),
            shape((m, D, plan.units), F32),
            shape((m, plan.units, D), F32),
            shape((m, SROWS, plan.width), F32),
            shape((m, 2, plan.width), F32),
            shape((m, 1, plan.units), F32),
            shape((LEN, D), BF16),
            shape((devices * slots, D), BF16),
        ],
        grad_pick,
        slot_col,
        columns,
        pick_columns,
        pos[None],
        attn_in,
        attn_out,
        ffn_in,
        ffn_out,
        shared_half,
        *saved,
        gap,
        *halves[0][:2],
        *halves[1][:2],
        scratch=[
            pltpu.VMEM((SROWS - LEN, D), F32),
            pltpu.VMEM((3, HEADS * HP, LEN), BF16),
            pltpu.VMEM((m, plan.width // HD * HP, D), BF16),
        ],
    )

    def give(slot_grads):
        return lax.all_to_all(
            slot_grads.reshape(devices, slots, D), BOTH, 0, 0, tiled=True
        ).reshape(-1, D)

    def more_grads(state):
        sent, slot = token_slots(state[0])
        asked = own_index(ask(sent)[0])[:, None]
        hot = one_hot(slot[:, 0], devices * slots)
        got = give(dot("ts,td->sd", hot, word_grads).astype(BF16))
        return state[0] + 1, add_rows(TN, asked, got, state[1])

    given = give(slot_grads)
    tail_sent = pack_tail(plan, 1 - h, piece_grads)
    tail = pack_tail(plan, h, piece_grads, swap(tail_sent, "head", 1, 2))
    grad_table = call(
        rows_grad_kernel, jax.ShapeDtypeStruct((plan.rows, D), F32), grad_logits, chosen
    )
    tail, given, grad_table = lax.optimization_barrier((tail, given, grad_table))
    if plan.special:
        tail = lax.all_to_all(tail, "dp", 0, 0, tiled=False)

    grad_table = lax.while_loop(
        lambda state: state[0] < rounds, more_grads, (jnp.int32(1), grad_table)
    )[1]
    table_lines = table_pack(plan, place, own_index(asked_first), given, grad_table)
    before = lax.ppermute(table_lines[share:], "dp", [(i, i + 1) for i in range(n - 1)])

    tail, table_lines, loss_local = lax.optimization_barrier((tail, table_lines, loss_local))
    gradient, numbers = merge(
        plan, place, loss_local.reshape(1), table_lines, before, reduce_tail(plan, tail)
    )

    numbers = numbers + swap(numbers, "head", 1, 2)
    totals = gather_to_all(numbers, plan)
    vector_start = plan.table + plan.width * D * 4 + 2 * D * plan.units + (LEN + 2) * plan.width
    lines = jax.ShapeDtypeStruct((share, 1, LANES), F32)
    *updated, norm, loss_sum = call(
        functools.partial(adam_kernel, plan, vector_start),
        [lines, lines, lines] + [jax.ShapeDtypeStruct((1,), F32)] * 2,
        place,
        totals,
        chunk,
        gradient,
        first_moment.reshape(share, 1, LANES),
        second_moment.reshape(share, 1, LANES),
        scratch=[pltpu.VMEM((share, LANES), F32)] * 7 + [pltpu.SemaphoreType.DMA((7, 4))],
        smem=1,
        hbm=(2, 3, 4, 5),
        hbm_out=(0, 1, 2),
        smem_out=(3, 4),
    )
    updated = [value.reshape(1, share_len) for value in updated]
    weights = call(round_kernel, jax.ShapeDtypeStruct((1, share_len), BF16), updated[0])
    return (loss_sum.reshape(()), norm.reshape(()), *updated, weights)


def solution(mesh):
    return jax.shard_map(
        local,
        mesh=mesh,
        in_specs=(
            P("head", "dp"),
            P("head", "dp"),
            P("head", "dp"),
            P("dp", None),
            P("dp", None),
            P("dp", None),
            P("dp", None),
            P("dp", None, None),
            P(None, None, "head"),
            P("dp", None, "head"),
        ),
        out_specs=(P(), P(), P("head", "dp"), P("head", "dp"), P("head", "dp"), P("head", "dp")),
        check_vma=False,
    )
```

```python
import functools

import jax
import jax.numpy as jnp
from jax import lax
from jax.experimental import pallas as pl
from jax.experimental.pallas import tpu as pltpu
from jax.sharding import PartitionSpec as P

D = 312
HEADS = 12
HD = 26
HP = 32
FF = 1200
VOCAB = 30522
THD = 64
LEN = 512
STEP = 10
SROWS = 522

ATT_WEIGHT = 1.0
SOFTEN_FACTOR = 2.0
CLIP_NORM = 1.0
BETA_ONE = 0.9
BETA_TWO = 0.999
RATE_MATRIX = 0.06
RATE_VECTOR = 0.6
WEIGHT_DECAY = 0.01
ADAM_EPS = 1e-08
NORM_EPS = 1e-12
MASKED = -1000000000.0

F32 = jnp.float32
BF16 = jnp.bfloat16
LANES = 128
BOTH = ("dp", "head")
VMEM_BYTES = 56 * 1024 * 1024


def ceil_to(value, unit):
    return -(-value // unit) * unit


def call(kernel, out_shape, *args, scratch=(), smem=0, hbm=(), hbm_out=(), smem_out=()):
    space = lambda index: pltpu.SMEM if index < smem else pl.ANY if index in hbm else pltpu.VMEM
    in_specs = [pl.BlockSpec(memory_space=space(index)) for index in range(len(args))]
    outs = out_shape if isinstance(out_shape, list) else [out_shape]
    out_specs = [
        pl.BlockSpec(
            memory_space=pl.ANY
            if index in hbm_out
            else pltpu.SMEM
            if index in smem_out
            else pltpu.VMEM
        )
        for index in range(len(outs))
    ]
    out_specs = out_specs if isinstance(out_shape, list) else out_specs[0]
    return pl.pallas_call(
        kernel,
        out_shape=out_shape,
        in_specs=in_specs,
        out_specs=out_specs,
        scratch_shapes=list(scratch),
        compiler_params=pltpu.CompilerParams(vmem_limit_bytes=VMEM_BYTES),
    )(*args)


class Plan:
    def __init__(self, n, m, share):
        self.n, self.m, self.share = n, m, share
        self.rows_share = share // LANES
        self.vocab = VOCAB // m
        self.width = D // m
        self.units = FF // m
        self.first = [min(-(-d * share // D), self.vocab) for d in range(n + 1)]
        widest = -(-share // D)
        self.rows = ceil_to(widest + 3, 16)
        table = self.vocab * D
        self.table = table
        self.tail_row = table // LANES
        self.tail_off = table % LANES
        self.tail_rows = n * self.rows_share - self.tail_row
        self.tail_pad = ceil_to(self.tail_rows + 40, 16)
        w, u = self.width, self.units
        self.pieces = []
        base = self.tail_off
        for rows, wide in ((3 * D, w), (w, D), (D, u), (u, D), (SROWS, w), (2, w), (1, u)):
            self.pieces.append((base, wide, rows))
            base += rows * wide
        self.special = n == 16 and self.tail_row // self.rows_share == n - 2
        if self.special:
            self.low_rows = (n - 1) * self.rows_share - self.tail_row
            self.slice_rows = ceil_to(-(-self.rows_share // 8), 16)
            self.half_rows = 4 * self.slice_rows


def period(width):
    step = 16
    while step * width % LANES:
        step *= 2
    return step, step * width // LANES


def rows_at(start, count, stride):
    return pl.ds(start, count) if count == 1 else pl.ds(start, count, stride=stride)


def spread_rows(src, dst, base, width, rows):
    step, lane_rows = period(width)
    tiles = -(-width // LANES)
    for phase in range(min(step, rows)):
        count = len(range(phase, rows, step))
        line, off = divmod(base + phase * width, LANES)
        loaded = [
            src[rows_at(line + j, count, lane_rows), :] for j in range(tiles + (1 if off else 0))
        ]
        lane = lax.broadcasted_iota(jnp.int32, (count, LANES), 1)
        for tile in range(tiles):
            value = loaded[tile]
            if off:
                value = jnp.where(
                    lane < LANES - off,
                    pltpu.roll(value, LANES - off, 1),
                    pltpu.roll(loaded[tile + 1], LANES - off, 1),
                )
            dst[tile, rows_at(phase, count, step), :] = value


def pack_rows(src, dst, base, width, rows):
    step, lane_rows = period(width)
    tiles = -(-width // LANES)
    for phase in range(min(step, rows)):
        count = len(range(phase, rows, step))
        line, off = divmod(base + phase * width, LANES)
        loaded = [
            src[tile, rows_at(phase, count, step), :] for tile in range(tiles)
        ]
        lane = lax.broadcasted_iota(jnp.int32, (count, LANES), 1)
        rolled = [pltpu.roll(value, off, 1) if off else value for value in loaded]
        for j in range(-(-(off + width) // LANES)):
            value = jnp.zeros((count, LANES), F32)
            if j < tiles:
                value = jnp.where(lane >= off, rolled[j], value)
            if off and j > 0:
                value = jnp.where(lane < off, rolled[j - 1], value)
            at = rows_at(line + j, count, lane_rows)
            dst[at, :] = dst[at, :] + value


def column_tiles(width):
    return [(t, t * LANES, min(LANES, width - t * LANES)) for t in range(-(-width // LANES))]


def shift_lines(source, count, start, max_line):
    low, high = start // LANES, lax.rem(start, LANES)
    first = source[0:count, :]
    second = source[1 : count + 1, :]
    for line in range(1, max_line + 1):
        first = jnp.where(low == line, source[line : count + line, :], first)
        second = jnp.where(low == line, source[line + 1 : count + line + 1, :], second)
    lane = lax.broadcasted_iota(jnp.int32, (count, LANES), 1)
    back = lax.rem(LANES - high, LANES)
    return jnp.where(lane < LANES - high, pltpu.roll(first, back, 1), pltpu.roll(second, back, 1))


def bring(source, target, sem):
    copy = pltpu.make_async_copy(source, target, sem)
    copy.start()
    copy.wait()


def share_rows_kernel(plan, place, chunk, out, lines, sem):
    share, low = plan.rows_share, plan.low_rows
    lines[share & -8 :, :] = jnp.zeros((lines.shape[0] - (share & -8), LANES), F32)
    bring(chunk.at[:, 0, :], lines.at[0:share], sem)
    count = out.shape[0]
    begins_late = place[2] == plan.n - 2
    first = share - low
    out[...] = jnp.where(
        begins_late, lines[first : first + count, :], lines[0:count, :]
    ).astype(BF16)


def share_rows(plan, place, chunk):
    count = 8 * plan.slice_rows
    return call(
        functools.partial(share_rows_kernel, plan),
        jax.ShapeDtypeStruct((count, LANES), BF16),
        place,
        chunk,
        scratch=[
            pltpu.VMEM((ceil_to(count + plan.rows_share - plan.low_rows, 8), LANES), F32),
            pltpu.SemaphoreType.DMA,
        ],
        smem=1,
        hbm=(1,),
    )


def table_rows_kernel(plan, place, chunk, after, out, joined, shifted, rows, sem):
    share = plan.rows_share
    lines = joined.shape[0]
    joined[share & -8 :, :] = jnp.zeros((lines - (share & -8), LANES), F32)
    bring(chunk.at[:, 0, :], joined.at[0:share], sem)
    joined[share : share + 8, :] = after[...]
    shifted[...] = jnp.zeros_like(shifted)
    shifted[0 : share + 2, :] = shift_lines(joined, share + 2, place[0], 2)
    spread_rows(shifted, rows, 0, D, plan.rows)
    row = lax.broadcasted_iota(jnp.int32, (plan.rows, LANES), 0)
    for tile, left, wide in column_tiles(D):
        value = jnp.where(row < place[1], rows[tile], 0.0).astype(BF16)
        out[:, left : left + wide] = value[:, 0:wide]


def table_rows(plan, place, chunk, after):
    lines = ceil_to(max(plan.rows_share + 16, plan.rows // 16 * 39 + 2), 8)
    return call(
        functools.partial(table_rows_kernel, plan),
        jax.ShapeDtypeStruct((plan.rows, D), BF16),
        place,
        chunk,
        after,
        scratch=[
            pltpu.VMEM((lines, LANES), F32),
            pltpu.VMEM((lines, LANES), F32),
            pltpu.VMEM((3, plan.rows, LANES), F32),
            pltpu.SemaphoreType.DMA,
        ],
        smem=1,
        hbm=(1,),
    )


def table_pack_kernel(plan, place, index, given, grads, out, rows, lines):
    total = grads[...] + mm(hot_rows(index[...], plan.rows), given[...], TN)
    rows[...] = jnp.zeros_like(rows)
    for tile, left, wide in column_tiles(D):
        rows[tile, 16 : 16 + plan.rows, 0:wide] = total[:, left : left + wide]
    lines[...] = jnp.zeros_like(lines)
    pack_rows(rows, lines, 0, D, plan.rows + 16)
    count = plan.rows_share + 8
    start = 39 * LANES - place[0]
    low, high = start // LANES - 36, lax.rem(start, LANES)
    first = lines[36 : 36 + count, :]
    second = lines[37 : 37 + count, :]
    for line in range(1, 4):
        first = jnp.where(low == line, lines[36 + line : 36 + line + count, :], first)
        second = jnp.where(low == line, lines[37 + line : 37 + line + count, :], second)
    lane = lax.broadcasted_iota(jnp.int32, (count, LANES), 1)
    back = lax.rem(LANES - high, LANES)
    value = jnp.where(
        lane < LANES - high, pltpu.roll(first, back, 1), pltpu.roll(second, back, 1)
    )
    line = lax.broadcasted_iota(jnp.int32, (count, LANES), 0)
    index = (line + place[2] * plan.rows_share) * LANES + lane
    out[...] = jnp.where(index < plan.table, value, 0.0)


def merge_kernel(plan, place, loss, table, before, *refs):
    extra, (out, numbers, whole, sem) = refs[:-4], refs[-4:]
    size = plan.slice_rows if plan.special else plan.rows_share
    share = plan.rows_share
    whole[...] = table[0:share, :]
    whole[0:8, :] = whole[0:8, :] + before[...]
    if plan.special:
        d, low = place[2], plan.low_rows
        for owner, first, count in ((plan.n - 2, share - low, low), (plan.n - 1, 0, share)):

            @pl.when(d == owner)
            def _(first=first, count=count):
                for index, part in enumerate(extra):
                    begin = first + index * size
                    end = min(begin + size, first + count)
                    whole[begin:end, :] = whole[begin:end, :] + part[0 : end - begin, :]

    else:
        whole[...] = whole[...] + extra[0][...]
    copy = pltpu.make_async_copy(whole, out.at[:, 0, :], sem)
    copy.start()
    value = whole[...]
    squares = jnp.sum(jnp.sum(value * value, axis=0, keepdims=True), axis=1, keepdims=True)
    line = lax.broadcasted_iota(jnp.int32, (8, LANES), 0)
    numbers[...] = jnp.where(
        line == 0, jnp.broadcast_to(squares, (8, LANES)), jnp.where(line == 1, loss[0], 0.0)
    )
    copy.wait()


def merge(plan, place, loss, table, before, extra):
    return call(
        functools.partial(merge_kernel, plan),
        [
            jax.ShapeDtypeStruct((plan.rows_share, 1, LANES), F32),
            jax.ShapeDtypeStruct((8, LANES), F32),
        ],
        place,
        loss,
        table,
        before,
        *extra,
        scratch=[pltpu.VMEM((plan.rows_share, LANES), F32), pltpu.SemaphoreType.DMA],
        smem=2,
        hbm_out=(0,),
    )


def adam_kernel(plan, edge, place, totals, *refs):
    ins, outs, refs = refs[:4], refs[4:7], refs[7:]
    norm_out, loss_out, held, sems = refs[0], refs[1], refs[2:9], refs[9]
    share, parts = plan.rows_share, sems.shape[1]
    size = ceil_to(-(-share // parts), 8)
    spans = [(part * size, min(size, share - part * size)) for part in range(parts)]

    def copies(part, arrays, scratch, first, outward):
        begin, count = spans[part]
        made = []
        for index, (array, kept) in enumerate(zip(arrays, scratch)):
            near = kept.at[pl.ds(begin, count)]
            far = array.at[pl.ds(begin, count), 0, :]
            pair = (near, far) if outward else (far, near)
            made.append(pltpu.make_async_copy(*pair, sems.at[first + index, part]))
        for copy in made:
            copy.start()
        return made

    coming = [copies(part, ins, held[:4], 0, False) for part in range(parts)]
    total = jnp.sum(totals[...], axis=0)
    norm = jnp.sqrt(total[0:1, :])
    norm_out[0] = jnp.max(norm)
    loss_out[0] = jnp.max(total[1:2, :])
    scale = CLIP_NORM / jnp.maximum(norm, CLIP_NORM)
    going = []
    for part in range(parts):
        begin, count = spans[part]
        for copy in coming[part]:
            copy.wait()
        at = slice(begin, begin + count)
        master, gradient, first, second = (kept[at, :] for kept in held[:4])
        clipped = gradient * scale
        moment = BETA_ONE * first + (1.0 - BETA_ONE) * clipped
        spread = BETA_TWO * second + (1.0 - BETA_TWO) * clipped * clipped
        step = (moment * (1.0 / (1.0 - BETA_ONE**STEP))) / (
            jnp.sqrt(spread * (1.0 / (1.0 - BETA_TWO**STEP))) + ADAM_EPS
        )
        lines = lax.broadcasted_iota(jnp.int32, (count, LANES), 0) + begin
        lane = lax.broadcasted_iota(jnp.int32, (count, LANES), 1)
        matrix_part = (lines + place[2] * share) * LANES + lane < edge
        rate = jnp.where(matrix_part, RATE_MATRIX, RATE_VECTOR)
        decay = jnp.where(matrix_part, WEIGHT_DECAY, 0.0)
        held[4][at, :] = master - rate * (step + decay * master)
        held[5][at, :] = moment
        held[6][at, :] = spread
        going.append(copies(part, outs, held[4:], 4, True))
    for made in going:
        for copy in made:
            copy.wait()


def round_kernel(value, out):
    out[...] = value[...].astype(BF16)


def mentor_kernel(plan, room, cuts, mentor, *refs):
    outs, stats = refs[:-1], refs[-1]
    m, masks, vocab = mentor.shape
    wide = 16 * LANES
    columns = []
    for part in range(m):
        pieces = [
            mentor[part, :, left : min(left + wide, vocab)].astype(F32) * (1.0 / SOFTEN_FACTOR)
            for left in range(0, vocab, wide)
        ]
        top = pieces[0]
        for piece in pieces[1:-1]:
            top = jnp.maximum(top, piece)
        top = jnp.maximum(
            jnp.max(top, axis=-1, keepdims=True), jnp.max(pieces[-1], axis=-1, keepdims=True)
        )
        total = jnp.exp(pieces[0] - top)
        for piece in pieces[1:-1]:
            total = total + jnp.exp(piece - top)
        total = jnp.sum(total, axis=-1, keepdims=True) + jnp.sum(
            jnp.exp(pieces[-1] - top), axis=-1, keepdims=True
        )
        columns.append((top, total))
    lane = lax.broadcasted_iota(jnp.int32, (m * masks, LANES), 1)
    top, total = (jnp.concatenate([column[k] for column in columns]) for k in range(2))
    both = jnp.where(lane == 0, top, jnp.where(lane == 1, total, 0.0))
    both = jnp.concatenate([both, jnp.zeros((LANES - m * masks, LANES), F32)])
    stats[...] = jnp.transpose(both)[0:8, :]
    for owner in range(plan.n):
        low = plan.first[owner]
        high = min(low + room, vocab)
        if high <= low:
            for out in outs:
                out[owner] = jnp.zeros(out.shape[1:], BF16)
            continue
        left = low // LANES * LANES
        right = min(ceil_to(high, LANES), vocab)
        for part in range(m):
            value = mentor[part, :, left:right].astype(F32)
            value = jnp.pad(value, ((0, 0), (0, ceil_to(high, LANES) + LANES - right)))
            if low > left:
                value = pltpu.roll(value, value.shape[1] - (low - left), 1)
            if high - low < room:
                value = jnp.pad(value[:, : high - low], ((0, 0), (0, room - (high - low))))
            value = value[:, 0:room].astype(BF16)
            for out, start in zip(outs, cuts):
                first = max(start, part * masks)
                last = min(start + out.shape[1], (part + 1) * masks)
                if first < last:
                    out[owner, first - start : last - start, :] = value[
                        first - part * masks : last - part * masks, :
                    ]


def table_pack(plan, place, index, given, grads):
    lines = ceil_to(max(plan.rows_share + 48, (plan.rows // 16 + 1) * 39 + 2), 8)
    return call(
        functools.partial(table_pack_kernel, plan),
        jax.ShapeDtypeStruct((plan.rows_share + 8, LANES), F32),
        place,
        index[:, None],
        given,
        grads,
        scratch=[
            pltpu.VMEM((3, plan.rows + 16, LANES), F32),
            pltpu.VMEM((lines, LANES), F32),
        ],
        smem=1,
    )


def unpack(plan, place, own, other, outs, lines, wide):
    share = plan.rows_share

    def load(tails):
        if not plan.special:
            lines[...] = tails[0][...].astype(F32)
            return
        half = plan.half_rows
        for quarter in range(4):
            y, x = divmod(quarter, 2)
            first = y * half
            end = min(first + half, share if x else plan.low_rows)
            at = first + (plan.low_rows if x else 0)
            size = half // CHUNKS
            for k in range(4):

                @pl.when(lax.rem(place[2], 4) == quarter ^ k)
                def _(k=k, at=at, length=end - first):
                    for chunk in range(CHUNKS):
                        rows = min(size, length - chunk * size)
                        lines[at + chunk * size : at + chunk * size + rows, :] = tails[
                            4 * chunk + k
                        ][...].astype(F32)[0:rows]

    for head in range(plan.m):
        mine = place[3] == head
        pl.when(mine)(lambda: load(own))
        pl.when(jnp.logical_not(mine))(lambda: load(other))
        for out, (base, width, rows) in zip(outs, plan.pieces):
            spread_rows(lines, wide, base, width, rows)
            for tile, left, part in column_tiles(width):
                if len(out.shape) == 4:
                    for kind in range(3):
                        value = wide[tile, kind * D : (kind + 1) * D, 0:part]
                        out[head, kind, :, left : left + part] = value.astype(BF16)
                else:
                    out[head, :, left : left + part] = wide[tile, 0:rows, 0:part].astype(BF16)


def piece_shapes(plan):
    shapes = [jax.ShapeDtypeStruct((plan.m, rows, width), BF16) for _, width, rows in plan.pieces]
    shapes[0] = jax.ShapeDtypeStruct((plan.m, 3, D, plan.width), BF16)
    return shapes


def piece_scratch(plan):
    tallest = max(rows for _, _, rows in plan.pieces)
    widest = max(-(-width // LANES) for _, width, _ in plan.pieces)
    return [pltpu.VMEM((plan.tail_pad, LANES), F32), pltpu.VMEM((widest, tallest, LANES), F32)]


def pack_kernel(plan, part_index, *refs):
    folding = plan.special and len(refs) == len(plan.pieces) + 4
    ins, refs = refs[: len(plan.pieces)], refs[len(plan.pieces) :]
    out, lines, wide = refs[-3:]
    lines[...] = refs[0][...] if len(refs) == 4 else jnp.zeros_like(lines)
    for source, (base, width, rows) in zip(ins, plan.pieces):
        for tile, left, part in column_tiles(width):
            if part < LANES:
                wide[tile, 0:rows, :] = jnp.zeros((rows, LANES), F32)
            if len(source.shape) == 4:
                for kind in range(3):
                    wide[tile, kind * D : (kind + 1) * D, 0:part] = source[
                        0, kind, :, left : left + part
                    ]
            else:
                wide[tile, 0:rows, 0:part] = source[0, :, left : left + part]
        pack_rows(wide, lines, base, width, rows)
    if not folding:
        out[...] = lines[...]
        return
    size, low, share = plan.slice_rows, plan.low_rows, plan.rows_share
    for index in range(8):
        for side, base, end in ((0, 0, low), (1, low, low + share)):
            first = base + index * size
            count = min(size, end - first)
            value = jnp.pad(lines[first : first + count, :], ((0, size - count), (0, 0)))
            out[2 * index + side] = value.astype(BF16)


def pack_tail(plan, part, pieces, *added):
    def chosen_block(value):
        rest = value.shape[1:]
        return pl.BlockSpec((1,) + rest, lambda i, part: (part[0],) + (0,) * len(rest))

    shape = jax.ShapeDtypeStruct((plan.tail_pad, LANES), F32)
    if plan.special and added:
        shape = jax.ShapeDtypeStruct((plan.n, plan.slice_rows, LANES), BF16)
    zeros = (0,) * len(shape.shape)
    return pl.pallas_call(
        functools.partial(pack_kernel, plan),
        out_shape=shape,
        grid_spec=pltpu.PrefetchScalarGridSpec(
            num_scalar_prefetch=1,
            grid=(1,),
            in_specs=[chosen_block(piece) for piece in pieces]
            + [pl.BlockSpec((plan.tail_pad, LANES), lambda i, part: (0, 0)) for _ in added],
            out_specs=pl.BlockSpec(shape.shape, lambda i, part: zeros),
            scratch_shapes=piece_scratch(plan),
        ),
        compiler_params=pltpu.CompilerParams(vmem_limit_bytes=VMEM_BYTES),
    )(part.reshape(1).astype(jnp.int32), *pieces, *added)


def slots_kernel(plan, slots, turn, ids, sent, slot_col):
    vocab, m = plan.vocab, plan.m

    def parts(value):
        head = jnp.zeros(value.shape, jnp.int32)
        for index in range(1, m):
            head = head + jnp.where(value >= index * vocab, 1, 0)
        row = value - head * vocab
        owner = jnp.zeros(value.shape, jnp.int32)
        for first in plan.first[1 : plan.n]:
            owner = owner + jnp.where(row >= first, 1, 0)
        return row, owner * m + head

    ids_row = ids[0:1, :]
    ids_col = jnp.transpose(jnp.broadcast_to(ids_row.astype(F32), (LANES, LEN)))[:, 0:1]
    ids_col = ids_col.astype(jnp.int32)
    row_row, owner_row = parts(ids_row)
    row_col, owner_col = parts(ids_col)
    same = ids_col == ids_row
    along = lax.broadcasted_iota(jnp.int32, (LEN, LEN), 1)
    down = lax.broadcasted_iota(jnp.int32, (LEN, LEN), 0)
    leader = jnp.min(jnp.where(same, along, LEN).astype(F32), axis=1, keepdims=True)
    lead_row = jnp.min(jnp.where(same, down, LEN).astype(F32), axis=0, keepdims=True)
    leads = lead_row == along[0:1, :].astype(F32)
    ahead = (owner_col == owner_row) & leads & (along.astype(F32) < leader)
    rank = jnp.sum(jnp.where(ahead, 1.0, 0.0), axis=1, keepdims=True).astype(jnp.int32)
    place = rank - turn[0] * slots
    slot = jnp.where((place >= 0) & (place < slots), owner_col * slots + place, -1)
    slot_col[...] = slot
    lane = lax.broadcasted_iota(jnp.int32, (LEN, LANES), 1)
    most = jnp.max(jnp.max(rank.astype(F32), axis=0, keepdims=True), axis=1, keepdims=True)
    needed = jnp.ones((1, 1), F32)
    for turn in range(1, LEN // slots):
        needed = needed + jnp.where(most >= turn * slots, 1.0, 0.0)
    lane_row = lax.broadcasted_iota(jnp.int32, (1, LANES), 1)
    inside = jnp.where(lane < slots, lane, -LEN * LEN)
    row_value = row_col.astype(F32)
    for device in range(sent.shape[0]):
        hit = slot - device * slots == inside
        asked = jnp.max(jnp.where(hit, row_value, -1.0), axis=0, keepdims=True)
        asked = jnp.where(lane_row == slots, needed, asked)
        sent[device : device + 1, :] = asked.astype(jnp.int32)


def add_rows_kernel(over, index, rows, total, out):
    size = rows.shape[0] if over == NN else out.shape[0]
    out[...] = total[...] + mm(hot_rows(index[...], size), rows[...], over)


def add_rows(over, index, rows, total):
    return call(
        functools.partial(add_rows_kernel, over),
        jax.ShapeDtypeStruct(total.shape, F32),
        index,
        rows,
        total,
    )


def rows_grad_kernel(grads, chosen, out):
    out[...] = mm(grads[...], chosen[...], TN)


def swap(value, axis, bit, size):
    return lax.ppermute(value, axis, [(i, i ^ bit) for i in range(size)])


def gather_to_all(value, plan):
    return lax.all_to_all(
        jnp.broadcast_to(value[None], (plan.n,) + value.shape), "dp", 0, 0, tiled=False
    )


def join_heads(value, head, m):
    if m != 2:
        return lax.all_gather(value, "head", axis=0, tiled=False)
    other = swap(value, "head", 1, m)
    mine_first = head == 0
    return jnp.stack([jnp.where(mine_first, value, other), jnp.where(mine_first, other, value)])


CHUNKS = 1


def tail_to_plane(plan, own):
    half = plan.half_rows
    size = half // CHUNKS
    d = lax.axis_index("dp")
    parts = []
    for first in range(0, half, size):
        part = lax.ppermute(own[first : first + size], "dp", [(14, 12), (15, 13)])
        parts.append(jnp.where(d >= 14, own[half + first : half + first + size], part))
    return parts


def tail_along_z(parts, step):
    pairs = [[(12, 4)], [(12, 8), (4, 0)]][step]
    perm = [(a + p, b + p) for a, b in pairs for p in range(4)]
    z = lax.axis_index("dp") // 4
    here = z == 1 if step == 0 else (z == 0) | (z == 2)
    return [jnp.where(here, lax.ppermute(part, "dp", perm), part) for part in parts]


def tail_in_plane(parts, n):
    return [one for part in parts for one in [part] + [swap(part, "dp", k, n) for k in (1, 2, 3)]]


def merge_stats(value, beside, plan):
    steps = [("head", 1 << bit, plan.m) for bit in range(plan.m.bit_length() - 1)]
    steps += [("dp", 1 << bit, plan.n) for bit in range(plan.n.bit_length() - 1)]
    for index, (axis, bit, size) in enumerate(steps):
        if index == 3:
            value, beside = lax.optimization_barrier((value, beside))
        other = swap(value, axis, bit, size)
        top = jnp.maximum(value[:2], other[:2])
        total = value[2:] * jnp.exp(value[:2] - top) + other[2:] * jnp.exp(other[:2] - top)
        value = jnp.concatenate([top, total])
    return value, beside


def gather_tail(plan, value):
    whole = lax.all_gather(value, "dp", axis=0, tiled=True)
    return jnp.pad(whole[plan.tail_row :], ((0, plan.tail_pad - plan.tail_rows), (0, 0)))


def reduce_tail(plan, tail):
    n, share = plan.n, plan.rows_share
    if not plan.special:
        total = lax.psum(tail, "dp")
        front = jnp.zeros((share, LANES), F32)
        start = lax.axis_index("dp") * share - plan.tail_row + share
        start = jnp.clip(start, 0, plan.tail_pad)
        padded = jnp.concatenate([front, total[: plan.tail_rows], front])
        return [lax.dynamic_slice_in_dim(padded, start, share)]
    mine = jnp.sum(tail.astype(F32), axis=0)
    whole = []
    for k in range(7):
        whole.append(lax.ppermute(mine, "dp", [(2 * k, n - 2), (2 * k + 1, n - 1)]))
    return whole + [mine]


def attention_kernel(proj, teacher, columns, sent_row, grad_q, grad_k, loss):
    @pl.when(pl.program_id(0) == 0)
    def _():
        loss[...] = jnp.zeros_like(loss)

    allowed = columns[:, 2:3] == sent_row[...]
    weight = columns[:, 3:4].astype(F32)
    plain = columns[:, 4:5].astype(F32)

    def probs(queries, key_heads, scale):
        scores = lax.dot_general(
            queries, key_heads, (((0,), (0,)), ((), ())), preferred_element_type=F32
        )
        scores = jnp.where(allowed, scores * scale, MASKED)
        exponent = jnp.exp(scores - jnp.max(scores, axis=-1, keepdims=True))
        return exponent * (1.0 / jnp.sum(exponent, axis=-1, keepdims=True))

    teacher_prob = probs(teacher[0, 0], teacher[1, 0], THD ** (-0.5))
    queries, key_heads = proj[0, 0], proj[1, 0]
    prob = probs(queries, key_heads, HD ** (-0.5))
    gap = (prob - teacher_prob) * weight
    loss[...] += jnp.sum(gap * gap, axis=0, keepdims=True) * ATT_WEIGHT
    pulled = prob * gap
    inner = jnp.sum(pulled, axis=-1, keepdims=True)
    grad_scores = (
        (pulled - prob * inner) * (plain * (2.0 * ATT_WEIGHT))
    ).astype(BF16)
    grad_q[0] = lax.dot_general(
        key_heads, grad_scores, (((1,), (1,)), ((), ())), preferred_element_type=F32
    )
    grad_k[0] = lax.dot_general(
        queries, grad_scores, (((1,), (0,)), ((), ())), preferred_element_type=F32
    )


def map_attention(first, heads, proj, teacher, columns, sent_row):
    whole = lambda i: (0, 0)
    return pl.pallas_call(
        attention_kernel,
        out_shape=[
            jax.ShapeDtypeStruct((heads, HP, LEN), F32),
            jax.ShapeDtypeStruct((heads, HP, LEN), F32),
            jax.ShapeDtypeStruct((1, LEN), F32),
        ],
        grid=(heads,),
        in_specs=[
            pl.BlockSpec((3, 1, HP, LEN), lambda i: (0, first + i, 0, 0)),
            pl.BlockSpec((2, 1, THD, LEN), lambda i: (0, first + i, 0, 0)),
            pl.BlockSpec(columns.shape, whole),
            pl.BlockSpec((1, LEN), whole),
        ],
        out_specs=[
            pl.BlockSpec((1, HP, LEN), lambda i: (i, 0, 0)),
            pl.BlockSpec((1, HP, LEN), lambda i: (i, 0, 0)),
            pl.BlockSpec((1, LEN), whole),
        ],
        compiler_params=pltpu.CompilerParams(vmem_limit_bytes=VMEM_BYTES),
    )(proj, teacher, columns, sent_row)


def mm(left, right, over):
    return lax.dot_general(left, right, (over, ((), ())), preferred_element_type=F32)


NN, NT, TN = ((1,), (0,)), ((1,), (1,)), ((0,), (0,))


def exact(hot, value, over, parts=3):
    total = None
    for _ in range(parts):
        piece = value.astype(BF16)
        value = value - piece.astype(F32)
        term = mm(hot, piece, over)
        total = term if total is None else total + term
    return total


def head_spread(width, per_head):
    row = lax.broadcasted_iota(jnp.int32, (width, per_head * HP), 0)
    column = lax.broadcasted_iota(jnp.int32, (width, per_head * HP), 1)
    for head in range(1, per_head):
        column = column - jnp.where(row >= head * HD, HP - HD, 0)
    return jnp.where(row == column, 1.0, 0.0).astype(BF16)


def hot_rows(index, size):
    column = lax.broadcasted_iota(jnp.int32, (index.shape[0], size), 1)
    return jnp.where(index == column, 1.0, 0.0).astype(BF16)


def softmax_rows(scores, allowed):
    scores = jnp.where(allowed, scores, MASKED)
    exponent = jnp.exp(scores - jnp.max(scores, axis=-1, keepdims=True))
    return exponent * (1.0 / jnp.sum(exponent, axis=-1, keepdims=True))


def norm_pull(gradient, normed, inverse, gain_row):
    scaled = gradient * gain_row
    inner_part = (
        scaled
        - jnp.mean(scaled, -1, keepdims=True)
        - normed * jnp.mean(scaled * normed, -1, keepdims=True)
    )
    return (
        inner_part * inverse,
        jnp.sum(gradient * normed, 0, keepdims=True),
        jnp.sum(gradient, 0, keepdims=True),
    )


ROOT_HALF = 0.5**0.5
BELL = (2.0 * 3.141592653589793) ** -0.5


def forward_kernel(plan, place, *refs):
    tails = len(refs) - 29
    own, other, refs = refs[: tails // 2], refs[tails // 2 : tails], refs[tails:]
    back, more_words, slot_col, columns, pick_columns, sent_row, *refs = refs
    attn_in, attn_out, ffn_in, ffn_out, shared_half, qv_bias, up_bias = refs[:7]
    (
        chosen,
        normed_zero,
        inverse_zero,
        proj,
        prob,
        mixed,
        normed_one,
        inverse_one,
        state_low,
        pre_act,
        hidden_act,
        normed_two,
        inverse_two,
        shared,
        lines,
        wide_rows,
    ) = refs[7:]
    unpack(plan, place, own, other, refs[:7], lines, wide_rows)
    m, _, _, width = attn_in.shape
    per_head = width // HD
    for part in range(m):
        shared[:, part * width : (part + 1) * width] = shared_half[part].astype(F32)
    position_hot = hot_rows(columns[:, 0:1], LEN)
    state = mm(hot_rows(slot_col[...], back.shape[0]), back[...], NN) + more_words[...]
    state = state + mm(position_hot, shared[0:LEN, :].astype(BF16), NN)
    state = state + jnp.where(columns[:, 1:2] == 0, shared[LEN : LEN + 1, :], shared[LEN + 1 : LEN + 2, :])
    state, (normed, inverse) = norm_forward(
        state, shared[LEN + 2 : LEN + 3, :], shared[LEN + 3 : LEN + 4, :]
    )
    normed_zero[...] = normed
    inverse_zero[...] = inverse
    gathered = state.astype(BF16)
    base = LEN + 4
    row = lambda index: shared[base + index : base + index + 1, :]

    spread = head_spread(width, per_head)
    for part in range(m):
        for kind in range(3):
            wide = mm(attn_in[part, kind], spread, NN).astype(BF16)
            value = mm(wide, gathered, ((0,), (1,)))
            if kind != 1:
                bias_row = qv_bias[part, kind // 2 : kind // 2 + 1, :]
                bias = mm(spread, jnp.broadcast_to(bias_row, (8, width)), ((0,), (1,)))
                value = value + bias[:, 0:1]
            value = value.astype(BF16).reshape(per_head, HP, LEN)
            proj[kind, part * per_head : (part + 1) * per_head] = value

    pick_hot = hot_rows(pick_columns[:, 0:1], LEN)
    allowed = pick_columns[:, 1:2] == sent_row[...]
    masks = pick_columns.shape[0]
    branch = jnp.zeros((masks, D), F32)
    for part in range(m):
        wide_out = mm(spread, attn_out[part], TN).astype(BF16)
        for index in range(per_head):
            head = part * per_head + index
            query = mm(pick_hot, proj[0, head], NT).astype(BF16)
            value = softmax_rows(mm(query, proj[1, head], NN) * HD ** (-0.5), allowed)
            prob[head] = value
            mix = mm(value.astype(BF16), proj[2, head], NT).astype(BF16)
            mixed[part, :, index * HP : (index + 1) * HP] = mix
            branch = branch + mm(mix, wide_out[index * HP : (index + 1) * HP, :], NN)
    state_one, (normed, inverse) = norm_forward(
        exact(pick_hot, state, NN) + branch + row(4), row(0), row(1)
    )
    normed_one[...] = normed
    inverse_one[...] = inverse
    low = state_one.astype(BF16)
    state_low[...] = low
    branch = jnp.zeros((masks, D), F32)
    for part in range(m):
        pre = mm(low, ffn_in[part], NN) + up_bias[part].astype(F32)
        pre_act[part] = pre
        act = (0.5 * pre * (1.0 + lax.erf(pre * ROOT_HALF))).astype(BF16)
        hidden_act[part] = act
        branch = branch + mm(act, ffn_out[part], NN)
    state_two, (normed, inverse) = norm_forward(state_one + branch + row(5), row(2), row(3))
    normed_two[...] = normed
    inverse_two[...] = inverse
    low = state_two.astype(BF16)
    for index in range(chosen.shape[0]):
        chosen[index] = low


def pick_gap_kernel(last_sentence, teacher, prob, pick_columns, sent_row, out):
    pick_hot = hot_rows(pick_columns[:, 0:1], LEN)
    pick_sentence = pick_columns[:, 1:2]
    allowed = pick_sentence == sent_row[...]
    weight = jnp.where(pick_sentence < last_sentence[0], 2.0 * ATT_WEIGHT, 0.0)
    for head in range(prob.shape[0]):
        query = mm(pick_hot, teacher[0, head], NT).astype(BF16)
        value = softmax_rows(mm(query, teacher[1, head], NN) * THD ** (-0.5), allowed)
        out[head] = (prob[head] - value) * weight


def backward_kernel(
    grad_pick,
    slot_col,
    columns,
    pick_columns,
    pos_row,
    attn_in,
    attn_out,
    ffn_in,
    ffn_out,
    shared_half,
    normed_zero,
    inverse_zero,
    proj,
    prob,
    mixed,
    normed_one,
    inverse_one,
    state_low,
    pre_act,
    hidden_act,
    normed_two,
    inverse_two,
    gap,
    map_q_low,
    map_k_low,
    map_q_high,
    map_k_high,
    grad_attn_in,
    grad_attn_out,
    grad_ffn_in,
    grad_ffn_out,
    grad_shared,
    grad_qv,
    grad_up,
    word_grads,
    slot_grads,
    shared,
    grad_proj,
    wide_out,
):
    m, _, _, width = attn_in.shape
    per_head = width // HD
    pos = pick_columns[:, 0:1]
    masks = pos.shape[0]
    for part in range(m):
        shared[:, part * width : (part + 1) * width] = shared_half[part, LEN:, :].astype(F32)
    row = lambda index: shared[index : index + 1, :]
    spread = head_spread(width, per_head)
    score_scale = HD ** (-0.5)

    repeats = pos == pos_row[...]
    order = lax.broadcasted_iota(jnp.int32, (masks, masks), 1)
    lead = jnp.min(jnp.where(repeats, order, masks).astype(F32), axis=1, keepdims=True)
    leads = lead == lax.broadcasted_iota(jnp.int32, (masks, 1), 0).astype(F32)
    gradient = exact(jnp.where(repeats, 1.0, 0.0).astype(BF16), grad_pick[...], NN)
    gradient = jnp.where(leads, gradient, 0.0)

    grad_res, gain_two, bias_two = norm_pull(
        gradient, normed_two[...], inverse_two[...], row(6)
    )
    grad_branch = grad_res.astype(BF16)
    grad_one = grad_res
    for part in range(m):
        pre = pre_act[part]
        grad_hidden = mm(grad_branch, ffn_out[part], NT)
        slope = 0.5 * (1.0 + lax.erf(pre * ROOT_HALF)) + pre * jnp.exp(-0.5 * pre * pre) * BELL
        grad_pre = (grad_hidden * slope).astype(BF16)
        grad_ffn_out[part] = mm(hidden_act[part], grad_branch, TN)
        grad_ffn_in[part] = mm(state_low[...], grad_pre, TN)
        grad_up[part] = jnp.sum(grad_pre.astype(F32), 0, keepdims=True)
        grad_one = grad_one + mm(grad_pre, ffn_in[part], NT)
    grad_mid, gain_one, bias_one = norm_pull(grad_one, normed_one[...], inverse_one[...], row(4))
    grad_attended = grad_mid.astype(BF16)

    pick_hot = hot_rows(pos, LEN)
    for part in range(m):
        narrow = mm(mixed[part], spread, NT).astype(BF16)
        grad_attn_out[part] = mm(narrow, grad_attended, TN)
        wide_out[part] = mm(spread, attn_out[part], TN).astype(BF16)
        for index in range(per_head):
            head = part * per_head + index
            at = slice(head * HP, (head + 1) * HP)
            map_q, map_k = (map_q_low, map_k_low) if head < HEADS // 2 else (map_q_high, map_k_high)
            grad_mixed = mm(
                grad_attended, wide_out[part, index * HP : (index + 1) * HP, :], NT
            ).astype(BF16)
            value = prob[head]
            grad_prob = mm(grad_mixed, proj[2, head], NN) + gap[head]
            grad_proj[2, at, :] = mm(grad_mixed, value.astype(BF16), TN).astype(BF16)
            grad_scores = value * (
                grad_prob - jnp.sum(value * grad_prob, axis=-1, keepdims=True)
            )
            grad_scores = jnp.where(leads, grad_scores, 0.0).astype(BF16)
            grad_query = (mm(grad_scores, proj[1, head], NT) * score_scale).astype(BF16)
            grad_proj[0, at, :] = (
                map_q[head % (HEADS // 2)] * score_scale + mm(grad_query, pick_hot, TN)
            ).astype(BF16)
            query = mm(pick_hot, proj[0, head], NT).astype(BF16)
            grad_proj[1, at, :] = (
                (map_k[head % (HEADS // 2)] + mm(query, grad_scores, TN)) * score_scale
            ).astype(BF16)

    normed = normed_zero[...]
    gathered = (normed * row(2) + row(3)).astype(BF16)
    grad_in = exact(pick_hot, grad_mid, TN)
    ones = jnp.ones((8, LEN), BF16)
    for part in range(m):
        for kind in range(3):
            first = part * per_head * HP
            narrow = mm(spread, grad_proj[kind, first : first + per_head * HP, :], NN).astype(BF16)
            grad_attn_in[part, kind] = mm(gathered, narrow, ((0,), (1,)))
            grad_in = grad_in + mm(narrow, attn_in[part, kind], ((0,), (1,)))
            if kind != 1:
                sums = mm(ones, narrow, NT)
                grad_qv[part, kind // 2 : kind // 2 + 1, :] = sums[0:1, :]
    grad_embed, gain_zero, bias_zero = norm_pull(grad_in, normed, inverse_zero[...], row(2))
    low = grad_embed.astype(BF16)
    word_grads[...] = low
    slot_grads[...] = mm(hot_rows(slot_col[...], slot_grads.shape[0]), low, TN).astype(BF16)
    positions = exact(hot_rows(columns[:, 0:1], LEN), grad_embed, TN, 2)
    ones_type = columns[:, 1:2] == 1
    rows = [
        jnp.sum(jnp.where(ones_type, 0.0, grad_embed), axis=0, keepdims=True),
        jnp.sum(jnp.where(ones_type, grad_embed, 0.0), axis=0, keepdims=True),
        gain_zero,
        bias_zero,
        gain_one,
        bias_one,
        gain_two,
        bias_two,
        jnp.sum(grad_mid, axis=0, keepdims=True),
        jnp.sum(grad_res, axis=0, keepdims=True),
    ]
    for part in range(m):
        at = slice(part * width, (part + 1) * width)
        grad_shared[part, 0:LEN, :] = positions[:, at]
        for index, value in enumerate(rows):
            grad_shared[part, LEN + index : LEN + index + 1, :] = value[:, at]


def masked_logits(places, chosen, words):
    soft = (chosen[...] * (1.0 / SOFTEN_FACTOR)).astype(BF16)
    column = lax.broadcasted_iota(jnp.int32, (1, words.shape[0]), 1)
    mask = jnp.where(column < places[1], 0.0, -1e30)
    return mm(soft, words[...], NT) + mask, mask


def logits_kernel(block, places, chosen, words, out):
    logits, _ = masked_logits(places, chosen, words)
    top = jnp.max(logits, axis=-1, keepdims=True)
    total = jnp.sum(jnp.exp(logits - top), axis=-1, keepdims=True)
    total = jnp.where(places[1] > 0, total, 0.0)
    lane = lax.broadcasted_iota(jnp.int32, (block, LANES), 1)
    both = jnp.where(lane == 0, top, jnp.where(lane == 1, total, 0.0))
    out[...] = jnp.transpose(both)[0:8, :]


def logits_stats(plan, place, chosen, words):
    picks = chosen.shape[0]
    block = 640
    return pl.pallas_call(
        functools.partial(logits_kernel, block),
        out_shape=jax.ShapeDtypeStruct((8, picks), F32),
        grid=(picks // block,),
        in_specs=[
            pl.BlockSpec(memory_space=pltpu.SMEM),
            pl.BlockSpec((block, chosen.shape[1]), lambda i: (i, 0)),
            pl.BlockSpec(words.shape, lambda i: (0, 0)),
        ],
        out_specs=pl.BlockSpec((8, block), lambda i: (0, i)),
        compiler_params=pltpu.CompilerParams(vmem_limit_bytes=VMEM_BYTES),
    )(place, chosen, words)


def grad_logits_kernel(block, places, chosen, words, *refs):
    parts_in, (stats, grads, own_pull, other_pull, losses, mentor) = refs[:-6], refs[-6:]
    first = 0
    size = sum(part.shape[1] for part in parts_in)
    for part in parts_in:
        for source in range(part.shape[0]):
            begin = source * size + first
            mentor[begin : begin + part.shape[1], :] = part[source]
        first += part.shape[1]
    step = pl.program_id(0)
    log_total = stats[0:1, :] + jnp.log(stats[2:3, :])
    log_mentor = stats[1:2, :] + jnp.log(stats[3:4, :])
    line = lax.broadcasted_iota(jnp.int32, (LANES, block), 0)
    both = jnp.transpose(jnp.where(line == 0, log_total, log_mentor))
    column_total, mentor_total = both[:, 0:1], both[:, 1:2]
    logits, mask = masked_logits(places, chosen, words)
    target = jnp.exp(mentor[...].astype(F32) * (1.0 / SOFTEN_FACTOR) + (mask - mentor_total))
    student = jnp.exp(logits - column_total)
    value = ((student - target) * (1.0 / SOFTEN_FACTOR)).astype(BF16)
    grads[...] = value
    sources, masks = own_pull.shape[:2]
    pulled = mm(value, words[...], NN).reshape(sources, 2, masks, D)
    first_head = places[3] == 0
    own_pull[...] = jnp.where(first_head, pulled[:, 0], pulled[:, 1])
    other_pull[...] = jnp.where(first_head, pulled[:, 1], pulled[:, 0]).astype(BF16)

    @pl.when(step == 0)
    def _():
        losses[...] = jnp.zeros_like(losses)

    cross = jnp.sum(jnp.sum(target * logits, axis=0, keepdims=True), axis=1, keepdims=True)
    own_share = jnp.sum(log_total, axis=1, keepdims=True)
    row = lax.broadcasted_iota(jnp.int32, (8, LANES), 0)
    losses[...] += jnp.where(row == 0, cross, jnp.where(row == 1, own_share, 0.0))


def grad_logits_call(plan, place, chosen, words, mentor, stats):
    picks = chosen.shape[0]
    sources = 8
    block = picks // plan.n * sources
    masks = picks // plan.n // plan.m
    rows = words.shape[0]
    return pl.pallas_call(
        functools.partial(grad_logits_kernel, block),
        out_shape=[
            jax.ShapeDtypeStruct((picks, rows), BF16),
            jax.ShapeDtypeStruct((plan.n, masks, D), F32),
            jax.ShapeDtypeStruct((plan.n, masks, D), BF16),
            jax.ShapeDtypeStruct((8, LANES), F32),
        ],
        grid=(picks // block,),
        in_specs=[
            pl.BlockSpec(memory_space=pltpu.SMEM),
            pl.BlockSpec((block, chosen.shape[1]), lambda i: (i, 0)),
            pl.BlockSpec(words.shape, lambda i: (0, 0)),
        ]
        + [pl.BlockSpec((sources,) + part.shape[1:], lambda i: (i, 0, 0)) for part in mentor]
        + [pl.BlockSpec((4, block), lambda i: (0, i))],
        out_specs=[
            pl.BlockSpec((block, rows), lambda i: (i, 0)),
            pl.BlockSpec((sources, masks, D), lambda i: (i, 0, 0)),
            pl.BlockSpec((sources, masks, D), lambda i: (i, 0, 0)),
            pl.BlockSpec((8, LANES), lambda i: (0, 0)),
        ],
        scratch_shapes=[pltpu.VMEM((block, rows), BF16)],
        compiler_params=pltpu.CompilerParams(vmem_limit_bytes=VMEM_BYTES),
    )(place, chosen, words, *mentor, stats)


def dot(spec, left, right, **options):
    return jnp.einsum(spec, left, right, preferred_element_type=F32, **options)


def one_hot(index, size):
    return (index[:, None] == jnp.arange(size, dtype=jnp.int32)[None, :]).astype(BF16)


def norm_forward(value, gain_row, bias_row):
    centred = value - jnp.mean(value, axis=-1, keepdims=True)
    inverse = lax.rsqrt(jnp.mean(centred * centred, axis=-1, keepdims=True) + NORM_EPS)
    normed = centred * inverse
    return (normed * gain_row + bias_row, (normed, inverse))


def local(
    master,
    first_moment,
    second_moment,
    token_ids,
    token_types,
    counts,
    mask_pos,
    teacher_states,
    teacher_qk,
    mentor_logits,
):
    n, m = lax.axis_size("dp"), lax.axis_size("head")
    d, h = lax.axis_index("dp"), lax.axis_index("head")
    share_len = master.shape[1]
    assert share_len % LANES == 0 and token_ids.shape[0] == m == 2
    plan = Plan(n, m, share_len)
    share = plan.rows_share
    devices = n * m
    slots = max(8, 1024 // devices)
    masks = mask_pos.shape[1]
    picks = devices * masks

    own_row = lambda value: lax.dynamic_index_in_dim(value, h, 0, keepdims=False)
    ids, types, sizes, pos = (own_row(v) for v in (token_ids, token_types, counts, mask_pos))

    order = jnp.arange(LEN, dtype=jnp.int32)

    def token_slots(turn):
        return call(
            functools.partial(slots_kernel, plan, slots),
            [
                jax.ShapeDtypeStruct((devices, LANES), jnp.int32),
                jax.ShapeDtypeStruct((LEN, 1), jnp.int32),
            ],
            jnp.reshape(turn, (1,)).astype(jnp.int32),
            jnp.broadcast_to(ids[None], (8, LEN)),
            smem=1,
        )

    sent_first, slot_col = token_slots(jnp.int32(0))

    def ask(sent):
        got = lax.all_to_all(sent, BOTH, 0, 0, tiled=True)
        asked = got[:, :slots].reshape(-1)
        return asked, got[:, slots]

    first_row = jnp.minimum((d * share_len + D - 1) // D, plan.vocab)
    row_count = jnp.minimum(((d + 1) * share_len + D - 1) // D, plan.vocab) - first_row

    chunk = master.reshape(share, 1, LANES)
    after = lax.ppermute(
        master[0, : 8 * LANES].reshape(8, LANES), "dp", [(i + 1, i) for i in range(n - 1)]
    )
    shift = jnp.where(row_count > 0, first_row * D - d * share_len, 0)
    place = jnp.stack([shift, row_count, d, h]).astype(jnp.int32)
    if plan.special:
        tail_part = share_rows(plan, place, chunk)
    else:
        tail_part = chunk.reshape(share, LANES).astype(BF16)

    words_own = table_rows(plan, place, chunk, after)

    own_index = lambda asked: jnp.where(asked >= 0, asked - first_row, -1)

    def fetch(asked):
        rows = dot(
            "sv,vd->sd", one_hot(own_index(asked), plan.rows), words_own
        ).astype(BF16)
        return lax.all_to_all(
            rows.reshape(devices, slots, D), BOTH, 0, 0, tiled=True
        ).reshape(-1, D)

    asked_first, needs = ask(sent_first)
    if plan.special:
        tail_part = tail_along_z(tail_to_plane(plan, tail_part), 0)
        asked_first, tail_part, words_own = lax.optimization_barrier(
            (asked_first, tail_part, words_own)
        )

    rounds = jnp.max(needs)
    back = fetch(asked_first)

    room = plan.rows

    send_mentor = lambda block: lax.all_to_all(block, "dp", 0, 0, tiled=False)
    cut = 32
    block_first, block_second, mentor_stats = call(
        functools.partial(mentor_kernel, plan, room, (0, cut)),
        [
            jax.ShapeDtypeStruct((n, cut, room), BF16),
            jax.ShapeDtypeStruct((n, m * masks - cut, room), BF16),
            jax.ShapeDtypeStruct((8, LANES), F32),
        ],
        mentor_logits,
    )

    teacher_weight = join_heads(teacher_qk, h, m)
    states = own_row(teacher_states)
    teacher_proj = dot("hdce,ld->chel", teacher_weight, states).astype(BF16)
    teacher_proj = teacher_proj.reshape(2, HEADS, THD, LEN)

    if plan.special:
        tail_part = tail_along_z(tail_part, 1)

    def more_words(state):
        sent, slot = token_slots(state[0])
        return state[0] + 1, add_rows(NN, slot, fetch(ask(sent)[0]), state[1])

    more_words = lax.while_loop(
        lambda state: state[0] < rounds, more_words, (jnp.int32(1), jnp.zeros((LEN, D), F32))
    )[1]
    tail_own = tail_in_plane(tail_part, n) if plan.special else [gather_tail(plan, tail_part)]


    ends = jnp.cumsum(sizes)
    passed = (order[:, None] >= ends[None, :]).astype(jnp.int32)
    sentence = jnp.sum(passed, axis=-1)
    within = order - jnp.sum(passed * sizes[None, :], axis=-1)
    valid = (sentence < sizes.shape[0] - 1).astype(jnp.int32)

    pick_sentence = jnp.sum(jnp.where(pos[:, None] == order[None, :], sentence[None, :], 0), 1)
    picked_any = jnp.sum((pos[:, None] == order[None, :]).astype(jnp.int32), axis=0) > 0
    columns = [within, types, sentence, valid, 1 - picked_any.astype(jnp.int32)]
    columns = jnp.stack(columns + [order] * 3, axis=1)
    pick_columns = jnp.stack([pos, pick_sentence], axis=1)

    tail_other = [swap(part, "head", 1, 2) for part in tail_own]
    back, tail_own, tail_other, block_first, teacher_proj, columns, pick_columns = (
        lax.optimization_barrier(
            (back, tail_own, tail_other, block_first, teacher_proj, columns, pick_columns)
        )
    )
    mentor_first = send_mentor(block_first)

    shape = jax.ShapeDtypeStruct
    attn_in, attn_out, ffn_in, ffn_out, shared_half, _, _, chosen_own, *saved = call(
        functools.partial(forward_kernel, plan),
        piece_shapes(plan)
        + [
            shape((n, masks, D), BF16),
            shape((LEN, D), F32),
            shape((LEN, 1), F32),
            shape((3, HEADS, HP, LEN), BF16),
            shape((HEADS, masks, LEN), F32),
            shape((m, masks, plan.width // HD * HP), BF16),
            shape((masks, D), F32),
            shape((masks, 1), F32),
            shape((masks, D), BF16),
            shape((m, masks, plan.units), F32),
            shape((m, masks, plan.units), BF16),
            shape((masks, D), F32),
            shape((masks, 1), F32),
        ],
        place,
        *tail_own,
        *tail_other,
        back,
        more_words,
        slot_col,
        columns,
        pick_columns,
        sentence[None],
        scratch=[pltpu.VMEM((SROWS, D), F32)] + piece_scratch(plan),
        smem=1,
    )
    proj = saved[2]

    chosen_own, mentor_first = lax.optimization_barrier((chosen_own, mentor_first))
    gap = call(
        pick_gap_kernel,
        shape((HEADS, masks, LEN), F32),
        jnp.array([sizes.shape[0] - 1], jnp.int32),
        teacher_proj,
        saved[3],
        pick_columns,
        sentence[None],
        smem=1,
    )
    chosen = lax.all_to_all(chosen_own, "dp", 0, 0, tiled=False)
    chosen, gap = lax.optimization_barrier((chosen, gap))
    halves = [
        map_attention(first, HEADS // 2, proj, teacher_proj, columns, sentence[None])
        for first in (0, HEADS // 2)
    ]
    chosen = join_heads(chosen, h, m)
    chosen = jnp.swapaxes(chosen, 0, 1).reshape(picks, D)
    chosen, block_second = lax.optimization_barrier((chosen, block_second))
    mentor_second = send_mentor(block_second)
    student = logits_stats(plan, place, chosen, words_own)
    nothing = jnp.concatenate([jnp.full((1, picks), -1e30, F32), jnp.zeros((1, picks), F32)])
    at = (0, d * m * masks)
    mentor_all = lax.dynamic_update_slice(nothing, mentor_stats[:2, : m * masks], at)
    stats = jnp.concatenate([student[:1], mentor_all[:1], student[1:2], mentor_all[1:]])
    stats, halves[0] = merge_stats(stats, halves[0], plan)
    mentor_here = [mentor_first, mentor_second]
    grad_logits, own_pull, other_pull, losses = grad_logits_call(
        plan, place, chosen, words_own, mentor_here, stats
    )
    map_rows = halves[0][2] + halves[1][2]
    loss_local = jnp.sum(map_rows) + losses[1, 0] / devices - losses[0, 0]
    mine = own_pull + swap(other_pull, "head", 1, 2).astype(F32)
    grad_pick = jnp.sum(
        lax.all_to_all(mine.astype(BF16), "dp", 0, 0, tiled=False).astype(F32), axis=0
    )

    *piece_grads, word_grads, slot_grads = call(
        backward_kernel,
        [
            shape((m, 3, D, plan.width), F32),
            shape((m, plan.width, D), F32),
            shape((m, D, plan.units), F32),
            shape((m, plan.units, D), F32),
            shape((m, SROWS, plan.width), F32),
            shape((m, 2, plan.width), F32),
            shape((m, 1, plan.units), F32),
            shape((LEN, D), BF16),
            shape((devices * slots, D), BF16),
        ],
        grad_pick,
        slot_col,
        columns,
        pick_columns,
        pos[None],
        attn_in,
        attn_out,
        ffn_in,
        ffn_out,
        shared_half,
        *saved,
        gap,
        *halves[0][:2],
        *halves[1][:2],
        scratch=[
            pltpu.VMEM((SROWS - LEN, D), F32),
            pltpu.VMEM((3, HEADS * HP, LEN), BF16),
            pltpu.VMEM((m, plan.width // HD * HP, D), BF16),
        ],
    )

    def give(slot_grads):
        return lax.all_to_all(
            slot_grads.reshape(devices, slots, D), BOTH, 0, 0, tiled=True
        ).reshape(-1, D)

    def more_grads(state):
        sent, slot = token_slots(state[0])
        asked = own_index(ask(sent)[0])[:, None]
        hot = one_hot(slot[:, 0], devices * slots)
        got = give(dot("ts,td->sd", hot, word_grads).astype(BF16))
        return state[0] + 1, add_rows(TN, asked, got, state[1])

    given = give(slot_grads)
    tail_sent = pack_tail(plan, 1 - h, piece_grads)
    tail = pack_tail(plan, h, piece_grads, swap(tail_sent, "head", 1, 2))
    grad_table = call(
        rows_grad_kernel, jax.ShapeDtypeStruct((plan.rows, D), F32), grad_logits, chosen
    )
    tail, given, grad_table = lax.optimization_barrier((tail, given, grad_table))
    if plan.special:
        tail = lax.all_to_all(tail, "dp", 0, 0, tiled=False)

    grad_table = lax.while_loop(
        lambda state: state[0] < rounds, more_grads, (jnp.int32(1), grad_table)
    )[1]
    table_lines = table_pack(plan, place, own_index(asked_first), given, grad_table)
    before = lax.ppermute(table_lines[share:], "dp", [(i, i + 1) for i in range(n - 1)])

    tail, table_lines, before, loss_local = lax.optimization_barrier(
        (tail, table_lines, before, loss_local)
    )
    gradient, numbers = merge(
        plan, place, loss_local.reshape(1), table_lines, before, reduce_tail(plan, tail)
    )

    numbers = numbers + swap(numbers, "head", 1, 2)
    totals = gather_to_all(numbers, plan)
    vector_start = plan.table + plan.width * D * 4 + 2 * D * plan.units + (LEN + 2) * plan.width
    lines = jax.ShapeDtypeStruct((share, 1, LANES), F32)
    *updated, norm, loss_sum = call(
        functools.partial(adam_kernel, plan, vector_start),
        [lines, lines, lines] + [jax.ShapeDtypeStruct((1,), F32)] * 2,
        place,
        totals,
        chunk,
        gradient,
        first_moment.reshape(share, 1, LANES),
        second_moment.reshape(share, 1, LANES),
        scratch=[pltpu.VMEM((share, LANES), F32)] * 7 + [pltpu.SemaphoreType.DMA((7, 4))],
        smem=1,
        hbm=(2, 3, 4, 5),
        hbm_out=(0, 1, 2),
        smem_out=(3, 4),
    )
    updated = [value.reshape(1, share_len) for value in updated]
    weights = call(round_kernel, jax.ShapeDtypeStruct((1, share_len), BF16), updated[0])
    return (loss_sum.reshape(()), norm.reshape(()), *updated, weights)


def solution(mesh):
    return jax.shard_map(
        local,
        mesh=mesh,
        in_specs=(
            P("head", "dp"),
            P("head", "dp"),
            P("head", "dp"),
            P("dp", None),
            P("dp", None),
            P("dp", None),
            P("dp", None),
            P("dp", None, None),
            P(None, None, "head"),
            P("dp", None, "head"),
        ),
        out_specs=(P(), P(), P("head", "dp"), P("head", "dp"), P("head", "dp"), P("head", "dp")),
        check_vma=False,
    )
```
